32 devices in a mesh: lat: 16 (over z, x, core), lon: 2 (over y).
Axes of the slice: x: 2, y: 2, z: 4, core: 2. Of those that a mesh axis runs over, the one named last changes fastest.
Arguments:
- cotangent: bfloat16 [256, 512, 1024], P(None, 'lat', 'lon'), may hold values from -6 to 6
- block_input: bfloat16 [256, 512, 1024], P(None, 'lat', 'lon'), may hold values from -6 to 6
- filtered: bfloat16 [256, 512, 1024], P(None, 'lat', 'lon'), may hold values from -6 to 6
- spectral_saved: float32 [128, 256, 2, 128], P('lat', 'lon'), may hold values from -6 to 6
- spectral_gain: float32 [128, 256, 2, 128], P('lat', 'lon'), may hold values from -6 to 6
- w_in: bfloat16 [256, 512], replicated, may hold values from -0.375 to 0.375
- w_out: bfloat16 [512, 256], replicated, may hold values from -0.25 to 0.25
- w_disco: bfloat16 [256, 256], replicated, may hold values from -0.375 to 0.375
- quad_weights: float32 [64], replicated, may hold values from 0.05 to 0.35
- lat_offsets: int32 [512, 12], replicated, may hold values from -2 to 2, as said below
- lon_offsets: int32 [512, 12], replicated, may hold values from -2 to 2, as said below
- weight_index: int32 [512, 12], replicated, may hold values from 0 to 63
Outputs:
- grad_input: bfloat16 [256, 512, 1024], P(None, 'lat', 'lon')
- grad_gain: float32 [128, 256, 2, 128], P('lat', 'lon')
- grad_w_in: float32 [256, 512], replicated
- grad_w_out: float32 [512, 256], replicated
- grad_w_disco: float32 [256, 256], replicated
The draws below stay inside these ranges and needn't reach their ends.
Inputs may be any that keep to these rules, and one draw needn't show every extreme that they name: `lat_offsets`: in every row the first tap lies exactly 2 rows away, to the north in half of the rows and to the south in the other half. `lon_offsets`: in every row the first tap lies exactly 2 columns away, to the east in half of the rows and to the west in the other half.
All inputs are finite; a program needn't handle non-finite values.
Results may differ from the reference program's by a relative error of at most 0.0069.
Values may be sent and summed in bfloat16 or wider, within the bound.
No kernel may reach another device: no remote copies, remote signals or barrier semaphores. Data moves between devices by JAX's collectives and lax.ppermute only.
A program may use at most 320 MiB of HBM per device.

```python
import math
import jax
import jax.numpy as jnp
import numpy as np
from jax import lax

C = 256
H = 512
NLAT = 512
NLON = 1024
L = 128
M = 128
TAPS = 12
REACH = 2
NQ = 64


def reach_table(key):
    first, second = jax.random.split(key)
    spread = jax.random.randint(first, (NLAT, TAPS), -REACH, REACH + 1)
    order = jax.random.permutation(second, NLAT)
    leading = jnp.where(order % 2 == 0, REACH, -REACH)
    return jnp.concatenate([leading[:, None], spread[:, 1:]], axis=1).astype(jnp.int32)


def draw_lat_offsets(key, part):
    key = jax.random.fold_in(key, 11)
    return reach_table(key)


def draw_lon_offsets(key, part):
    key = jax.random.fold_in(key, 23)
    return reach_table(key)


def place_ends(entries, rng, smallest, high):
    longest = entries.shape.index(max(entries.shape))
    spots = []
    for shift in (0, 1):
        where = [jax.random.randint(jax.random.fold_in(rng, axis), (), 0, length) for axis, length in enumerate(entries.shape)]
        where[longest] = (where[longest] + shift) % entries.shape[longest]
        spots.append(tuple(where))
    return entries.at[spots[0]].set(smallest).at[spots[1]].set(high)


def block_levels(key, extent, shards, least, largest):
    level = 1.0
    for dim, shards_of in shards:
        steps = jax.random.uniform(jax.random.fold_in(jax.random.fold_in(key, 6), dim), (shards_of,), jnp.float32, least / len(shards), largest / len(shards))
        level = level * jnp.repeat(jnp.exp(steps), extent[dim] // shards_of).reshape((-1,) + (1,) * (len(extent) - 1 - dim))
    return level


def gaussian(stream_key, shape, scale, bound, cuts=(), kind=jnp.bfloat16):
    result = scale * jax.random.normal(stream_key, shape, jnp.float32)
    if cuts:
        result = result * block_levels(stream_key, shape, cuts, -0.22, 0.18)
    return jnp.clip(result, -bound, bound).astype(kind)


def setup_inputs(seed: int = 0) -> dict:
    splits = jax.random.split(jax.random.key(seed), 13)
    return {
        "cotangent": gaussian(splits[0], (C, NLAT, NLON), 1.0, 6.0, ((1, 16), (2, 2))),
        "block_input": gaussian(splits[1], (C, NLAT, NLON), 1.0, 6.0, ((1, 16), (2, 2))),
        "filtered": gaussian(splits[2], (C, NLAT, NLON), 1.0, 6.0, ((1, 16), (2, 2))),
        "spectral_saved": gaussian(splits[3], (L, C, 2, M), 1.0, 6.0, ((0, 16), (1, 2)), jnp.float32),
        "spectral_gain": gaussian(splits[4], (L, C, 2, M), 1.0, 6.0, ((0, 16), (1, 2)), jnp.float32),
        "w_in": gaussian(splits[5], (C, H), C ** -0.5, 0.375),
        "w_out": gaussian(splits[6], (H, C), H ** -0.5, 0.25),
        "w_disco": gaussian(splits[7], (C, C), C ** -0.5, 0.375),
        "quad_weights": jnp.clip(jax.random.uniform(splits[8], (NQ,), jnp.float32, 0.05, 0.35), 0.05, 0.35),
        "lat_offsets": draw_lat_offsets(jax.random.fold_in(splits[12], 71), 0),
        "lon_offsets": draw_lon_offsets(jax.random.fold_in(splits[12], 71), 0),
        "weight_index": place_ends(jax.random.randint(splits[11], (NLAT, TAPS), 0, NQ), jax.random.fold_in(splits[11], 1), 0, NQ - 1).astype(jnp.int32),
    }


root_half = 0.7071067811865476
root_two_pi = 2.5066282746310002

def gelu_value(value):
    return value * 0.5 * (1.0 + lax.erf(value * root_half))

def gelu_slope(value):
    return 0.5 * (1.0 + lax.erf(value * root_half)) + value * jnp.exp(-0.5 * value * value) / root_two_pi

def legendre_tables():
    degree = np.arange(L)[:, None] * 1.0
    order = np.arange(M)[None, :] * 1.0
    upper = np.where(degree > order, np.sqrt((4.0 * degree * degree - 1.0) / np.maximum(degree * degree - order * order, 1.0)), 0.0)
    lower = np.where(degree > order + 1.0, np.sqrt(np.maximum((degree - 1.0) ** 2 - order * order, 0.0) / np.maximum(4.0 * (degree - 1.0) ** 2 - 1.0, 1.0)), 0.0)
    counter = np.arange(1, M) * 1.0
    diagonal_log = np.concatenate([np.zeros(1), np.cumsum(0.5 * np.log((2.0 * counter + 1.0) / (2.0 * counter)))]) - 0.5 * np.log(2.0)
    return (upper, lower, diagonal_log)

def legendre_rows(theta):
    upper, lower, diagonal_log = legendre_tables()
    float_type = theta.dtype
    cosine = jnp.cos(theta)[:, None]
    sine = jnp.sin(theta)
    orders = jnp.arange(M, dtype=jnp.int32)
    start_value = jnp.exp(jnp.asarray(diagonal_log, float_type)[None, :] + orders.astype(float_type)[None, :] * jnp.log(sine)[:, None])

    def advance(carry, inputs):
        previous, before = carry
        degree, coef_up, coef_low = inputs
        fresh = jnp.where((orders == degree)[None, :], start_value, coef_up[None, :] * (cosine * previous - coef_low[None, :] * before))
        return ((fresh, previous), fresh)
    empty = jnp.zeros_like(start_value)
    final, table = lax.scan(advance, (empty, empty), (jnp.arange(L, dtype=jnp.int32), jnp.asarray(upper, float_type), jnp.asarray(lower, float_type)))
    weight = jnp.sqrt(sine * (math.pi / NLAT))
    return table * weight[None, :, None]

def forward_table():
    column = jnp.arange(NLON, dtype=jnp.int32)[:, None]
    order = jnp.arange(M, dtype=jnp.int32)[None, :]
    angle = (column * order % NLON).astype(jnp.float32) * (2.0 * math.pi / NLON)
    factor = jnp.where(order == 0, 1.0, 2.0).astype(jnp.float32) / math.sqrt(NLON)
    return jnp.concatenate([factor * jnp.cos(angle), -factor * jnp.sin(angle)], axis=1).astype(jnp.bfloat16)

def inverse_table():
    order = jnp.arange(M, dtype=jnp.int32)[:, None]
    column = jnp.arange(NLON, dtype=jnp.int32)[None, :]
    angle = (column * order % NLON).astype(jnp.float32) * (2.0 * math.pi / NLON)
    return (jnp.concatenate([jnp.cos(angle), -jnp.sin(angle)], axis=0) / math.sqrt(NLON)).astype(jnp.bfloat16)

def disco_kernel(quad_weights, lat_offsets, lon_offsets, weight_index):
    span = jnp.arange(-REACH, REACH + 1, dtype=jnp.int32)
    slots = jnp.arange(NQ, dtype=jnp.int32)
    values = lax.optimization_barrier(jnp.sum(jnp.where(weight_index[:, :, None] == slots[None, None, :], quad_weights[None, None, :], 0.0), axis=2))
    north = (lat_offsets[:, :, None] == span[None, None, :]).astype(quad_weights.dtype)
    east = (lon_offsets[:, :, None] == span[None, None, :]).astype(quad_weights.dtype)
    return lax.optimization_barrier(jnp.sum(values[:, :, None, None] * north[:, :, :, None] * east[:, :, None, :], axis=1))

def disco_apply(padded, kernel):
    height = kernel.shape[0]
    width = padded.shape[2] - 2 * REACH
    total = jnp.zeros((padded.shape[0], height, width), kernel.dtype)
    for north in range(2 * REACH + 1):
        for east in range(2 * REACH + 1):
            total = total + kernel[None, :, north, east, None] * padded[:, north:north + height, east:east + width]
    return total

def disco_adjoint(padded, kernel_rim):
    height = kernel_rim.shape[0] - 2 * REACH
    width = padded.shape[2] - 2 * REACH
    total = jnp.zeros((padded.shape[0], height, width), kernel_rim.dtype)
    for north in range(2 * REACH + 1):
        for east in range(2 * REACH + 1):
            row_shift = 2 * REACH - north
            col_shift = 2 * REACH - east
            total = total + kernel_rim[None, row_shift:row_shift + height, north, east, None] * padded[:, row_shift:row_shift + height, col_shift:col_shift + width]
    return total

def wrap_pad(field):
    padded = jnp.pad(field, ((0, 0), (REACH, REACH), (0, 0)))
    return jnp.concatenate([padded[:, :, NLON - REACH:], padded, padded[:, :, :REACH]], axis=2)

def reference(cotangent, block_input, filtered, spectral_saved, spectral_gain, w_in, w_out, w_disco, quad_weights, lat_offsets, lon_offsets, weight_index):
    band = min(NLAT, 32)
    blocks = NLAT // band

    def mlp_block(carry, index):
        sum_in, sum_out = carry
        part_in = lax.dynamic_slice_in_dim(filtered, index * band, band, 1).reshape(C, band * NLON)
        part_cot = lax.dynamic_slice_in_dim(cotangent, index * band, band, 1).reshape(C, band * NLON)
        hidden_pre = jnp.dot(w_in.T, part_in, preferred_element_type=jnp.float32)
        activation = gelu_value(hidden_pre).astype(jnp.bfloat16)
        grad_act = jnp.dot(w_out, part_cot, preferred_element_type=jnp.float32)
        grad_pre = (grad_act * gelu_slope(hidden_pre)).astype(jnp.bfloat16)
        sum_in = sum_in + jnp.dot(part_in, grad_pre.T, preferred_element_type=jnp.float32)
        sum_out = sum_out + jnp.dot(activation, part_cot.T, preferred_element_type=jnp.float32)
        grad_part = jnp.dot(w_in, grad_pre, preferred_element_type=jnp.float32).astype(jnp.bfloat16)
        return ((sum_in, sum_out), grad_part.reshape(C, band, NLON))
    start_sums = (jnp.zeros((C, H), jnp.float32), jnp.zeros((H, C), jnp.float32))
    mlp_sums, pieces = lax.scan(mlp_block, start_sums, jnp.arange(blocks, dtype=jnp.int32))
    grad_filtered = jnp.transpose(pieces, (1, 0, 2, 3)).reshape(C, NLAT, NLON)
    coeffs = jnp.dot(grad_filtered.reshape(C * NLAT, NLON), forward_table(), preferred_element_type=jnp.float32).astype(jnp.bfloat16).reshape(C, NLAT, 2, M)
    theta = (jnp.arange(NLAT, dtype=jnp.int32).astype(jnp.float32) + 0.5) * (math.pi / NLAT)
    legendre = legendre_rows(theta).astype(jnp.bfloat16)
    owned = jnp.einsum('ljm,cjrm->lcrm', legendre.astype(jnp.float32), coeffs.astype(jnp.float32))
    real_part = owned[:, :, 0]
    imag_part = owned[:, :, 1]
    grad_gain = jnp.stack([real_part * spectral_saved[:, :, 0] + imag_part * spectral_saved[:, :, 1], imag_part * spectral_saved[:, :, 0] - real_part * spectral_saved[:, :, 1]], axis=2)
    scaled = jnp.stack([spectral_gain[:, :, 0] * real_part + spectral_gain[:, :, 1] * imag_part, spectral_gain[:, :, 0] * imag_part - spectral_gain[:, :, 1] * real_part], axis=2).astype(jnp.bfloat16)
    synthesis = jnp.einsum('ljm,lcrm->cjrm', legendre.astype(jnp.float32), scaled.astype(jnp.float32)).astype(jnp.bfloat16)
    spectral_grad = jnp.dot(synthesis.reshape(C * NLAT, 2 * M), inverse_table(), preferred_element_type=jnp.float32).reshape(C, NLAT, NLON)
    kernel = disco_kernel(quad_weights, lat_offsets, lon_offsets, weight_index)
    kernel_pad = jnp.pad(kernel, ((REACH, REACH), (0, 0), (0, 0)))
    input_pad = wrap_pad(block_input)
    grad_mixed = jnp.dot(w_disco, grad_filtered.reshape(C, NLAT * NLON), preferred_element_type=jnp.float32).astype(jnp.bfloat16).reshape(C, NLAT, NLON)
    grad_pad = wrap_pad(grad_mixed)

    def disco_block(carry, index):
        start = index * band
        input_part = lax.dynamic_slice_in_dim(input_pad, start, band + 2 * REACH, 1)
        mixed = disco_apply(input_part, lax.dynamic_slice_in_dim(kernel, start, band, 0)).astype(jnp.bfloat16)
        part_grad = lax.dynamic_slice_in_dim(grad_filtered, start, band, 1)
        carry = carry + jnp.dot(mixed.reshape(C, band * NLON), part_grad.reshape(C, band * NLON).T, preferred_element_type=jnp.float32)
        grad_part = lax.dynamic_slice_in_dim(grad_pad, start, band + 2 * REACH, 1)
        kernel_part = lax.dynamic_slice_in_dim(kernel_pad, start, band + 2 * REACH, 0)
        local_grad = disco_adjoint(grad_part, kernel_part)
        combined = (local_grad + lax.dynamic_slice_in_dim(spectral_grad, start, band, 1)).astype(jnp.bfloat16)
        return (carry, combined)
    disco_sum, outputs = lax.scan(disco_block, jnp.zeros((C, C), jnp.float32), jnp.arange(blocks, dtype=jnp.int32))
    grad_input = jnp.transpose(outputs, (1, 0, 2, 3)).reshape(C, NLAT, NLON)
    scale = 1.0 / math.sqrt(NLAT * NLON)
    return (grad_input, grad_gain, mlp_sums[0] * scale, mlp_sums[1] * scale, disco_sum * scale)
```

```python
import functools
import math

import jax
import jax.numpy as jnp
import numpy as np
from jax import lax
from jax.experimental import pallas as pl
from jax.experimental.pallas import tpu as pltpu
from jax.sharding import PartitionSpec as P

NLAT = 512
NLON = 1024
L = 128
M = 128
REACH = 2
NQ = 64


root_half = 0.7071067811865476
root_two_pi = 2.5066282746310002


def padded_2(block, sides, width):
    for axis, dim in sides:
        count = lax.axis_size(axis)
        forward = [(i, i + 1) for i in range(count - 1)]
        forward.append((count - 1, 0))
        backward = [(target, source) for source, target in forward]
        low = lax.ppermute(
            lax.slice_in_dim(block, block.shape[dim] - width, None, axis=dim), axis, forward
        )
        high = lax.ppermute(lax.slice_in_dim(block, 0, width, axis=dim), axis, backward)
        block = jnp.concatenate([low, block, high], axis=dim)
    return block


def gelu_value(value):
    return value * 0.5 * (1.0 + lax.erf(value * root_half))


def gelu_slope(value):
    return (
        0.5 * (1.0 + lax.erf(value * root_half))
        + value * jnp.exp(-0.5 * value * value) / root_two_pi
    )


def legendre_tables():
    degree = np.arange(L)[:, None] * 1.0
    order = np.arange(M)[None, :] * 1.0
    upper = np.where(
        degree > order,
        np.sqrt(
            np.maximum(4.0 * degree * degree - 1.0, 0.0)
            / np.maximum(degree * degree - order * order, 1.0)
        ),
        0.0,
    )
    lower = np.where(
        degree > order + 1.0,
        np.sqrt(
            np.maximum((degree - 1.0) ** 2 - order * order, 0.0)
            / np.maximum(4.0 * (degree - 1.0) ** 2 - 1.0, 1.0)
        ),
        0.0,
    )
    counter = np.arange(1, M) * 1.0
    diagonal_log = np.concatenate(
        [np.zeros(1), np.cumsum(0.5 * np.log((2.0 * counter + 1.0) / (2.0 * counter)))]
    ) - 0.5 * np.log(2.0)
    return (upper, lower, diagonal_log)


def legendre_rows(theta):
    upper, lower, diagonal_log = legendre_tables()
    float_type = theta.dtype
    cosine = jnp.cos(theta)[:, None]
    sine = jnp.sin(theta)
    orders = jnp.arange(M, dtype=jnp.int32)
    start_value = jnp.exp(
        jnp.asarray(diagonal_log, float_type)[None, :]
        + orders.astype(float_type)[None, :] * jnp.log(sine)[:, None]
    )

    def advance(carry, inputs):
        previous, before = carry
        degree, coef_up, coef_low = inputs
        fresh = jnp.where(
            (orders == degree)[None, :],
            start_value,
            coef_up[None, :] * (cosine * previous - coef_low[None, :] * before),
        )
        return ((fresh, previous), fresh)

    empty = jnp.zeros_like(start_value)
    final, table = lax.scan(
        advance,
        (empty, empty),
        (
            jnp.arange(L, dtype=jnp.int32),
            jnp.asarray(upper, float_type),
            jnp.asarray(lower, float_type),
        ),
    )
    weight = jnp.sqrt(sine * (math.pi / NLAT))
    return table * weight[None, :, None]


def forward_table():
    column = jnp.arange(NLON, dtype=jnp.int32)[:, None]
    order = jnp.arange(M, dtype=jnp.int32)[None, :]
    angle = (column * order % NLON).astype(jnp.float32) * (2.0 * math.pi / NLON)
    factor = jnp.where(order == 0, 1.0, 2.0).astype(jnp.float32) / math.sqrt(NLON)
    return jnp.concatenate([factor * jnp.cos(angle), -factor * jnp.sin(angle)], axis=1).astype(
        jnp.bfloat16
    )


def inverse_table():
    order = jnp.arange(M, dtype=jnp.int32)[:, None]
    column = jnp.arange(NLON, dtype=jnp.int32)[None, :]
    angle = (column * order % NLON).astype(jnp.float32) * (2.0 * math.pi / NLON)
    return (jnp.concatenate([jnp.cos(angle), -jnp.sin(angle)], axis=0) / math.sqrt(NLON)).astype(
        jnp.bfloat16
    )


def disco_kernel(quad_weights, lat_offsets, lon_offsets, weight_index):
    span = jnp.arange(-REACH, REACH + 1, dtype=jnp.int32)
    slots = jnp.arange(NQ, dtype=jnp.int32)
    values = jnp.sum(
        jnp.where(
            weight_index[:, :, None] == slots[None, None, :], quad_weights[None, None, :], 0.0
        ),
        axis=2,
    )
    north = (lat_offsets[:, :, None] == span[None, None, :]).astype(quad_weights.dtype)
    east = (lon_offsets[:, :, None] == span[None, None, :]).astype(quad_weights.dtype)
    return jnp.sum(values[:, :, None, None] * north[:, :, :, None] * east[:, :, None, :], axis=1)


def disco_apply(padded, kernel):
    height = kernel.shape[0]
    width = padded.shape[2] - 2 * REACH
    total = jnp.zeros((padded.shape[0], height, width), kernel.dtype)
    for north in range(2 * REACH + 1):
        for east in range(2 * REACH + 1):
            total = (
                total
                + kernel[None, :, north, east, None]
                * padded[:, north : north + height, east : east + width]
            )
    return total


def disco_adjoint(padded, kernel_rim):
    height = kernel_rim.shape[0] - 2 * REACH
    width = padded.shape[2] - 2 * REACH
    total = jnp.zeros((padded.shape[0], height, width), kernel_rim.dtype)
    for north in range(2 * REACH + 1):
        for east in range(2 * REACH + 1):
            row_shift = 2 * REACH - north
            col_shift = 2 * REACH - east
            total = (
                total
                + kernel_rim[None, row_shift : row_shift + height, north, east, None]
                * padded[:, row_shift : row_shift + height, col_shift : col_shift + width]
            )
    return total


def inside_rows(padded, first_row):
    height = padded.shape[1]
    latitude = first_row - REACH + jnp.arange(height, dtype=jnp.int32)
    keep = (latitude >= 0) & (latitude < NLAT)
    return jnp.where(keep[None, :, None], padded, jnp.zeros((), padded.dtype))


def shards_general(
    cotangent,
    block_input,
    filtered,
    spectral_saved,
    spectral_gain,
    w_in,
    w_out,
    w_disco,
    quad_weights,
    lat_offsets,
    lon_offsets,
    weight_index,
):
    channels, rows, columns = cotangent.shape
    lat_count = lax.axis_size("lat")
    first_row = lax.axis_index("lat") * rows
    cells = rows * columns
    flat_in = filtered.reshape(channels, cells)
    flat_cot = cotangent.reshape(channels, cells)
    hidden_pre = lax.dot_general(
        w_in, flat_in, (((0,), (0,)), ((), ())), preferred_element_type=jnp.float32
    )
    activation = gelu_value(hidden_pre).astype(jnp.bfloat16)
    grad_act = jnp.dot(w_out, flat_cot, preferred_element_type=jnp.float32)
    grad_pre = (grad_act * gelu_slope(hidden_pre)).astype(jnp.bfloat16)
    grad_in_part = lax.dot_general(
        flat_in, grad_pre, (((1,), (1,)), ((), ())), preferred_element_type=jnp.float32
    )
    grad_out_part = lax.dot_general(
        activation, flat_cot, (((1,), (1,)), ((), ())), preferred_element_type=jnp.float32
    )
    grad_flat = jnp.dot(w_in, grad_pre, preferred_element_type=jnp.float32).astype(jnp.bfloat16)
    grad_filtered = grad_flat.reshape(channels, rows, columns)
    spread = lax.all_to_all(grad_filtered, "lon", split_axis=0, concat_axis=2, tiled=True)
    local_channels = spread.shape[0]
    coeffs = (
        jnp.dot(
            spread.reshape(local_channels * rows, NLON),
            forward_table(),
            preferred_element_type=jnp.float32,
        )
        .astype(jnp.bfloat16)
        .reshape(local_channels, rows, 2, M)
    )
    theta_rows = ((first_row + jnp.arange(rows, dtype=jnp.int32)).astype(jnp.float32) + 0.5) * (
        math.pi / NLAT
    )
    legendre = legendre_rows(theta_rows).astype(jnp.bfloat16)
    owned_count = L // lat_count
    weights = lax.slice_in_dim(legendre, 0, owned_count * lax.axis_size("lat"), axis=0)
    owned = lax.psum_scatter(
        jnp.einsum("ljm,cjrm->lcrm", weights, coeffs, preferred_element_type=jnp.float32),
        "lat",
        scatter_dimension=0,
        tiled=True,
    )
    real_part = owned[:, :, 0]
    imag_part = owned[:, :, 1]
    grad_gain = jnp.stack(
        [
            real_part * spectral_saved[:, :, 0] + imag_part * spectral_saved[:, :, 1],
            imag_part * spectral_saved[:, :, 0] - real_part * spectral_saved[:, :, 1],
        ],
        axis=2,
    )
    scaled = jnp.stack(
        [
            spectral_gain[:, :, 0] * real_part + spectral_gain[:, :, 1] * imag_part,
            spectral_gain[:, :, 0] * imag_part - spectral_gain[:, :, 1] * real_part,
        ],
        axis=2,
    ).astype(jnp.bfloat16)
    piece = lax.all_gather(scaled, "lat", axis=0, tiled=True)
    weights = lax.slice_in_dim(legendre, 0, piece.shape[0], axis=0)
    synthesis = (
        jnp.zeros((local_channels, rows, 2, M), jnp.float32)
        + jnp.einsum("ljm,lcrm->cjrm", weights, piece, preferred_element_type=jnp.float32)
    ).astype(jnp.bfloat16)
    grid_rows = jnp.dot(
        synthesis.reshape(local_channels * rows, 2 * M),
        inverse_table(),
        preferred_element_type=jnp.float32,
    ).reshape(local_channels, rows, NLON)
    spectral_grad = lax.all_to_all(grid_rows, "lon", split_axis=2, concat_axis=0, tiled=True)
    kernel = disco_kernel(quad_weights, lat_offsets, lon_offsets, weight_index)
    kernel_pad = jnp.pad(kernel, ((REACH, REACH), (0, 0), (0, 0)))
    kernel_rim = lax.dynamic_slice_in_dim(kernel_pad, first_row, rows + 2 * REACH, 0)
    stacked_rims = padded_2(
        jnp.stack((block_input, grad_filtered)), (("lat", 2), ("lon", 3)), REACH
    )
    input_pad = inside_rows(stacked_rims[0], first_row)
    grad_source = inside_rows(stacked_rims[1], first_row)
    grad_pad = lax.dot_general(
        w_disco, grad_source, (((1,), (0,)), ((), ())), preferred_element_type=jnp.float32
    ).astype(jnp.bfloat16)
    mixed = disco_apply(input_pad, kernel_rim[REACH : REACH + rows]).astype(jnp.bfloat16)
    grad_disco_part = lax.dot_general(
        mixed.reshape(channels, cells),
        grad_flat,
        (((1,), (1,)), ((), ())),
        preferred_element_type=jnp.float32,
    )
    disco_grad = disco_adjoint(grad_pad, kernel_rim)
    grad_input = (spectral_grad + disco_grad).astype(jnp.bfloat16)
    total_in, total_out, total_disco = lax.psum(
        (grad_in_part, grad_out_part, grad_disco_part), ("lat", "lon")
    )
    scale = 1.0 / math.sqrt(NLAT * NLON)
    return (grad_input, grad_gain, total_in * scale, total_out * scale, total_disco * scale)


BAND = 16
LANES = 128
MIB = 1024 * 1024


def mm(a, b):
    return jnp.dot(a, b, preferred_element_type=jnp.float32)


def mm_nt(a, b):
    return lax.dot_general(a, b, (((1,), (1,)), ((), ())), preferred_element_type=jnp.float32)


def mm_tn(a, b):
    return lax.dot_general(a, b, (((0,), (0,)), ((), ())), preferred_element_type=jnp.float32)


def params(mib):
    return pltpu.CompilerParams(vmem_limit_bytes=mib * MIB)


def whole_block(shape):
    return pl.BlockSpec(shape, lambda *_: (0,) * len(shape))


def rows_first(block, stage, flat, width):
    channels = block.shape[0]
    for tile in range(width // LANES):
        stage[tile] = (
            block[:, :, tile * LANES : (tile + 1) * LANES]
            .astype(jnp.float32)
            .reshape(channels * BAND, LANES)
        )
    for row in range(BAND):
        for tile in range(width // LANES):
            start = row * width + tile * LANES
            flat[:, start : start + LANES] = stage[
                tile, pl.ds(row, channels, stride=BAND), :
            ].astype(jnp.bfloat16)


def gelu_both(value):
    decay = jnp.exp(value * value * -0.5)
    base = 1.0 + (0.3275911 * root_half) * jnp.abs(value)
    inverse = pl.reciprocal(base, approx=True)
    inverse = inverse * (2.0 - base * inverse)
    poly = 0.5 * 1.061405429
    for term in (-1.453152027, 1.421413741, -0.284496736, 0.254829592):
        poly = poly * inverse + 0.5 * term
    tail = poly * inverse * decay
    chance = jnp.where(value >= 0.0, 1.0 - tail, tail)
    return chance, decay


def mlp_kernel(
    side, x_ref, ct_ref, win_t, win, wout, table,
    gf_ref, own_ref, send_ref, edge_ref, gin_ref, gout_ref,
    stage, xs, cs, low, high,
    *, steps, width, chunk,
):
    step = pl.program_id(0)

    @pl.when(step == 0)
    def _():
        gin_ref[...] = jnp.zeros_like(gin_ref)
        gout_ref[...] = jnp.zeros_like(gout_ref)

    rows_first(x_ref, stage, xs, width)
    rows_first(ct_ref, stage, cs, width)
    column = pl.multiple_of(step * width, width)
    per = chunk // width

    def body(index, carry):
        cells = pl.ds(pl.multiple_of(index * chunk, chunk), chunk)
        x = xs[:, cells]
        c = cs[:, cells]
        pre = mm(win_t[...], x)
        grad = mm(wout[...], c)
        chance, decay = gelu_both(pre)
        act = (pre * chance).astype(jnp.bfloat16)
        gp = (grad * (chance + pre * decay * (1.0 / root_two_pi))).astype(jnp.bfloat16)
        gf = mm(win[...], gp).astype(jnp.bfloat16)
        for part in range(per):
            gf_ref[index * per + part, :, pl.ds(column, width)] = gf[
                :, part * width : (part + 1) * width
            ]
        gin_ref[...] += mm_nt(x, gp)
        gout_ref[...] += mm_nt(act, c)
        return carry

    lax.fori_loop(0, BAND * width // chunk, body, 0)

    @pl.when(step == steps - 1)
    def _():
        orders = low.shape[0] // BAND

        def transform(row, carry):
            out = mm_nt(table[...], gf_ref[row])
            low[pl.ds(row, orders, stride=BAND), :] = out[:orders, :LANES]
            high[pl.ds(row, orders, stride=BAND), :] = out[:orders, LANES:]
            edge_ref[row] = out[orders:].astype(jnp.bfloat16)
            return carry

        lax.fori_loop(0, BAND, transform, 0)
        first = side[0] == 0
        shape = own_ref.shape

        @pl.when(first)
        def _():
            own_ref[...] = low[...].astype(jnp.bfloat16).reshape(shape)
            send_ref[...] = high[...].astype(jnp.bfloat16).reshape(shape)

        @pl.when(jnp.logical_not(first))
        def _():
            own_ref[...] = high[...].astype(jnp.bfloat16).reshape(shape)
            send_ref[...] = low[...].astype(jnp.bfloat16).reshape(shape)


def mlp_call(band, side, filtered, cotangent, win_t, win, wout, table):
    channels, rows, columns = filtered.shape
    hidden = wout.shape[0]
    width = LANES
    steps = columns // width
    chunk = 4 * width
    orders = table.shape[0] - 16
    block = pl.BlockSpec((channels, BAND, width), lambda i: (0, band, i))
    cells = BAND * columns
    return pl.pallas_call(
        functools.partial(mlp_kernel, steps=steps, width=width, chunk=chunk),
        grid=(steps,),
        in_specs=[
            pl.BlockSpec(memory_space=pltpu.SMEM),
            block,
            block,
            whole_block(win_t.shape),
            whole_block(win.shape),
            whole_block(wout.shape),
            whole_block(table.shape),
        ],
        out_specs=[
            whole_block((BAND, channels, columns)),
            whole_block((orders, BAND, LANES)),
            whole_block((orders, BAND, LANES)),
            whole_block((BAND, 16, channels)),
            whole_block((channels, hidden)),
            whole_block((hidden, channels)),
        ],
        out_shape=[
            jax.ShapeDtypeStruct((BAND, channels, columns), jnp.bfloat16),
            jax.ShapeDtypeStruct((orders, BAND, LANES), jnp.bfloat16),
            jax.ShapeDtypeStruct((orders, BAND, LANES), jnp.bfloat16),
            jax.ShapeDtypeStruct((BAND, 16, channels), jnp.bfloat16),
            jax.ShapeDtypeStruct((channels, hidden), jnp.float32),
            jax.ShapeDtypeStruct((hidden, channels), jnp.float32),
        ],
        scratch_shapes=[
            pltpu.VMEM((width // LANES, channels * BAND, LANES), jnp.float32),
            pltpu.VMEM((channels, BAND * width), jnp.bfloat16),
            pltpu.VMEM((channels, BAND * width), jnp.bfloat16),
            pltpu.VMEM((orders * BAND, LANES), jnp.float32),
            pltpu.VMEM((orders * BAND, LANES), jnp.float32),
        ],
        compiler_params=params(56),
        cost_estimate=pl.CostEstimate(
            flops=2 * cells * channels * (5 * hidden + orders),
            bytes_accessed=6 * channels * cells,
            transcendentals=2 * hidden * cells,
        ),
        name="mlp",
    )(side, filtered, cotangent, win_t, win, wout, table)


def stencil_kernel(
    taps, first, second, top, bottom, edges, place, bi_ref,
    q_ref, gd_ref,
    field, rim, stage, flat,
    *, rows,
):
    band = pl.program_id(0)
    channels, columns = field.shape[1:]

    @pl.when(band == 0)
    def _():
        gd_ref[...] = jnp.zeros_like(gd_ref)
        field[0:REACH] = top[...]
        field[REACH : REACH + BAND] = first[...]
        field[REACH + BAND : REACH + 2 * BAND] = second[...]
        field[rows + REACH :] = bottom[...]

        def spread(row, carry):
            rim[row] = mm_tn(edges[row], place[...]).astype(jnp.bfloat16)
            return carry

        lax.fori_loop(0, rows + 2 * REACH, spread, 0)

    rows_first(bi_ref, stage, flat, columns)
    lane = lax.broadcasted_iota(jnp.int32, (16, LANES), 1)
    span = 2 * REACH + 1

    def row_body(row, carry):
        top_row = band * BAND + row

        def tile_body(tile, inner):
            part = pl.ds(pl.multiple_of(tile * 16, 16), 16)
            sums = [None] * span
            for north in range(span):
                source = top_row + 2 * REACH - north
                here = field[source, part, :].astype(jnp.float32)
                ends = rim[source, part, :].astype(jnp.float32)
                for east in range(span):
                    past = east - REACH
                    shifted = here
                    if past < 0:
                        rim_tile = jnp.where(lane < -past, ends, here[:, :LANES])
                        shifted = jnp.concatenate([rim_tile, here[:, LANES:]], axis=1)
                    if past > 0:
                        rim_tile = jnp.where(lane >= LANES - past, ends, here[:, -LANES:])
                        shifted = jnp.concatenate([here[:, :-LANES], rim_tile], axis=1)
                    weight = taps[(source * span + north) * span + east]
                    term = shifted * weight
                    sums[east] = term if sums[east] is None else sums[east] + term
            total = sums[REACH]
            for east in range(span):
                if east != REACH:
                    total = total + pltpu.roll(sums[east], (east - REACH) % columns, 1)
            q_ref[row, part, :] = total.astype(jnp.bfloat16)
            return inner

        lax.fori_loop(0, channels // 16, tile_body, 0)
        cells = pl.ds(pl.multiple_of(row * columns, columns), columns)
        gd_ref[...] += mm_nt(flat[:, cells], q_ref[row])
        return carry

    lax.fori_loop(0, BAND, row_body, 0)


def stencil_call(taps, first, second, top, bottom, edges, place, block_input):
    channels, rows, columns = block_input.shape
    cells = rows * columns
    vmem = pl.BlockSpec(memory_space=pltpu.VMEM)
    return pl.pallas_call(
        functools.partial(stencil_kernel, rows=rows),
        grid=(rows // BAND,),
        in_specs=[pl.BlockSpec(memory_space=pltpu.SMEM)]
        + [vmem] * 6
        + [pl.BlockSpec((channels, BAND, columns), lambda i: (0, i, 0))],
        out_specs=[
            pl.BlockSpec((BAND, channels, columns), lambda i: (i, 0, 0)),
            whole_block((channels, channels)),
        ],
        out_shape=[
            jax.ShapeDtypeStruct((rows, channels, columns), jnp.bfloat16),
            jax.ShapeDtypeStruct((channels, channels), jnp.float32),
        ],
        scratch_shapes=[
            pltpu.VMEM((rows + 2 * REACH, channels, columns), jnp.bfloat16),
            pltpu.VMEM((rows + 2 * REACH, channels, LANES), jnp.bfloat16),
            pltpu.VMEM((columns // LANES, channels * BAND, LANES), jnp.float32),
            pltpu.VMEM((channels, BAND * columns), jnp.bfloat16),
        ],
        compiler_params=params(60),
        cost_estimate=pl.CostEstimate(
            flops=60 * channels * cells + 2 * channels * channels * cells,
            bytes_accessed=6 * channels * cells,
            transcendentals=0,
        ),
        name="stencil",
    )(taps, first, second, top, bottom, edges, place, block_input)


def legendre_kernel(leg, r0, r1, gain, owned_ref, s0, s1, stage, *, steps, block):
    order = pl.program_id(0)
    degrees = leg.shape[1]
    half = leg.shape[2] // 2
    total = None
    for band, ref in enumerate((r0, r1)):
        pair = jnp.concatenate(
            [ref[:, r].reshape(half, LANES) for r in range(2)], axis=1
        )
        term = mm(leg[0, :, band * half : (band + 1) * half], pair)
        total = term if total is None else total + term
    real = total[:, :LANES]
    imag = total[:, LANES:]
    owned_ref[:, 0, 0] = real.reshape(owned_ref.shape[0], -1, LANES)
    owned_ref[:, 0, 1] = imag.reshape(owned_ref.shape[0], -1, LANES)
    g = gain[:, 0, 0].reshape(degrees, LANES)
    k = gain[:, 0, 1].reshape(degrees, LANES)
    scaled = jnp.concatenate([g * real + k * imag, g * imag - k * real], axis=1).astype(
        jnp.bfloat16
    )
    synth = mm_tn(leg[0], scaled)
    for r in range(2):
        stage[pl.ds(r * steps + order, 2 * half, stride=block), :] = synth[
            :, r * LANES : (r + 1) * LANES
        ]

    @pl.when(order == steps - 1)
    def _():
        s0[...] = stage[: half * block].astype(jnp.bfloat16).reshape(s0.shape)
        s1[...] = stage[half * block :].astype(jnp.bfloat16).reshape(s1.shape)


def legendre_call(leg, r0, r1, gain):
    owners, _, steps, band, lanes = r0.shape
    degrees = leg.shape[1]
    block = 2 * steps
    r_spec = pl.BlockSpec((owners, 2, None, band, lanes), lambda m: (0, 0, m, 0, 0))
    g_shape = (owners, 1, 2, degrees // owners, lanes)
    g_spec = pl.BlockSpec(g_shape, lambda m: (0, m, 0, 0, 0))
    out = (owners, band, block, lanes)
    return pl.pallas_call(
        functools.partial(legendre_kernel, steps=steps, block=block),
        grid=(steps,),
        in_specs=[
            pl.BlockSpec((1, degrees, leg.shape[2]), lambda m: (m, 0, 0)),
            r_spec,
            r_spec,
            g_spec,
        ],
        out_specs=[g_spec, whole_block(out), whole_block(out)],
        out_shape=[
            jax.ShapeDtypeStruct(gain.shape, jnp.float32),
            jax.ShapeDtypeStruct(out, jnp.bfloat16),
            jax.ShapeDtypeStruct(out, jnp.bfloat16),
        ],
        scratch_shapes=[pltpu.VMEM((2 * owners * band * block, lanes), jnp.float32)],
        compiler_params=params(48),
        cost_estimate=pl.CostEstimate(
            flops=8 * steps * degrees * leg.shape[2] * 256,
            bytes_accessed=7 * MIB,
            transcendentals=0,
        ),
        name="legendre",
    )(leg, r0, r1, gain)


def final_kernel(side, q_ref, own, other, table, wd, *rest):
    out_ref, stage = rest[-2:]
    width = q_ref.shape[2]
    orders = table.shape[0]

    def body(row, carry):
        q = q_ref[row]
        for half, ref in enumerate((own, other)):
            base = pl.multiple_of((side[0] + half) % 2 * LANES, LANES)
            synth = ref[:, row].reshape(orders, LANES)
            out = mm_tn(synth, table[...]) + mm(wd[pl.ds(base, LANES), :], q)
            for tile in range(width // LANES):
                stage[tile, pl.ds(base * BAND + row, LANES, stride=BAND), :] = out[
                    :, tile * LANES : (tile + 1) * LANES
                ]
        return carry

    lax.fori_loop(0, BAND, body, 0)
    channels = out_ref.shape[0]
    for tile in range(width // LANES):
        out_ref[:, :, tile * LANES : (tile + 1) * LANES] = (
            stage[tile].astype(jnp.bfloat16).reshape(channels, BAND, LANES)
        )


def final_call(band, side, q, own, other, table, wd, previous):
    rows, channels, columns = q.shape
    width = 2 * LANES
    cells = BAND * columns
    extra = [] if previous is None else [previous]
    return pl.pallas_call(
        final_kernel,
        grid=(columns // width,),
        in_specs=[
            pl.BlockSpec(memory_space=pltpu.SMEM),
            pl.BlockSpec((BAND, channels, width), lambda i: (band, 0, i)),
            whole_block(own.shape),
            whole_block(other.shape),
            pl.BlockSpec((table.shape[0], width), lambda i: (0, i)),
            whole_block(wd.shape),
        ]
        + [pl.BlockSpec(memory_space=pl.ANY)] * len(extra),
        out_specs=pl.BlockSpec((channels, BAND, width), lambda i: (0, band, i)),
        out_shape=jax.ShapeDtypeStruct((channels, rows, columns), jnp.bfloat16),
        scratch_shapes=[pltpu.VMEM((width // LANES, channels * BAND, LANES), jnp.float32)],
        input_output_aliases={6: 0} if extra else {},
        compiler_params=params(48),
        cost_estimate=pl.CostEstimate(
            flops=2 * cells * channels * (channels + table.shape[0]),
            bytes_accessed=5 * channels * cells,
            transcendentals=0,
        ),
        name="final",
    )(side, q, own, other, table, wd, *extra)


def gain_kernel(gain, out, *, degrees):
    for degree in range(degrees):
        for r in range(2):
            part = gain[pl.ds(degree * 2 * LANES + r, LANES, stride=2), :]
            out[pl.ds(r * degrees + degree, LANES, stride=2 * degrees), :] = part.T


def gain_call(gain):
    degrees, channels, _, orders = gain.shape
    flat = gain.reshape(degrees * channels * 2, orders)
    return pl.pallas_call(
        functools.partial(gain_kernel, degrees=degrees),
        out_shape=jax.ShapeDtypeStruct((orders * 2 * degrees, channels), jnp.float32),
        name="gain",
    )(flat)


def grad_gain_kernel(owned, saved, out, *, degrees):
    for degree in range(degrees):
        real = owned[pl.ds(degree, LANES, stride=2 * degrees), :].T
        imag = owned[pl.ds(degrees + degree, LANES, stride=2 * degrees), :].T
        start = degree * 2 * LANES
        s = saved[pl.ds(start, LANES, stride=2), :]
        t = saved[pl.ds(start + 1, LANES, stride=2), :]
        out[pl.ds(start, LANES, stride=2), :] = real * s + imag * t
        out[pl.ds(start + 1, LANES, stride=2), :] = imag * s - real * t


def grad_gain_call(owned, saved):
    degrees, channels, _, orders = saved.shape
    flat = saved.reshape(degrees * channels * 2, orders)
    out = pl.pallas_call(
        functools.partial(grad_gain_kernel, degrees=degrees),
        out_shape=jax.ShapeDtypeStruct(flat.shape, jnp.float32),
        name="grad_gain",
    )(owned, flat)
    return out.reshape(saved.shape)


def legendre_whole():
    upper, lower, diagonal_log = legendre_tables()
    theta = (np.arange(NLAT) + 0.5) * (math.pi / NLAT)
    sine, cosine = np.sin(theta)[None], np.cos(theta)[None]
    orders = np.arange(M)
    start = np.exp(diagonal_log[:, None] + orders[:, None] * np.log(sine))
    table = np.zeros((M, L, NLAT))
    previous = before = np.zeros((M, NLAT))
    for degree in range(L):
        fresh = np.where(
            (orders == degree)[:, None],
            start,
            upper[degree][:, None] * (cosine * previous - lower[degree][:, None] * before),
        )
        table[:, degree] = fresh
        previous, before = fresh, previous
    return table * np.sqrt(sine * (math.pi / NLAT))[None]


def host_tables(lat_count, lon_count):
    columns, rows, own = NLON // lon_count, NLAT // lat_count, M // lat_count
    angle = (np.arange(M)[:, None] * np.arange(NLON)[None, :] % NLON) * (2.0 * math.pi / NLON)
    waves = np.stack([np.cos(angle), -np.sin(angle)]) / math.sqrt(NLON)
    factor = np.where(np.arange(M) == 0, 1.0, 2.0)[None, :, None]

    def arrange(table):
        table = table.reshape(2, lat_count, own, lon_count, columns)
        return table.transpose(3, 1, 0, 2, 4).reshape(lon_count, 2 * M, columns)

    pick = np.zeros((lon_count, 16, columns))
    for row, column in enumerate((0, 1, columns - 2, columns - 1)):
        pick[:, row, column] = 1.0
    forward = np.concatenate([arrange(waves * factor), pick], axis=1)
    legendre = legendre_whole().reshape(M, L, lat_count, rows // BAND, BAND)
    legendre = legendre.transpose(0, 1, 3, 2, 4).reshape(M, L, NLAT)
    kind = jnp.bfloat16
    return forward.astype(kind), arrange(waves).astype(kind), legendre.astype(kind)


def shards_banded(
    cotangent,
    block_input,
    filtered,
    spectral_saved,
    spectral_gain,
    w_in,
    w_out,
    w_disco,
    quad_weights,
    lat_offsets,
    lon_offsets,
    weight_index,
):
    channels, rows, columns = cotangent.shape
    lat_count = lax.axis_size("lat")
    lon_count = lax.axis_size("lon")
    lat_index = lax.axis_index("lat")
    lon_index = lax.axis_index("lon")
    own = M // lat_count
    degrees = L // lat_count
    side = lon_index.reshape(1).astype(jnp.int32)
    forward, inverse, legendre = host_tables(lat_count, lon_count)
    forward = lax.dynamic_index_in_dim(jnp.asarray(forward), lon_index, 0, keepdims=False)
    inverse = lax.dynamic_index_in_dim(jnp.asarray(inverse), lon_index, 0, keepdims=False)
    legendre = lax.dynamic_slice_in_dim(jnp.asarray(legendre), lat_index * own, own, 0)
    swap = [(i, (i + 1) % lon_count) for i in range(lon_count)]
    exchange = functools.partial(lax.all_to_all, axis_name="lat", split_axis=0, concat_axis=0, tiled=True)

    gain = exchange(
        gain_call(spectral_gain).reshape(lat_count, own, 2, degrees, LANES)
    )
    w_in_t = w_in.T
    bands = []
    received = []
    for band in range(rows // BAND):
        bands.append(mlp_call(band, side, filtered, cotangent, w_in_t, w_in, w_out, forward))
        _, kept, sent, _, _, _ = bands[-1]
        arrived = lax.ppermute(sent, "lon", swap)
        summed = (kept.astype(jnp.float32) + arrived.astype(jnp.float32)).astype(jnp.bfloat16)
        received.append(exchange(summed.reshape(lat_count, 2, own, BAND, LANES)))
    first, second = bands[0], bands[1]

    kernel = disco_kernel(quad_weights, lat_offsets, lon_offsets, weight_index)
    kernel_pad = jnp.pad(kernel, ((REACH, REACH), (0, 0), (0, 0)))
    kernel_rim = lax.dynamic_slice_in_dim(kernel_pad, lat_index * rows, rows + 2 * REACH, 0)
    down = [(i, (i + 1) % lat_count) for i in range(lat_count)]
    up = [(target, source) for source, target in down]
    sides = lax.ppermute(jnp.concatenate([first[3], second[3]], axis=0), "lon", swap)
    top, top_side = lax.ppermute(
        (second[0][BAND - REACH :], sides[rows - REACH :]), "lat", down
    )
    bottom, bottom_side = lax.ppermute((first[0][:REACH], sides[:REACH]), "lat", up)
    edges = jnp.concatenate([top_side, sides, bottom_side], axis=0)
    place = np.zeros((16, LANES), np.float32)
    for row, lane in enumerate((0, 1, LANES - 2, LANES - 1)):
        place[row, lane] = 1.0
    q, disco_part = stencil_call(
        kernel_rim.reshape(-1),
        first[0],
        second[0],
        top,
        bottom,
        edges,
        jnp.asarray(place, jnp.bfloat16),
        block_input,
    )
    total_in, total_out, total_disco = lax.psum(
        (first[4] + second[4], first[5] + second[5], disco_part), ("lat", "lon")
    )

    owned, s0, s1 = legendre_call(legendre, received[0], received[1], gain)
    result = None
    for band, synth in enumerate((s0, s1)):
        local = exchange(synth)
        other = lax.ppermute(local, "lon", swap)
        result = final_call(band, side, q, local, other, inverse, w_disco, result)
    owned = exchange(owned).reshape(M * 2 * degrees, LANES)
    grad_gain = grad_gain_call(owned, spectral_saved)
    scale = 1.0 / math.sqrt(NLAT * NLON)
    return (result, grad_gain, total_in * scale, total_out * scale, total_disco * scale)


def shards(*arrays):
    channels, rows, columns = arrays[0].shape
    lat_count = lax.axis_size("lat")
    lon_count = lax.axis_size("lon")
    fits = (
        rows == 2 * BAND
        and lon_count == 2
        and channels == lon_count * LANES
        and columns % (2 * LANES) == 0
        and M == LANES
        and M // lat_count == 8
        and L // lat_count == 8
    )
    return shards_banded(*arrays) if fits else shards_general(*arrays)


def solution(mesh):
    placed = (
        P(None, "lat", "lon"),
        P(None, "lat", "lon"),
        P(None, "lat", "lon"),
        P("lat", "lon", None, None),
        P("lat", "lon", None, None),
        P(),
        P(),
        P(),
        P(),
        P(),
        P(),
        P(),
    )
    return jax.shard_map(
        shards,
        mesh=mesh,
        in_specs=placed,
        out_specs=(P(None, "lat", "lon"), P("lat", "lon", None, None), P(), P(), P()),
        check_vma=False,
    )
```

```python
import functools
import math

import jax
import jax.numpy as jnp
import numpy as np
from jax import lax
from jax.experimental import pallas as pl
from jax.experimental.pallas import tpu as pltpu
from jax.sharding import PartitionSpec as P

NLAT = 512
NLON = 1024
L = 128
M = 128
REACH = 2
NQ = 64


root_half = 0.7071067811865476
root_two_pi = 2.5066282746310002


def padded_2(block, sides, width):
    for axis, dim in sides:
        count = lax.axis_size(axis)
        forward = [(i, i + 1) for i in range(count - 1)]
        forward.append((count - 1, 0))
        backward = [(target, source) for source, target in forward]
        low = lax.ppermute(
            lax.slice_in_dim(block, block.shape[dim] - width, None, axis=dim), axis, forward
        )
        high = lax.ppermute(lax.slice_in_dim(block, 0, width, axis=dim), axis, backward)
        block = jnp.concatenate([low, block, high], axis=dim)
    return block


def gelu_value(value):
    return value * 0.5 * (1.0 + lax.erf(value * root_half))


def gelu_slope(value):
    return (
        0.5 * (1.0 + lax.erf(value * root_half))
        + value * jnp.exp(-0.5 * value * value) / root_two_pi
    )


def legendre_tables():
    degree = np.arange(L)[:, None] * 1.0
    order = np.arange(M)[None, :] * 1.0
    upper = np.where(
        degree > order,
        np.sqrt(
            np.maximum(4.0 * degree * degree - 1.0, 0.0)
            / np.maximum(degree * degree - order * order, 1.0)
        ),
        0.0,
    )
    lower = np.where(
        degree > order + 1.0,
        np.sqrt(
            np.maximum((degree - 1.0) ** 2 - order * order, 0.0)
            / np.maximum(4.0 * (degree - 1.0) ** 2 - 1.0, 1.0)
        ),
        0.0,
    )
    counter = np.arange(1, M) * 1.0
    diagonal_log = np.concatenate(
        [np.zeros(1), np.cumsum(0.5 * np.log((2.0 * counter + 1.0) / (2.0 * counter)))]
    ) - 0.5 * np.log(2.0)
    return (upper, lower, diagonal_log)


def legendre_rows(theta):
    upper, lower, diagonal_log = legendre_tables()
    float_type = theta.dtype
    cosine = jnp.cos(theta)[:, None]
    sine = jnp.sin(theta)
    orders = jnp.arange(M, dtype=jnp.int32)
    start_value = jnp.exp(
        jnp.asarray(diagonal_log, float_type)[None, :]
        + orders.astype(float_type)[None, :] * jnp.log(sine)[:, None]
    )

    def advance(carry, inputs):
        previous, before = carry
        degree, coef_up, coef_low = inputs
        fresh = jnp.where(
            (orders == degree)[None, :],
            start_value,
            coef_up[None, :] * (cosine * previous - coef_low[None, :] * before),
        )
        return ((fresh, previous), fresh)

    empty = jnp.zeros_like(start_value)
    final, table = lax.scan(
        advance,
        (empty, empty),
        (
            jnp.arange(L, dtype=jnp.int32),
            jnp.asarray(upper, float_type),
            jnp.asarray(lower, float_type),
        ),
    )
    weight = jnp.sqrt(sine * (math.pi / NLAT))
    return table * weight[None, :, None]


def forward_table():
    column = jnp.arange(NLON, dtype=jnp.int32)[:, None]
    order = jnp.arange(M, dtype=jnp.int32)[None, :]
    angle = (column * order % NLON).astype(jnp.float32) * (2.0 * math.pi / NLON)
    factor = jnp.where(order == 0, 1.0, 2.0).astype(jnp.float32) / math.sqrt(NLON)
    return jnp.concatenate([factor * jnp.cos(angle), -factor * jnp.sin(angle)], axis=1).astype(
        jnp.bfloat16
    )


def inverse_table():
    order = jnp.arange(M, dtype=jnp.int32)[:, None]
    column = jnp.arange(NLON, dtype=jnp.int32)[None, :]
    angle = (column * order % NLON).astype(jnp.float32) * (2.0 * math.pi / NLON)
    return (jnp.concatenate([jnp.cos(angle), -jnp.sin(angle)], axis=0) / math.sqrt(NLON)).astype(
        jnp.bfloat16
    )


def disco_kernel(quad_weights, lat_offsets, lon_offsets, weight_index):
    span = jnp.arange(-REACH, REACH + 1, dtype=jnp.int32)
    slots = jnp.arange(NQ, dtype=jnp.int32)
    values = jnp.sum(
        jnp.where(
            weight_index[:, :, None] == slots[None, None, :], quad_weights[None, None, :], 0.0
        ),
        axis=2,
    )
    north = (lat_offsets[:, :, None] == span[None, None, :]).astype(quad_weights.dtype)
    east = (lon_offsets[:, :, None] == span[None, None, :]).astype(quad_weights.dtype)
    return jnp.sum(values[:, :, None, None] * north[:, :, :, None] * east[:, :, None, :], axis=1)


def disco_apply(padded, kernel):
    height = kernel.shape[0]
    width = padded.shape[2] - 2 * REACH
    total = jnp.zeros((padded.shape[0], height, width), kernel.dtype)
    for north in range(2 * REACH + 1):
        for east in range(2 * REACH + 1):
            total = (
                total
                + kernel[None, :, north, east, None]
                * padded[:, north : north + height, east : east + width]
            )
    return total


def disco_adjoint(padded, kernel_rim):
    height = kernel_rim.shape[0] - 2 * REACH
    width = padded.shape[2] - 2 * REACH
    total = jnp.zeros((padded.shape[0], height, width), kernel_rim.dtype)
    for north in range(2 * REACH + 1):
        for east in range(2 * REACH + 1):
            row_shift = 2 * REACH - north
            col_shift = 2 * REACH - east
            total = (
                total
                + kernel_rim[None, row_shift : row_shift + height, north, east, None]
                * padded[:, row_shift : row_shift + height, col_shift : col_shift + width]
            )
    return total


def inside_rows(padded, first_row):
    height = padded.shape[1]
    latitude = first_row - REACH + jnp.arange(height, dtype=jnp.int32)
    keep = (latitude >= 0) & (latitude < NLAT)
    return jnp.where(keep[None, :, None], padded, jnp.zeros((), padded.dtype))


def shards_general(
    cotangent,
    block_input,
    filtered,
    spectral_saved,
    spectral_gain,
    w_in,
    w_out,
    w_disco,
    quad_weights,
    lat_offsets,
    lon_offsets,
    weight_index,
):
    channels, rows, columns = cotangent.shape
    lat_count = lax.axis_size("lat")
    first_row = lax.axis_index("lat") * rows
    cells = rows * columns
    flat_in = filtered.reshape(channels, cells)
    flat_cot = cotangent.reshape(channels, cells)
    hidden_pre = lax.dot_general(
        w_in, flat_in, (((0,), (0,)), ((), ())), preferred_element_type=jnp.float32
    )
    activation = gelu_value(hidden_pre).astype(jnp.bfloat16)
    grad_act = jnp.dot(w_out, flat_cot, preferred_element_type=jnp.float32)
    grad_pre = (grad_act * gelu_slope(hidden_pre)).astype(jnp.bfloat16)
    grad_in_part = lax.dot_general(
        flat_in, grad_pre, (((1,), (1,)), ((), ())), preferred_element_type=jnp.float32
    )
    grad_out_part = lax.dot_general(
        activation, flat_cot, (((1,), (1,)), ((), ())), preferred_element_type=jnp.float32
    )
    grad_flat = jnp.dot(w_in, grad_pre, preferred_element_type=jnp.float32).astype(jnp.bfloat16)
    grad_filtered = grad_flat.reshape(channels, rows, columns)
    spread = lax.all_to_all(grad_filtered, "lon", split_axis=0, concat_axis=2, tiled=True)
    local_channels = spread.shape[0]
    coeffs = (
        jnp.dot(
            spread.reshape(local_channels * rows, NLON),
            forward_table(),
            preferred_element_type=jnp.float32,
        )
        .astype(jnp.bfloat16)
        .reshape(local_channels, rows, 2, M)
    )
    theta_rows = ((first_row + jnp.arange(rows, dtype=jnp.int32)).astype(jnp.float32) + 0.5) * (
        math.pi / NLAT
    )
    legendre = legendre_rows(theta_rows).astype(jnp.bfloat16)
    owned_count = L // lat_count
    weights = lax.slice_in_dim(legendre, 0, owned_count * lax.axis_size("lat"), axis=0)
    owned = lax.psum_scatter(
        jnp.einsum("ljm,cjrm->lcrm", weights, coeffs, preferred_element_type=jnp.float32),
        "lat",
        scatter_dimension=0,
        tiled=True,
    )
    real_part = owned[:, :, 0]
    imag_part = owned[:, :, 1]
    grad_gain = jnp.stack(
        [
            real_part * spectral_saved[:, :, 0] + imag_part * spectral_saved[:, :, 1],
            imag_part * spectral_saved[:, :, 0] - real_part * spectral_saved[:, :, 1],
        ],
        axis=2,
    )
    scaled = jnp.stack(
        [
            spectral_gain[:, :, 0] * real_part + spectral_gain[:, :, 1] * imag_part,
            spectral_gain[:, :, 0] * imag_part - spectral_gain[:, :, 1] * real_part,
        ],
        axis=2,
    ).astype(jnp.bfloat16)
    piece = lax.all_gather(scaled, "lat", axis=0, tiled=True)
    weights = lax.slice_in_dim(legendre, 0, piece.shape[0], axis=0)
    synthesis = (
        jnp.zeros((local_channels, rows, 2, M), jnp.float32)
        + jnp.einsum("ljm,lcrm->cjrm", weights, piece, preferred_element_type=jnp.float32)
    ).astype(jnp.bfloat16)
    grid_rows = jnp.dot(
        synthesis.reshape(local_channels * rows, 2 * M),
        inverse_table(),
        preferred_element_type=jnp.float32,
    ).reshape(local_channels, rows, NLON)
    spectral_grad = lax.all_to_all(grid_rows, "lon", split_axis=2, concat_axis=0, tiled=True)
    kernel = disco_kernel(quad_weights, lat_offsets, lon_offsets, weight_index)
    kernel_pad = jnp.pad(kernel, ((REACH, REACH), (0, 0), (0, 0)))
    kernel_rim = lax.dynamic_slice_in_dim(kernel_pad, first_row, rows + 2 * REACH, 0)
    stacked_rims = padded_2(
        jnp.stack((block_input, grad_filtered)), (("lat", 2), ("lon", 3)), REACH
    )
    input_pad = inside_rows(stacked_rims[0], first_row)
    grad_source = inside_rows(stacked_rims[1], first_row)
    grad_pad = lax.dot_general(
        w_disco, grad_source, (((1,), (0,)), ((), ())), preferred_element_type=jnp.float32
    ).astype(jnp.bfloat16)
    mixed = disco_apply(input_pad, kernel_rim[REACH : REACH + rows]).astype(jnp.bfloat16)
    grad_disco_part = lax.dot_general(
        mixed.reshape(channels, cells),
        grad_flat,
        (((1,), (1,)), ((), ())),
        preferred_element_type=jnp.float32,
    )
    disco_grad = disco_adjoint(grad_pad, kernel_rim)
    grad_input = (spectral_grad + disco_grad).astype(jnp.bfloat16)
    total_in, total_out, total_disco = lax.psum(
        (grad_in_part, grad_out_part, grad_disco_part), ("lat", "lon")
    )
    scale = 1.0 / math.sqrt(NLAT * NLON)
    return (grad_input, grad_gain, total_in * scale, total_out * scale, total_disco * scale)


BAND = 16
LANES = 128
PARTS = 2
MIB = 1024 * 1024


def mm(a, b):
    return jnp.dot(a, b, preferred_element_type=jnp.float32)


def mm_nt(a, b):
    return lax.dot_general(a, b, (((1,), (1,)), ((), ())), preferred_element_type=jnp.float32)


def mm_tn(a, b):
    return lax.dot_general(a, b, (((0,), (0,)), ((), ())), preferred_element_type=jnp.float32)


def params(mib):
    return pltpu.CompilerParams(vmem_limit_bytes=mib * MIB)


def whole_block(shape):
    return pl.BlockSpec(shape, lambda *_: (0,) * len(shape))


def rows_first(block, stage, flat, width):
    channels = block.shape[0]
    for tile in range(width // LANES):
        stage[tile] = (
            block[:, :, tile * LANES : (tile + 1) * LANES]
            .astype(jnp.float32)
            .reshape(channels * BAND, LANES)
        )
    for row in range(BAND):
        for tile in range(width // LANES):
            start = row * width + tile * LANES
            flat[:, start : start + LANES] = stage[
                tile, pl.ds(row, channels, stride=BAND), :
            ].astype(jnp.bfloat16)


def gelu_both(value):
    decay = jnp.exp(value * value * -0.5)
    base = 1.0 + (0.3275911 * root_half) * jnp.abs(value)
    inverse = pl.reciprocal(base, approx=True)
    inverse = inverse * (2.0 - base * inverse)
    poly = 0.5 * 1.061405429
    for term in (-1.453152027, 1.421413741, -0.284496736, 0.254829592):
        poly = poly * inverse + 0.5 * term
    tail = poly * inverse * decay
    chance = jnp.where(value >= 0.0, 1.0 - tail, tail)
    return chance, decay


def mlp_kernel(
    side, x_ref, ct_ref, win_t, win, wout, table,
    gf_ref, own_ref, send_ref, edge_ref, gin_ref, gout_ref,
    stage, xs, cs, low, high,
    *, steps, width, chunk,
):
    step = pl.program_id(0)

    @pl.when(step == 0)
    def _():
        gin_ref[...] = jnp.zeros_like(gin_ref)
        gout_ref[...] = jnp.zeros_like(gout_ref)

    rows_first(x_ref, stage, xs, width)
    rows_first(ct_ref, stage, cs, width)
    column = pl.multiple_of(step * width, width)
    per = chunk // width

    def body(index, carry):
        cells = pl.ds(pl.multiple_of(index * chunk, chunk), chunk)
        x = xs[:, cells]
        c = cs[:, cells]
        pre = mm(win_t[...], x)
        grad = mm(wout[...], c)
        chance, decay = gelu_both(pre)
        act = (pre * chance).astype(jnp.bfloat16)
        gp = (grad * (chance + pre * decay * (1.0 / root_two_pi))).astype(jnp.bfloat16)
        gf = mm(win[...], gp).astype(jnp.bfloat16)
        for part in range(per):
            gf_ref[index * per + part, :, pl.ds(column, width)] = gf[
                :, part * width : (part + 1) * width
            ]
        gin_ref[...] += mm_nt(x, gp)
        gout_ref[...] += mm_nt(act, c)
        return carry

    lax.fori_loop(0, BAND * width // chunk, body, 0)

    @pl.when(step == steps - 1)
    def _():
        orders = low.shape[0] // BAND

        def transform(row, carry):
            out = mm_nt(table[...], gf_ref[row])
            low[pl.ds(row, orders, stride=BAND), :] = out[:orders, :LANES]
            high[pl.ds(row, orders, stride=BAND), :] = out[:orders, LANES:]
            edge_ref[row] = out[orders:].astype(jnp.bfloat16)
            return carry

        lax.fori_loop(0, BAND, transform, 0)
        first = side[0] == 0
        shape = own_ref.shape

        @pl.when(first)
        def _():
            own_ref[...] = low[...].astype(jnp.bfloat16).reshape(shape)
            send_ref[...] = high[...].astype(jnp.bfloat16).reshape(shape)

        @pl.when(jnp.logical_not(first))
        def _():
            own_ref[...] = high[...].astype(jnp.bfloat16).reshape(shape)
            send_ref[...] = low[...].astype(jnp.bfloat16).reshape(shape)


def mlp_call(band, side, filtered, cotangent, win_t, win, wout, table):
    channels, rows, columns = filtered.shape
    hidden = wout.shape[0]
    width = LANES
    steps = columns // width
    chunk = 4 * width
    orders = table.shape[0] - 16
    block = pl.BlockSpec((channels, BAND, width), lambda i: (0, band, i))
    cells = BAND * columns
    return pl.pallas_call(
        functools.partial(mlp_kernel, steps=steps, width=width, chunk=chunk),
        grid=(steps,),
        in_specs=[
            pl.BlockSpec(memory_space=pltpu.SMEM),
            block,
            block,
            whole_block(win_t.shape),
            whole_block(win.shape),
            whole_block(wout.shape),
            whole_block(table.shape),
        ],
        out_specs=[
            whole_block((BAND, channels, columns)),
            whole_block((orders, BAND, LANES)),
            whole_block((orders, BAND, LANES)),
            whole_block((BAND, 16, channels)),
            whole_block((channels, hidden)),
            whole_block((hidden, channels)),
        ],
        out_shape=[
            jax.ShapeDtypeStruct((BAND, channels, columns), jnp.bfloat16),
            jax.ShapeDtypeStruct((orders, BAND, LANES), jnp.bfloat16),
            jax.ShapeDtypeStruct((orders, BAND, LANES), jnp.bfloat16),
            jax.ShapeDtypeStruct((BAND, 16, channels), jnp.bfloat16),
            jax.ShapeDtypeStruct((channels, hidden), jnp.float32),
            jax.ShapeDtypeStruct((hidden, channels), jnp.float32),
        ],
        scratch_shapes=[
            pltpu.VMEM((width // LANES, channels * BAND, LANES), jnp.float32),
            pltpu.VMEM((channels, BAND * width), jnp.bfloat16),
            pltpu.VMEM((channels, BAND * width), jnp.bfloat16),
            pltpu.VMEM((orders * BAND, LANES), jnp.float32),
            pltpu.VMEM((orders * BAND, LANES), jnp.float32),
        ],
        compiler_params=params(56),
        cost_estimate=pl.CostEstimate(
            flops=2 * cells * channels * (5 * hidden + orders),
            bytes_accessed=6 * channels * cells,
            transcendentals=2 * hidden * cells,
        ),
        name="mlp",
    )(side, filtered, cotangent, win_t, win, wout, table)


def stencil_kernel(taps, first, second, top, bottom, edges, place, *rest, rows):
    q_ref, field, rim = rest[-3:]
    channels, columns = field.shape[1:]
    field[0:REACH] = top[...]
    field[REACH : REACH + BAND] = first[...]
    field[REACH + BAND : REACH + 2 * BAND] = second[...]
    field[rows + REACH :] = bottom[...]

    def spread(row, carry):
        rim[row] = mm_tn(edges[row], place[...])[: rim.shape[1]].astype(jnp.bfloat16)
        return carry

    lax.fori_loop(0, rows + 2 * REACH, spread, 0)
    lane = lax.broadcasted_iota(jnp.int32, (16, LANES), 1)
    span = 2 * REACH + 1

    def row_body(row, carry):
        def tile_body(tile, inner):
            part = pl.ds(pl.multiple_of(tile * 16, 16), 16)
            sums = [None] * span
            for north in range(span):
                source = row + 2 * REACH - north
                here = field[source, part, :].astype(jnp.float32)
                ends = rim[source, part, :].astype(jnp.float32)
                for east in range(span):
                    past = east - REACH
                    shifted = here
                    if past < 0:
                        rim_tile = jnp.where(lane < -past, ends, here[:, :LANES])
                        shifted = jnp.concatenate([rim_tile, here[:, LANES:]], axis=1)
                    if past > 0:
                        rim_tile = jnp.where(lane >= LANES - past, ends, here[:, -LANES:])
                        shifted = jnp.concatenate([here[:, :-LANES], rim_tile], axis=1)
                    weight = taps[(source * span + north) * span + east]
                    term = shifted * weight
                    sums[east] = term if sums[east] is None else sums[east] + term
            total = sums[REACH]
            for east in range(span):
                if east != REACH:
                    total = total + pltpu.roll(sums[east], (east - REACH) % columns, 1)
            q_ref[row, part, :] = total.astype(jnp.bfloat16)
            return inner

        return lax.fori_loop(0, channels // 16, tile_body, carry)

    lax.fori_loop(0, rows, row_body, 0)


def stencil_call(part, parts, taps, first, second, top, bottom, edges, place, previous):
    rows = edges.shape[0] - 2 * REACH
    _, channels, columns = first.shape
    some = channels // parts
    extra = [] if previous is None else [previous]

    def piece(count):
        return pl.BlockSpec((count, some, columns), lambda i: (0, part, 0))

    return pl.pallas_call(
        functools.partial(stencil_kernel, rows=rows),
        grid=(1,),
        in_specs=[
            pl.BlockSpec(memory_space=pltpu.SMEM),
            piece(BAND),
            piece(BAND),
            piece(REACH),
            piece(REACH),
            pl.BlockSpec(edges.shape[:2] + (LANES,), lambda i: (0, 0, part * some // LANES)),
            pl.BlockSpec(memory_space=pltpu.VMEM),
        ]
        + [pl.BlockSpec(memory_space=pl.ANY)] * len(extra),
        out_specs=piece(rows),
        out_shape=jax.ShapeDtypeStruct((rows, channels, columns), jnp.bfloat16),
        scratch_shapes=[
            pltpu.VMEM((rows + 2 * REACH, some, columns), jnp.bfloat16),
            pltpu.VMEM((rows + 2 * REACH, some, LANES), jnp.bfloat16),
        ],
        input_output_aliases={7: 0} if extra else {},
        compiler_params=params(48),
        cost_estimate=pl.CostEstimate(
            flops=60 * some * rows * columns,
            bytes_accessed=4 * some * rows * columns,
            transcendentals=0,
        ),
        name="stencil",
    )(taps, first, second, top, bottom, edges, place, *extra)


def disco_kernel_grad(bi_ref, q_ref, gd_ref, stage, flat):
    columns = q_ref.shape[2]

    @pl.when(pl.program_id(0) == 0)
    def _():
        gd_ref[...] = jnp.zeros_like(gd_ref)

    rows_first(bi_ref, stage, flat, columns)

    def body(row, carry):
        cells = pl.ds(pl.multiple_of(row * columns, columns), columns)
        gd_ref[...] += mm_nt(flat[:, cells], q_ref[row])
        return carry

    lax.fori_loop(0, BAND, body, 0)


def disco_grad_call(block_input, q):
    channels, rows, columns = block_input.shape
    return pl.pallas_call(
        disco_kernel_grad,
        grid=(rows // BAND,),
        in_specs=[
            pl.BlockSpec((channels, BAND, columns), lambda i: (0, i, 0)),
            pl.BlockSpec((BAND, channels, columns), lambda i: (i, 0, 0)),
        ],
        out_specs=whole_block((channels, channels)),
        out_shape=jax.ShapeDtypeStruct((channels, channels), jnp.float32),
        scratch_shapes=[
            pltpu.VMEM((columns // LANES, channels * BAND, LANES), jnp.float32),
            pltpu.VMEM((channels, BAND * columns), jnp.bfloat16),
        ],
        compiler_params=params(48),
        cost_estimate=pl.CostEstimate(
            flops=2 * channels * channels * rows * columns,
            bytes_accessed=4 * channels * rows * columns,
            transcendentals=0,
        ),
        name="disco_weight",
    )(block_input, q)


def legendre_kernel(leg, r0, r1, gain, owned_ref, s0, s1, stage, *, steps, block):
    order = pl.program_id(0)
    degrees = leg.shape[1]
    half = leg.shape[2] // 2
    total = None
    for band, ref in enumerate((r0, r1)):
        pair = jnp.concatenate(
            [ref[:, r].reshape(half, LANES) for r in range(2)], axis=1
        )
        term = mm(leg[0, :, band * half : (band + 1) * half], pair)
        total = term if total is None else total + term
    real = total[:, :LANES]
    imag = total[:, LANES:]
    owned_ref[:, 0, 0] = real.reshape(owned_ref.shape[0], -1, LANES)
    owned_ref[:, 0, 1] = imag.reshape(owned_ref.shape[0], -1, LANES)
    g = gain[:, 0, 0].reshape(degrees, LANES)
    k = gain[:, 0, 1].reshape(degrees, LANES)
    scaled = jnp.concatenate([g * real + k * imag, g * imag - k * real], axis=1).astype(
        jnp.bfloat16
    )
    synth = mm_tn(leg[0], scaled)
    for r in range(2):
        stage[pl.ds(r * steps + order, 2 * half, stride=block), :] = synth[
            :, r * LANES : (r + 1) * LANES
        ]

    @pl.when(order == steps - 1)
    def _():
        s0[...] = stage[: half * block].astype(jnp.bfloat16).reshape(s0.shape)
        s1[...] = stage[half * block :].astype(jnp.bfloat16).reshape(s1.shape)


def legendre_call(leg, r0, r1, gain):
    owners, _, steps, band, lanes = r0.shape
    degrees = leg.shape[1]
    block = 2 * steps
    r_spec = pl.BlockSpec((owners, 2, None, band, lanes), lambda m: (0, 0, m, 0, 0))
    g_shape = (owners, 1, 2, degrees // owners, lanes)
    g_spec = pl.BlockSpec(g_shape, lambda m: (0, m, 0, 0, 0))
    out = (owners, band, block, lanes)
    return pl.pallas_call(
        functools.partial(legendre_kernel, steps=steps, block=block),
        grid=(steps,),
        in_specs=[
            pl.BlockSpec((1, degrees, leg.shape[2]), lambda m: (m, 0, 0)),
            r_spec,
            r_spec,
            g_spec,
        ],
        out_specs=[g_spec, whole_block(out), whole_block(out)],
        out_shape=[
            jax.ShapeDtypeStruct(gain.shape, jnp.float32),
            jax.ShapeDtypeStruct(out, jnp.bfloat16),
            jax.ShapeDtypeStruct(out, jnp.bfloat16),
        ],
        scratch_shapes=[pltpu.VMEM((2 * owners * band * block, lanes), jnp.float32)],
        compiler_params=params(48),
        cost_estimate=pl.CostEstimate(
            flops=8 * steps * degrees * leg.shape[2] * 256,
            bytes_accessed=7 * MIB,
            transcendentals=0,
        ),
        name="legendre",
    )(leg, r0, r1, gain)


def final_kernel(side, q_ref, own, other, table, wd, *rest):
    out_ref, stage = rest[-2:]
    width = q_ref.shape[2]
    orders = table.shape[0]

    def body(row, carry):
        q = q_ref[row]
        for half, ref in enumerate((own, other)):
            base = pl.multiple_of((side[0] + half) % 2 * LANES, LANES)
            synth = ref[:, row].reshape(orders, LANES)
            out = mm_tn(synth, table[...]) + mm(wd[pl.ds(base, LANES), :], q)
            for tile in range(width // LANES):
                stage[tile, pl.ds(base * BAND + row, LANES, stride=BAND), :] = out[
                    :, tile * LANES : (tile + 1) * LANES
                ]
        return carry

    lax.fori_loop(0, BAND, body, 0)
    channels = out_ref.shape[0]
    for tile in range(width // LANES):
        out_ref[:, :, tile * LANES : (tile + 1) * LANES] = (
            stage[tile].astype(jnp.bfloat16).reshape(channels, BAND, LANES)
        )


def final_call(band, side, q, own, other, table, wd, previous):
    rows, channels, columns = q.shape
    width = 2 * LANES
    cells = BAND * columns
    extra = [] if previous is None else [previous]
    return pl.pallas_call(
        final_kernel,
        grid=(columns // width,),
        in_specs=[
            pl.BlockSpec(memory_space=pltpu.SMEM),
            pl.BlockSpec((BAND, channels, width), lambda i: (band, 0, i)),
            whole_block(own.shape),
            whole_block(other.shape),
            pl.BlockSpec((table.shape[0], width), lambda i: (0, i)),
            whole_block(wd.shape),
        ]
        + [pl.BlockSpec(memory_space=pl.ANY)] * len(extra),
        out_specs=pl.BlockSpec((channels, BAND, width), lambda i: (0, band, i)),
        out_shape=jax.ShapeDtypeStruct((channels, rows, columns), jnp.bfloat16),
        scratch_shapes=[pltpu.VMEM((width // LANES, channels * BAND, LANES), jnp.float32)],
        input_output_aliases={6: 0} if extra else {},
        compiler_params=params(48),
        cost_estimate=pl.CostEstimate(
            flops=2 * cells * channels * (channels + table.shape[0]),
            bytes_accessed=5 * channels * cells,
            transcendentals=0,
        ),
        name="final",
    )(side, q, own, other, table, wd, *extra)


def gain_kernel(gain, out, *, degrees):
    for degree in range(degrees):
        for r in range(2):
            part = gain[pl.ds(degree * 2 * LANES + r, LANES, stride=2), :]
            out[pl.ds(r * degrees + degree, LANES, stride=2 * degrees), :] = part.T


def gain_call(gain):
    degrees, channels, _, orders = gain.shape
    flat = gain.reshape(degrees * channels * 2, orders)
    return pl.pallas_call(
        functools.partial(gain_kernel, degrees=degrees),
        out_shape=jax.ShapeDtypeStruct((orders * 2 * degrees, channels), jnp.float32),
        name="gain",
    )(flat)


def grad_gain_kernel(owned, saved, out, *, degrees):
    for degree in range(degrees):
        real = owned[pl.ds(degree, LANES, stride=2 * degrees), :].T
        imag = owned[pl.ds(degrees + degree, LANES, stride=2 * degrees), :].T
        start = degree * 2 * LANES
        s = saved[pl.ds(start, LANES, stride=2), :]
        t = saved[pl.ds(start + 1, LANES, stride=2), :]
        out[pl.ds(start, LANES, stride=2), :] = real * s + imag * t
        out[pl.ds(start + 1, LANES, stride=2), :] = imag * s - real * t


def grad_gain_call(owned, saved):
    degrees, channels, _, orders = saved.shape
    flat = saved.reshape(degrees * channels * 2, orders)
    out = pl.pallas_call(
        functools.partial(grad_gain_kernel, degrees=degrees),
        out_shape=jax.ShapeDtypeStruct(flat.shape, jnp.float32),
        name="grad_gain",
    )(owned, flat)
    return out.reshape(saved.shape)


def legendre_whole():
    upper, lower, diagonal_log = legendre_tables()
    theta = (np.arange(NLAT) + 0.5) * (math.pi / NLAT)
    sine, cosine = np.sin(theta)[None], np.cos(theta)[None]
    orders = np.arange(M)
    start = np.exp(diagonal_log[:, None] + orders[:, None] * np.log(sine))
    table = np.zeros((M, L, NLAT))
    previous = before = np.zeros((M, NLAT))
    for degree in range(L):
        fresh = np.where(
            (orders == degree)[:, None],
            start,
            upper[degree][:, None] * (cosine * previous - lower[degree][:, None] * before),
        )
        table[:, degree] = fresh
        previous, before = fresh, previous
    return table * np.sqrt(sine * (math.pi / NLAT))[None]


def host_tables(lat_count, lon_count):
    columns, rows, own = NLON // lon_count, NLAT // lat_count, M // lat_count
    angle = (np.arange(M)[:, None] * np.arange(NLON)[None, :] % NLON) * (2.0 * math.pi / NLON)
    waves = np.stack([np.cos(angle), -np.sin(angle)]) / math.sqrt(NLON)
    factor = np.where(np.arange(M) == 0, 1.0, 2.0)[None, :, None]

    def arrange(table):
        table = table.reshape(2, lat_count, own, lon_count, columns)
        return table.transpose(3, 1, 0, 2, 4).reshape(lon_count, 2 * M, columns)

    pick = np.zeros((lon_count, 16, columns))
    for row, column in enumerate((0, 1, columns - 2, columns - 1)):
        pick[:, row, column] = 1.0
    forward = np.concatenate([arrange(waves * factor), pick], axis=1)
    legendre = legendre_whole().reshape(M, L, lat_count, rows // BAND, BAND)
    legendre = legendre.transpose(0, 1, 3, 2, 4).reshape(M, L, NLAT)
    kind = jnp.bfloat16
    return forward.astype(kind), arrange(waves).astype(kind), legendre.astype(kind)


def shards_banded(
    cotangent,
    block_input,
    filtered,
    spectral_saved,
    spectral_gain,
    w_in,
    w_out,
    w_disco,
    quad_weights,
    lat_offsets,
    lon_offsets,
    weight_index,
):
    channels, rows, columns = cotangent.shape
    lat_count = lax.axis_size("lat")
    lon_count = lax.axis_size("lon")
    lat_index = lax.axis_index("lat")
    lon_index = lax.axis_index("lon")
    own = M // lat_count
    degrees = L // lat_count
    side = lon_index.reshape(1).astype(jnp.int32)
    forward, inverse, legendre = host_tables(lat_count, lon_count)
    forward = lax.dynamic_index_in_dim(jnp.asarray(forward), lon_index, 0, keepdims=False)
    inverse = lax.dynamic_index_in_dim(jnp.asarray(inverse), lon_index, 0, keepdims=False)
    legendre = lax.dynamic_slice_in_dim(jnp.asarray(legendre), lat_index * own, own, 0)
    swap = [(i, (i + 1) % lon_count) for i in range(lon_count)]
    exchange = functools.partial(lax.all_to_all, axis_name="lat", split_axis=0, concat_axis=0, tiled=True)

    gain = exchange(
        gain_call(spectral_gain).reshape(lat_count, own, 2, degrees, LANES)
    )
    kernel = disco_kernel(quad_weights, lat_offsets, lon_offsets, weight_index)
    kernel_pad = jnp.pad(kernel, ((REACH, REACH), (0, 0), (0, 0)))
    kernel_rim = lax.dynamic_slice_in_dim(kernel_pad, lat_index * rows, rows + 2 * REACH, 0)
    taps = kernel_rim.reshape(-1)
    place = np.zeros((16, LANES), np.float32)
    for row, lane in enumerate((0, 1, LANES - 2, LANES - 1)):
        place[row, lane] = 1.0
    place = jnp.asarray(place, jnp.bfloat16)
    w_in_t = w_in.T

    def summed(kept, arrived):
        total = (kept.astype(jnp.float32) + arrived.astype(jnp.float32)).astype(jnp.bfloat16)
        return total.reshape(lat_count, 2, own, BAND, LANES)

    first = mlp_call(0, side, filtered, cotangent, w_in_t, w_in, w_out, forward)
    arrived0 = lax.ppermute(first[2], "lon", swap)
    second = mlp_call(1, side, filtered, cotangent, w_in_t, w_in, w_out, forward)
    down = [(i, (i + 1) % lat_count) for i in range(lat_count)]
    up = [(target, source) for source, target in down]
    sides = lax.ppermute(jnp.concatenate([first[3], second[3]], axis=0), "lon", swap)
    top, top_side = lax.ppermute(
        (second[0][BAND - REACH :], sides[rows - REACH :]), "lat", down
    )
    bottom, bottom_side = lax.ppermute((first[0][:REACH], sides[:REACH]), "lat", up)
    edges = jnp.concatenate([top_side, sides, bottom_side], axis=0)
    arrived1 = lax.ppermute(second[2], "lon", swap)
    total_in, total_out = lax.psum((first[4] + second[4], first[5] + second[5]), ("lat", "lon"))
    sum0, edges = lax.optimization_barrier((summed(first[1], arrived0), edges))
    received0 = exchange(sum0)
    stencil = functools.partial(
        stencil_call, taps=taps, first=first[0], second=second[0], top=top, bottom=bottom,
        edges=edges, place=place,
    )
    q = stencil(0, PARTS, previous=None)
    arrived1, q = lax.optimization_barrier((arrived1, q))
    received1 = exchange(summed(second[1], arrived1))
    q = stencil(1, PARTS, previous=q)
    received0, received1, q = lax.optimization_barrier((received0, received1, q))
    owned, s0, s1 = legendre_call(legendre, received0, received1, gain)
    local0 = exchange(s0)
    local1 = exchange(s1)
    q, owned = lax.optimization_barrier((q, owned))
    disco_part = disco_grad_call(block_input, q)
    disco_part, total_in, total_out = lax.optimization_barrier((disco_part, total_in, total_out))
    total_disco = lax.psum(disco_part, ("lat", "lon"))
    other0 = lax.ppermute(local0, "lon", swap)
    other1 = lax.ppermute(local1, "lon", swap)
    owned = exchange(owned).reshape(M * 2 * degrees, LANES)
    result = final_call(0, side, q, local0, other0, inverse, w_disco, None)
    result = final_call(1, side, q, local1, other1, inverse, w_disco, result)
    grad_gain = grad_gain_call(owned, spectral_saved)
    scale = 1.0 / math.sqrt(NLAT * NLON)
    return (result, grad_gain, total_in * scale, total_out * scale, total_disco * scale)


def shards(*arrays):
    channels, rows, columns = arrays[0].shape
    lat_count = lax.axis_size("lat")
    lon_count = lax.axis_size("lon")
    fits = (
        rows == 2 * BAND
        and lon_count == 2
        and channels == lon_count * LANES
        and columns % (2 * LANES) == 0
        and M == LANES
        and M // lat_count == 8
        and L // lat_count == 8
    )
    return shards_banded(*arrays) if fits else shards_general(*arrays)


def solution(mesh):
    placed = (
        P(None, "lat", "lon"),
        P(None, "lat", "lon"),
        P(None, "lat", "lon"),
        P("lat", "lon", None, None),
        P("lat", "lon", None, None),
        P(),
        P(),
        P(),
        P(),
        P(),
        P(),
        P(),
    )
    return jax.shard_map(
        shards,
        mesh=mesh,
        in_specs=placed,
        out_specs=(P(None, "lat", "lon"), P("lat", "lon", None, None), P(), P(), P()),
        check_vma=False,
    )
```

```python
import functools
import math

import jax
import jax.numpy as jnp
import numpy as np
from jax import lax
from jax.experimental import pallas as pl
from jax.experimental.pallas import tpu as pltpu
from jax.sharding import PartitionSpec as P

NLAT = 512
NLON = 1024
L = 128
M = 128
REACH = 2
NQ = 64


root_half = 0.7071067811865476
root_two_pi = 2.5066282746310002


def padded_2(block, sides, width):
    for axis, dim in sides:
        count = lax.axis_size(axis)
        forward = [(i, i + 1) for i in range(count - 1)]
        forward.append((count - 1, 0))
        backward = [(target, source) for source, target in forward]
        low = lax.ppermute(
            lax.slice_in_dim(block, block.shape[dim] - width, None, axis=dim), axis, forward
        )
        high = lax.ppermute(lax.slice_in_dim(block, 0, width, axis=dim), axis, backward)
        block = jnp.concatenate([low, block, high], axis=dim)
    return block


def gelu_value(value):
    return value * 0.5 * (1.0 + lax.erf(value * root_half))


def gelu_slope(value):
    return (
        0.5 * (1.0 + lax.erf(value * root_half))
        + value * jnp.exp(-0.5 * value * value) / root_two_pi
    )


def legendre_tables():
    degree = np.arange(L)[:, None] * 1.0
    order = np.arange(M)[None, :] * 1.0
    upper = np.where(
        degree > order,
        np.sqrt(
            np.maximum(4.0 * degree * degree - 1.0, 0.0)
            / np.maximum(degree * degree - order * order, 1.0)
        ),
        0.0,
    )
    lower = np.where(
        degree > order + 1.0,
        np.sqrt(
            np.maximum((degree - 1.0) ** 2 - order * order, 0.0)
            / np.maximum(4.0 * (degree - 1.0) ** 2 - 1.0, 1.0)
        ),
        0.0,
    )
    counter = np.arange(1, M) * 1.0
    diagonal_log = np.concatenate(
        [np.zeros(1), np.cumsum(0.5 * np.log((2.0 * counter + 1.0) / (2.0 * counter)))]
    ) - 0.5 * np.log(2.0)
    return (upper, lower, diagonal_log)


def legendre_rows(theta):
    upper, lower, diagonal_log = legendre_tables()
    float_type = theta.dtype
    cosine = jnp.cos(theta)[:, None]
    sine = jnp.sin(theta)
    orders = jnp.arange(M, dtype=jnp.int32)
    start_value = jnp.exp(
        jnp.asarray(diagonal_log, float_type)[None, :]
        + orders.astype(float_type)[None, :] * jnp.log(sine)[:, None]
    )

    def advance(carry, inputs):
        previous, before = carry
        degree, coef_up, coef_low = inputs
        fresh = jnp.where(
            (orders == degree)[None, :],
            start_value,
            coef_up[None, :] * (cosine * previous - coef_low[None, :] * before),
        )
        return ((fresh, previous), fresh)

    empty = jnp.zeros_like(start_value)
    final, table = lax.scan(
        advance,
        (empty, empty),
        (
            jnp.arange(L, dtype=jnp.int32),
            jnp.asarray(upper, float_type),
            jnp.asarray(lower, float_type),
        ),
    )
    weight = jnp.sqrt(sine * (math.pi / NLAT))
    return table * weight[None, :, None]


def forward_table():
    column = jnp.arange(NLON, dtype=jnp.int32)[:, None]
    order = jnp.arange(M, dtype=jnp.int32)[None, :]
    angle = (column * order % NLON).astype(jnp.float32) * (2.0 * math.pi / NLON)
    factor = jnp.where(order == 0, 1.0, 2.0).astype(jnp.float32) / math.sqrt(NLON)
    return jnp.concatenate([factor * jnp.cos(angle), -factor * jnp.sin(angle)], axis=1).astype(
        jnp.bfloat16
    )


def inverse_table():
    order = jnp.arange(M, dtype=jnp.int32)[:, None]
    column = jnp.arange(NLON, dtype=jnp.int32)[None, :]
    angle = (column * order % NLON).astype(jnp.float32) * (2.0 * math.pi / NLON)
    return (jnp.concatenate([jnp.cos(angle), -jnp.sin(angle)], axis=0) / math.sqrt(NLON)).astype(
        jnp.bfloat16
    )


def disco_kernel(quad_weights, lat_offsets, lon_offsets, weight_index):
    span = jnp.arange(-REACH, REACH + 1, dtype=jnp.int32)
    slots = jnp.arange(NQ, dtype=jnp.int32)
    values = jnp.sum(
        jnp.where(
            weight_index[:, :, None] == slots[None, None, :], quad_weights[None, None, :], 0.0
        ),
        axis=2,
    )
    north = (lat_offsets[:, :, None] == span[None, None, :]).astype(quad_weights.dtype)
    east = (lon_offsets[:, :, None] == span[None, None, :]).astype(quad_weights.dtype)
    return jnp.sum(values[:, :, None, None] * north[:, :, :, None] * east[:, :, None, :], axis=1)


def disco_apply(padded, kernel):
    height = kernel.shape[0]
    width = padded.shape[2] - 2 * REACH
    total = jnp.zeros((padded.shape[0], height, width), kernel.dtype)
    for north in range(2 * REACH + 1):
        for east in range(2 * REACH + 1):
            total = (
                total
                + kernel[None, :, north, east, None]
                * padded[:, north : north + height, east : east + width]
            )
    return total


def disco_adjoint(padded, kernel_rim):
    height = kernel_rim.shape[0] - 2 * REACH
    width = padded.shape[2] - 2 * REACH
    total = jnp.zeros((padded.shape[0], height, width), kernel_rim.dtype)
    for north in range(2 * REACH + 1):
        for east in range(2 * REACH + 1):
            row_shift = 2 * REACH - north
            col_shift = 2 * REACH - east
            total = (
                total
                + kernel_rim[None, row_shift : row_shift + height, north, east, None]
                * padded[:, row_shift : row_shift + height, col_shift : col_shift + width]
            )
    return total


def inside_rows(padded, first_row):
    height = padded.shape[1]
    latitude = first_row - REACH + jnp.arange(height, dtype=jnp.int32)
    keep = (latitude >= 0) & (latitude < NLAT)
    return jnp.where(keep[None, :, None], padded, jnp.zeros((), padded.dtype))


def shards_general(
    cotangent,
    block_input,
    filtered,
    spectral_saved,
    spectral_gain,
    w_in,
    w_out,
    w_disco,
    quad_weights,
    lat_offsets,
    lon_offsets,
    weight_index,
):
    channels, rows, columns = cotangent.shape
    lat_count = lax.axis_size("lat")
    first_row = lax.axis_index("lat") * rows
    cells = rows * columns
    flat_in = filtered.reshape(channels, cells)
    flat_cot = cotangent.reshape(channels, cells)
    hidden_pre = lax.dot_general(
        w_in, flat_in, (((0,), (0,)), ((), ())), preferred_element_type=jnp.float32
    )
    activation = gelu_value(hidden_pre).astype(jnp.bfloat16)
    grad_act = jnp.dot(w_out, flat_cot, preferred_element_type=jnp.float32)
    grad_pre = (grad_act * gelu_slope(hidden_pre)).astype(jnp.bfloat16)
    grad_in_part = lax.dot_general(
        flat_in, grad_pre, (((1,), (1,)), ((), ())), preferred_element_type=jnp.float32
    )
    grad_out_part = lax.dot_general(
        activation, flat_cot, (((1,), (1,)), ((), ())), preferred_element_type=jnp.float32
    )
    grad_flat = jnp.dot(w_in, grad_pre, preferred_element_type=jnp.float32).astype(jnp.bfloat16)
    grad_filtered = grad_flat.reshape(channels, rows, columns)
    spread = lax.all_to_all(grad_filtered, "lon", split_axis=0, concat_axis=2, tiled=True)
    local_channels = spread.shape[0]
    coeffs = (
        jnp.dot(
            spread.reshape(local_channels * rows, NLON),
            forward_table(),
            preferred_element_type=jnp.float32,
        )
        .astype(jnp.bfloat16)
        .reshape(local_channels, rows, 2, M)
    )
    theta_rows = ((first_row + jnp.arange(rows, dtype=jnp.int32)).astype(jnp.float32) + 0.5) * (
        math.pi / NLAT
    )
    legendre = legendre_rows(theta_rows).astype(jnp.bfloat16)
    owned_count = L // lat_count
    weights = lax.slice_in_dim(legendre, 0, owned_count * lax.axis_size("lat"), axis=0)
    owned = lax.psum_scatter(
        jnp.einsum("ljm,cjrm->lcrm", weights, coeffs, preferred_element_type=jnp.float32),
        "lat",
        scatter_dimension=0,
        tiled=True,
    )
    real_part = owned[:, :, 0]
    imag_part = owned[:, :, 1]
    grad_gain = jnp.stack(
        [
            real_part * spectral_saved[:, :, 0] + imag_part * spectral_saved[:, :, 1],
            imag_part * spectral_saved[:, :, 0] - real_part * spectral_saved[:, :, 1],
        ],
        axis=2,
    )
    scaled = jnp.stack(
        [
            spectral_gain[:, :, 0] * real_part + spectral_gain[:, :, 1] * imag_part,
            spectral_gain[:, :, 0] * imag_part - spectral_gain[:, :, 1] * real_part,
        ],
        axis=2,
    ).astype(jnp.bfloat16)
    piece = lax.all_gather(scaled, "lat", axis=0, tiled=True)
    weights = lax.slice_in_dim(legendre, 0, piece.shape[0], axis=0)
    synthesis = (
        jnp.zeros((local_channels, rows, 2, M), jnp.float32)
        + jnp.einsum("ljm,lcrm->cjrm", weights, piece, preferred_element_type=jnp.float32)
    ).astype(jnp.bfloat16)
    grid_rows = jnp.dot(
        synthesis.reshape(local_channels * rows, 2 * M),
        inverse_table(),
        preferred_element_type=jnp.float32,
    ).reshape(local_channels, rows, NLON)
    spectral_grad = lax.all_to_all(grid_rows, "lon", split_axis=2, concat_axis=0, tiled=True)
    kernel = disco_kernel(quad_weights, lat_offsets, lon_offsets, weight_index)
    kernel_pad = jnp.pad(kernel, ((REACH, REACH), (0, 0), (0, 0)))
    kernel_rim = lax.dynamic_slice_in_dim(kernel_pad, first_row, rows + 2 * REACH, 0)
    stacked_rims = padded_2(
        jnp.stack((block_input, grad_filtered)), (("lat", 2), ("lon", 3)), REACH
    )
    input_pad = inside_rows(stacked_rims[0], first_row)
    grad_source = inside_rows(stacked_rims[1], first_row)
    grad_pad = lax.dot_general(
        w_disco, grad_source, (((1,), (0,)), ((), ())), preferred_element_type=jnp.float32
    ).astype(jnp.bfloat16)
    mixed = disco_apply(input_pad, kernel_rim[REACH : REACH + rows]).astype(jnp.bfloat16)
    grad_disco_part = lax.dot_general(
        mixed.reshape(channels, cells),
        grad_flat,
        (((1,), (1,)), ((), ())),
        preferred_element_type=jnp.float32,
    )
    disco_grad = disco_adjoint(grad_pad, kernel_rim)
    grad_input = (spectral_grad + disco_grad).astype(jnp.bfloat16)
    total_in, total_out, total_disco = lax.psum(
        (grad_in_part, grad_out_part, grad_disco_part), ("lat", "lon")
    )
    scale = 1.0 / math.sqrt(NLAT * NLON)
    return (grad_input, grad_gain, total_in * scale, total_out * scale, total_disco * scale)


BAND = 16
LANES = 128
PARTS = 2
MIB = 1024 * 1024


def mm(a, b):
    return jnp.dot(a, b, preferred_element_type=jnp.float32)


def mm_nt(a, b):
    return lax.dot_general(a, b, (((1,), (1,)), ((), ())), preferred_element_type=jnp.float32)


def mm_tn(a, b):
    return lax.dot_general(a, b, (((0,), (0,)), ((), ())), preferred_element_type=jnp.float32)


def params(mib):
    return pltpu.CompilerParams(vmem_limit_bytes=mib * MIB)


def whole_block(shape):
    return pl.BlockSpec(shape, lambda *_: (0,) * len(shape))


def rows_first(block, stage, flat, width):
    channels = block.shape[0]
    for tile in range(width // LANES):
        stage[tile] = (
            block[:, :, tile * LANES : (tile + 1) * LANES]
            .astype(jnp.float32)
            .reshape(channels * BAND, LANES)
        )
    for row in range(BAND):
        for tile in range(width // LANES):
            start = row * width + tile * LANES
            flat[:, start : start + LANES] = stage[
                tile, pl.ds(row, channels, stride=BAND), :
            ].astype(jnp.bfloat16)


def gelu_both(value):
    decay = jnp.exp(value * value * -0.5)
    base = 1.0 + (0.3275911 * root_half) * jnp.abs(value)
    inverse = pl.reciprocal(base, approx=True)
    inverse = inverse * (2.0 - base * inverse)
    poly = 0.5 * 1.061405429
    for term in (-1.453152027, 1.421413741, -0.284496736, 0.254829592):
        poly = poly * inverse + 0.5 * term
    tail = poly * inverse * decay
    chance = jnp.where(value >= 0.0, 1.0 - tail, tail)
    return chance, decay


def mlp_kernel(
    side, x_ref, ct_ref, win_t, win, wout, table,
    gf_ref, own_ref, send_ref, edge_ref, gin_ref, gout_ref,
    stage, xs, cs, low, high,
    *, steps, width, chunk,
):
    step = pl.program_id(0)

    @pl.when(step == 0)
    def _():
        gin_ref[...] = jnp.zeros_like(gin_ref)
        gout_ref[...] = jnp.zeros_like(gout_ref)

    rows_first(x_ref, stage, xs, width)
    rows_first(ct_ref, stage, cs, width)
    column = pl.multiple_of(step * width, width)
    per = chunk // width

    def body(index, carry):
        cells = pl.ds(pl.multiple_of(index * chunk, chunk), chunk)
        x = xs[:, cells]
        c = cs[:, cells]
        pre = mm(win_t[...], x)
        grad = mm(wout[...], c)
        chance, decay = gelu_both(pre)
        act = (pre * chance).astype(jnp.bfloat16)
        gp = (grad * (chance + pre * decay * (1.0 / root_two_pi))).astype(jnp.bfloat16)
        gf = mm(win[...], gp).astype(jnp.bfloat16)
        for part in range(per):
            gf_ref[index * per + part, :, pl.ds(column, width)] = gf[
                :, part * width : (part + 1) * width
            ]
        gin_ref[...] += mm_nt(x, gp)
        gout_ref[...] += mm_nt(act, c)
        return carry

    lax.fori_loop(0, BAND * width // chunk, body, 0)

    @pl.when(step == steps - 1)
    def _():
        orders = low.shape[0] // BAND

        def transform(row, carry):
            out = mm_nt(table[...], gf_ref[row])
            low[pl.ds(row, orders, stride=BAND), :] = out[:orders, :LANES]
            high[pl.ds(row, orders, stride=BAND), :] = out[:orders, LANES:]
            edge_ref[row] = out[orders:].astype(jnp.bfloat16)
            return carry

        lax.fori_loop(0, BAND, transform, 0)
        first = side[0] == 0
        shape = own_ref.shape

        @pl.when(first)
        def _():
            own_ref[...] = low[...].astype(jnp.bfloat16).reshape(shape)
            send_ref[...] = high[...].astype(jnp.bfloat16).reshape(shape)

        @pl.when(jnp.logical_not(first))
        def _():
            own_ref[...] = high[...].astype(jnp.bfloat16).reshape(shape)
            send_ref[...] = low[...].astype(jnp.bfloat16).reshape(shape)


def mlp_call(band, side, filtered, cotangent, win_t, win, wout, table):
    channels, rows, columns = filtered.shape
    hidden = wout.shape[0]
    width = LANES
    steps = columns // width
    chunk = 4 * width
    orders = table.shape[0] - 16
    block = pl.BlockSpec((channels, BAND, width), lambda i: (0, band, i))
    cells = BAND * columns
    return pl.pallas_call(
        functools.partial(mlp_kernel, steps=steps, width=width, chunk=chunk),
        grid=(steps,),
        in_specs=[
            pl.BlockSpec(memory_space=pltpu.SMEM),
            block,
            block,
            whole_block(win_t.shape),
            whole_block(win.shape),
            whole_block(wout.shape),
            whole_block(table.shape),
        ],
        out_specs=[
            whole_block((BAND, channels, columns)),
            whole_block((orders, BAND, LANES)),
            whole_block((orders, BAND, LANES)),
            whole_block((BAND, 16, channels)),
            whole_block((channels, hidden)),
            whole_block((hidden, channels)),
        ],
        out_shape=[
            jax.ShapeDtypeStruct((BAND, channels, columns), jnp.bfloat16),
            jax.ShapeDtypeStruct((orders, BAND, LANES), jnp.bfloat16),
            jax.ShapeDtypeStruct((orders, BAND, LANES), jnp.bfloat16),
            jax.ShapeDtypeStruct((BAND, 16, channels), jnp.bfloat16),
            jax.ShapeDtypeStruct((channels, hidden), jnp.float32),
            jax.ShapeDtypeStruct((hidden, channels), jnp.float32),
        ],
        scratch_shapes=[
            pltpu.VMEM((width // LANES, channels * BAND, LANES), jnp.float32),
            pltpu.VMEM((channels, BAND * width), jnp.bfloat16),
            pltpu.VMEM((channels, BAND * width), jnp.bfloat16),
            pltpu.VMEM((orders * BAND, LANES), jnp.float32),
            pltpu.VMEM((orders * BAND, LANES), jnp.float32),
        ],
        compiler_params=params(56),
        cost_estimate=pl.CostEstimate(
            flops=2 * cells * channels * (5 * hidden + orders),
            bytes_accessed=6 * channels * cells,
            transcendentals=2 * hidden * cells,
        ),
        name="mlp",
    )(side, filtered, cotangent, win_t, win, wout, table)


def stencil_kernel(taps, first, second, top, bottom, edges, place, *rest, rows):
    q_ref, field, rim = rest[-3:]
    channels, columns = field.shape[1:]
    field[0:REACH] = top[...]
    field[REACH : REACH + BAND] = first[...]
    field[REACH + BAND : REACH + 2 * BAND] = second[...]
    field[rows + REACH :] = bottom[...]

    def spread(row, carry):
        rim[row] = mm_tn(edges[row], place[...])[: rim.shape[1]].astype(jnp.bfloat16)
        return carry

    lax.fori_loop(0, rows + 2 * REACH, spread, 0)
    lane = lax.broadcasted_iota(jnp.int32, (16, LANES), 1)
    span = 2 * REACH + 1

    def row_body(row, carry):
        def tile_body(tile, inner):
            part = pl.ds(pl.multiple_of(tile * 16, 16), 16)
            sums = [None] * span
            for north in range(span):
                source = row + 2 * REACH - north
                here = field[source, part, :]
                ends = rim[source, part, :]
                for east in range(span):
                    past = east - REACH
                    shifted = here
                    if past < 0:
                        rim_tile = jnp.where(lane < -past, ends, here[:, :LANES])
                        shifted = jnp.concatenate([rim_tile, here[:, LANES:]], axis=1)
                    if past > 0:
                        rim_tile = jnp.where(lane >= LANES - past, ends, here[:, -LANES:])
                        shifted = jnp.concatenate([here[:, :-LANES], rim_tile], axis=1)
                    weight = taps[(source * span + north) * span + east].astype(jnp.bfloat16)
                    term = shifted * weight
                    sums[east] = term if sums[east] is None else sums[east] + term
            total = sums[REACH].astype(jnp.float32)
            for east in range(span):
                if east != REACH:
                    moved = pltpu.roll(sums[east], (east - REACH) % columns, 1)
                    total = total + moved.astype(jnp.float32)
            q_ref[row, part, :] = total.astype(jnp.bfloat16)
            return inner

        return lax.fori_loop(0, channels // 16, tile_body, carry)

    lax.fori_loop(0, rows, row_body, 0)


def stencil_call(part, parts, taps, first, second, top, bottom, edges, place, previous):
    rows = edges.shape[0] - 2 * REACH
    _, channels, columns = first.shape
    some = channels // parts
    extra = [] if previous is None else [previous]

    def piece(count):
        return pl.BlockSpec((count, some, columns), lambda i: (0, part, 0))

    return pl.pallas_call(
        functools.partial(stencil_kernel, rows=rows),
        grid=(1,),
        in_specs=[
            pl.BlockSpec(memory_space=pltpu.SMEM),
            piece(BAND),
            piece(BAND),
            piece(REACH),
            piece(REACH),
            pl.BlockSpec(edges.shape[:2] + (LANES,), lambda i: (0, 0, part * some // LANES)),
            pl.BlockSpec(memory_space=pltpu.VMEM),
        ]
        + [pl.BlockSpec(memory_space=pl.ANY)] * len(extra),
        out_specs=piece(rows),
        out_shape=jax.ShapeDtypeStruct((rows, channels, columns), jnp.bfloat16),
        scratch_shapes=[
            pltpu.VMEM((rows + 2 * REACH, some, columns), jnp.bfloat16),
            pltpu.VMEM((rows + 2 * REACH, some, LANES), jnp.bfloat16),
        ],
        input_output_aliases={7: 0} if extra else {},
        compiler_params=params(48),
        cost_estimate=pl.CostEstimate(
            flops=60 * some * rows * columns,
            bytes_accessed=4 * some * rows * columns,
            transcendentals=0,
        ),
        name="stencil",
    )(taps, first, second, top, bottom, edges, place, *extra)


def disco_kernel_grad(bi_ref, q_ref, gd_ref, stage, flat):
    columns = q_ref.shape[2]

    @pl.when(pl.program_id(0) == 0)
    def _():
        gd_ref[...] = jnp.zeros_like(gd_ref)

    rows_first(bi_ref, stage, flat, columns)

    def body(row, carry):
        cells = pl.ds(pl.multiple_of(row * columns, columns), columns)
        gd_ref[...] += mm_nt(flat[:, cells], q_ref[row])
        return carry

    lax.fori_loop(0, BAND, body, 0)


def disco_grad_call(block_input, q):
    channels, rows, columns = block_input.shape
    return pl.pallas_call(
        disco_kernel_grad,
        grid=(rows // BAND,),
        in_specs=[
            pl.BlockSpec((channels, BAND, columns), lambda i: (0, i, 0)),
            pl.BlockSpec((BAND, channels, columns), lambda i: (i, 0, 0)),
        ],
        out_specs=whole_block((channels, channels)),
        out_shape=jax.ShapeDtypeStruct((channels, channels), jnp.float32),
        scratch_shapes=[
            pltpu.VMEM((columns // LANES, channels * BAND, LANES), jnp.float32),
            pltpu.VMEM((channels, BAND * columns), jnp.bfloat16),
        ],
        compiler_params=params(48),
        cost_estimate=pl.CostEstimate(
            flops=2 * channels * channels * rows * columns,
            bytes_accessed=4 * channels * rows * columns,
            transcendentals=0,
        ),
        name="disco_weight",
    )(block_input, q)


def legendre_kernel(leg, r0, r1, gain, owned_ref, s0, s1, stage, *, steps, block):
    order = pl.program_id(0)
    degrees = leg.shape[1]
    half = leg.shape[2] // 2
    total = None
    for band, ref in enumerate((r0, r1)):
        pair = jnp.concatenate(
            [ref[:, r].reshape(half, LANES) for r in range(2)], axis=1
        )
        term = mm(leg[0, :, band * half : (band + 1) * half], pair)
        total = term if total is None else total + term
    real = total[:, :LANES]
    imag = total[:, LANES:]
    owned_ref[:, 0, 0] = real.reshape(owned_ref.shape[0], -1, LANES)
    owned_ref[:, 0, 1] = imag.reshape(owned_ref.shape[0], -1, LANES)
    g = gain[:, 0, 0].reshape(degrees, LANES)
    k = gain[:, 0, 1].reshape(degrees, LANES)
    scaled = jnp.concatenate([g * real + k * imag, g * imag - k * real], axis=1).astype(
        jnp.bfloat16
    )
    synth = mm_tn(leg[0], scaled)
    for r in range(2):
        stage[pl.ds(r * steps + order, 2 * half, stride=block), :] = synth[
            :, r * LANES : (r + 1) * LANES
        ]

    @pl.when(order == steps - 1)
    def _():
        s0[...] = stage[: half * block].astype(jnp.bfloat16).reshape(s0.shape)
        s1[...] = stage[half * block :].astype(jnp.bfloat16).reshape(s1.shape)


def legendre_call(leg, r0, r1, gain):
    owners, _, steps, band, lanes = r0.shape
    degrees = leg.shape[1]
    block = 2 * steps
    r_spec = pl.BlockSpec((owners, 2, None, band, lanes), lambda m: (0, 0, m, 0, 0))
    g_shape = (owners, 1, 2, degrees // owners, lanes)
    g_spec = pl.BlockSpec(g_shape, lambda m: (0, m, 0, 0, 0))
    out = (owners, band, block, lanes)
    return pl.pallas_call(
        functools.partial(legendre_kernel, steps=steps, block=block),
        grid=(steps,),
        in_specs=[
            pl.BlockSpec((1, degrees, leg.shape[2]), lambda m: (m, 0, 0)),
            r_spec,
            r_spec,
            g_spec,
        ],
        out_specs=[g_spec, whole_block(out), whole_block(out)],
        out_shape=[
            jax.ShapeDtypeStruct(gain.shape, jnp.float32),
            jax.ShapeDtypeStruct(out, jnp.bfloat16),
            jax.ShapeDtypeStruct(out, jnp.bfloat16),
        ],
        scratch_shapes=[pltpu.VMEM((2 * owners * band * block, lanes), jnp.float32)],
        compiler_params=params(48),
        cost_estimate=pl.CostEstimate(
            flops=8 * steps * degrees * leg.shape[2] * 256,
            bytes_accessed=7 * MIB,
            transcendentals=0,
        ),
        name="legendre",
    )(leg, r0, r1, gain)


def final_kernel(side, q_ref, own, other, table, wd, *rest):
    out_ref, stage = rest[-2:]
    width = q_ref.shape[2]
    orders = table.shape[0]

    def body(row, carry):
        q = q_ref[row]
        for half, ref in enumerate((own, other)):
            base = pl.multiple_of((side[0] + half) % 2 * LANES, LANES)
            synth = ref[:, row].reshape(orders, LANES)
            out = mm_tn(synth, table[...]) + mm(wd[pl.ds(base, LANES), :], q)
            for tile in range(width // LANES):
                stage[tile, pl.ds(base * BAND + row, LANES, stride=BAND), :] = out[
                    :, tile * LANES : (tile + 1) * LANES
                ]
        return carry

    lax.fori_loop(0, BAND, body, 0)
    channels = out_ref.shape[0]
    for tile in range(width // LANES):
        out_ref[:, :, tile * LANES : (tile + 1) * LANES] = (
            stage[tile].astype(jnp.bfloat16).reshape(channels, BAND, LANES)
        )


def final_call(band, side, q, own, other, table, wd, previous):
    rows, channels, columns = q.shape
    width = 2 * LANES
    cells = BAND * columns
    extra = [] if previous is None else [previous]
    return pl.pallas_call(
        final_kernel,
        grid=(columns // width,),
        in_specs=[
            pl.BlockSpec(memory_space=pltpu.SMEM),
            pl.BlockSpec((BAND, channels, width), lambda i: (band, 0, i)),
            whole_block(own.shape),
            whole_block(other.shape),
            pl.BlockSpec((table.shape[0], width), lambda i: (0, i)),
            whole_block(wd.shape),
        ]
        + [pl.BlockSpec(memory_space=pl.ANY)] * len(extra),
        out_specs=pl.BlockSpec((channels, BAND, width), lambda i: (0, band, i)),
        out_shape=jax.ShapeDtypeStruct((channels, rows, columns), jnp.bfloat16),
        scratch_shapes=[pltpu.VMEM((width // LANES, channels * BAND, LANES), jnp.float32)],
        input_output_aliases={6: 0} if extra else {},
        compiler_params=params(48),
        cost_estimate=pl.CostEstimate(
            flops=2 * cells * channels * (channels + table.shape[0]),
            bytes_accessed=5 * channels * cells,
            transcendentals=0,
        ),
        name="final",
    )(side, q, own, other, table, wd, *extra)


def gain_kernel(gain, out, *, degrees):
    for degree in range(degrees):
        for r in range(2):
            part = gain[pl.ds(degree * 2 * LANES + r, LANES, stride=2), :]
            out[pl.ds(r * degrees + degree, LANES, stride=2 * degrees), :] = part.T


def gain_call(gain):
    degrees, channels, _, orders = gain.shape
    flat = gain.reshape(degrees * channels * 2, orders)
    return pl.pallas_call(
        functools.partial(gain_kernel, degrees=degrees),
        out_shape=jax.ShapeDtypeStruct((orders * 2 * degrees, channels), jnp.float32),
        name="gain",
    )(flat)


def grad_gain_kernel(owned, saved, out, *, degrees):
    for degree in range(degrees):
        real = owned[pl.ds(degree, LANES, stride=2 * degrees), :].T
        imag = owned[pl.ds(degrees + degree, LANES, stride=2 * degrees), :].T
        start = degree * 2 * LANES
        s = saved[pl.ds(start, LANES, stride=2), :]
        t = saved[pl.ds(start + 1, LANES, stride=2), :]
        out[pl.ds(start, LANES, stride=2), :] = real * s + imag * t
        out[pl.ds(start + 1, LANES, stride=2), :] = imag * s - real * t


def grad_gain_call(owned, saved):
    degrees, channels, _, orders = saved.shape
    flat = saved.reshape(degrees * channels * 2, orders)
    out = pl.pallas_call(
        functools.partial(grad_gain_kernel, degrees=degrees),
        out_shape=jax.ShapeDtypeStruct(flat.shape, jnp.float32),
        name="grad_gain",
    )(owned, flat)
    return out.reshape(saved.shape)


def legendre_whole():
    upper, lower, diagonal_log = legendre_tables()
    theta = (np.arange(NLAT) + 0.5) * (math.pi / NLAT)
    sine, cosine = np.sin(theta)[None], np.cos(theta)[None]
    orders = np.arange(M)
    start = np.exp(diagonal_log[:, None] + orders[:, None] * np.log(sine))
    table = np.zeros((M, L, NLAT))
    previous = before = np.zeros((M, NLAT))
    for degree in range(L):
        fresh = np.where(
            (orders == degree)[:, None],
            start,
            upper[degree][:, None] * (cosine * previous - lower[degree][:, None] * before),
        )
        table[:, degree] = fresh
        previous, before = fresh, previous
    return table * np.sqrt(sine * (math.pi / NLAT))[None]


def host_tables(lat_count, lon_count):
    columns, rows, own = NLON // lon_count, NLAT // lat_count, M // lat_count
    angle = (np.arange(M)[:, None] * np.arange(NLON)[None, :] % NLON) * (2.0 * math.pi / NLON)
    waves = np.stack([np.cos(angle), -np.sin(angle)]) / math.sqrt(NLON)
    factor = np.where(np.arange(M) == 0, 1.0, 2.0)[None, :, None]

    def arrange(table):
        table = table.reshape(2, lat_count, own, lon_count, columns)
        return table.transpose(3, 1, 0, 2, 4).reshape(lon_count, 2 * M, columns)

    pick = np.zeros((lon_count, 16, columns))
    for row, column in enumerate((0, 1, columns - 2, columns - 1)):
        pick[:, row, column] = 1.0
    forward = np.concatenate([arrange(waves * factor), pick], axis=1)
    legendre = legendre_whole().reshape(M, L, lat_count, rows // BAND, BAND)
    legendre = legendre.transpose(0, 1, 3, 2, 4).reshape(M, L, NLAT)
    kind = jnp.bfloat16
    return forward.astype(kind), arrange(waves).astype(kind), legendre.astype(kind)


def shards_banded(
    cotangent,
    block_input,
    filtered,
    spectral_saved,
    spectral_gain,
    w_in,
    w_out,
    w_disco,
    quad_weights,
    lat_offsets,
    lon_offsets,
    weight_index,
):
    channels, rows, columns = cotangent.shape
    lat_count = lax.axis_size("lat")
    lon_count = lax.axis_size("lon")
    lat_index = lax.axis_index("lat")
    lon_index = lax.axis_index("lon")
    own = M // lat_count
    degrees = L // lat_count
    side = lon_index.reshape(1).astype(jnp.int32)
    forward, inverse, legendre = host_tables(lat_count, lon_count)
    forward = lax.dynamic_index_in_dim(jnp.asarray(forward), lon_index, 0, keepdims=False)
    inverse = lax.dynamic_index_in_dim(jnp.asarray(inverse), lon_index, 0, keepdims=False)
    legendre = lax.dynamic_slice_in_dim(jnp.asarray(legendre), lat_index * own, own, 0)
    swap = [(i, (i + 1) % lon_count) for i in range(lon_count)]
    exchange = functools.partial(lax.all_to_all, axis_name="lat", split_axis=0, concat_axis=0, tiled=True)

    kernel = disco_kernel(quad_weights, lat_offsets, lon_offsets, weight_index)
    kernel_pad = jnp.pad(kernel, ((REACH, REACH), (0, 0), (0, 0)))
    kernel_rim = lax.dynamic_slice_in_dim(kernel_pad, lat_index * rows, rows + 2 * REACH, 0)
    taps = kernel_rim.reshape(-1)
    place = np.zeros((16, LANES), np.float32)
    for row, lane in enumerate((0, 1, LANES - 2, LANES - 1)):
        place[row, lane] = 1.0
    place = jnp.asarray(place, jnp.bfloat16)
    w_in_t = w_in.T

    def summed(kept, arrived):
        total = (kept.astype(jnp.float32) + arrived.astype(jnp.float32)).astype(jnp.bfloat16)
        return total.reshape(lat_count, 2, own, BAND, LANES)

    first = mlp_call(0, side, filtered, cotangent, w_in_t, w_in, w_out, forward)
    arrived0 = lax.ppermute(first[2], "lon", swap)
    second = mlp_call(1, side, filtered, cotangent, w_in_t, w_in, w_out, forward)
    down = [(i, (i + 1) % lat_count) for i in range(lat_count)]
    up = [(target, source) for source, target in down]
    sides = lax.ppermute(jnp.concatenate([first[3], second[3]], axis=0), "lon", swap)
    top, top_side = lax.ppermute(
        (second[0][BAND - REACH :], sides[rows - REACH :]), "lat", down
    )
    bottom, bottom_side = lax.ppermute((first[0][:REACH], sides[:REACH]), "lat", up)
    edges = jnp.concatenate([top_side, sides, bottom_side], axis=0)
    arrived1 = lax.ppermute(second[2], "lon", swap)
    spectral_gain, kept1 = lax.optimization_barrier((spectral_gain, second[1]))
    gain = gain_call(spectral_gain).reshape(lat_count, own, 2, degrees, LANES)
    sums = (first[4] + second[4], first[5] + second[5])
    sum0, gain, sums, edges = lax.optimization_barrier(
        (summed(first[1], arrived0), gain, sums, edges)
    )
    received0 = exchange(sum0)
    gain = exchange(gain)
    stencil = functools.partial(
        stencil_call, taps=taps, first=first[0], second=second[0], top=top, bottom=bottom,
        edges=edges, place=place,
    )
    q = stencil(0, PARTS, previous=None)
    arrived1, q = lax.optimization_barrier((arrived1, q))
    received1 = exchange(summed(kept1, arrived1))
    q = stencil(1, PARTS, previous=q)
    received0, received1, q = lax.optimization_barrier((received0, received1, q))
    owned, s0, s1 = legendre_call(legendre, received0, received1, gain)
    local0 = exchange(s0)
    local1 = exchange(s1)
    q, owned = lax.optimization_barrier((q, owned))
    disco_part = disco_grad_call(block_input, q)
    local0, disco_part = lax.optimization_barrier((local0, disco_part))
    other0 = lax.ppermute(local0, "lon", swap)
    everyone = functools.partial(
        lax.all_to_all, axis_name=("lat", "lon"), split_axis=0, concat_axis=0, tiled=True
    )
    count = lat_count * lon_count
    half = w_in.shape[1] // 2
    parts = (sums[0][:, :half], sums[0][:, half:], sums[1], disco_part)
    stacked = jnp.concatenate(parts, axis=0).astype(jnp.bfloat16)
    shares = everyone(stacked.reshape(count, -1, channels)).astype(jnp.float32).sum(axis=0)
    shares = jnp.broadcast_to(shares.astype(jnp.bfloat16)[None], (count,) + shares.shape)
    totals = everyone(shares).reshape(-1, channels).astype(jnp.float32)
    total_in = jnp.concatenate([totals[:channels], totals[channels : 2 * channels]], axis=1)
    total_out, total_disco = jnp.split(totals[2 * channels :], (2 * half,), axis=0)
    other1 = lax.ppermute(local1, "lon", swap)
    owned = exchange(owned).reshape(M * 2 * degrees, LANES)
    result = final_call(0, side, q, local0, other0, inverse, w_disco, None)
    result = final_call(1, side, q, local1, other1, inverse, w_disco, result)
    grad_gain = grad_gain_call(owned, spectral_saved)
    scale = 1.0 / math.sqrt(NLAT * NLON)
    return (result, grad_gain, total_in * scale, total_out * scale, total_disco * scale)


def shards(*arrays):
    channels, rows, columns = arrays[0].shape
    lat_count = lax.axis_size("lat")
    lon_count = lax.axis_size("lon")
    fits = (
        rows == 2 * BAND
        and lon_count == 2
        and channels == lon_count * LANES
        and columns % (2 * LANES) == 0
        and M == LANES
        and M // lat_count == 8
        and L // lat_count == 8
    )
    return shards_banded(*arrays) if fits else shards_general(*arrays)


def solution(mesh):
    placed = (
        P(None, "lat", "lon"),
        P(None, "lat", "lon"),
        P(None, "lat", "lon"),
        P("lat", "lon", None, None),
        P("lat", "lon", None, None),
        P(),
        P(),
        P(),
        P(),
        P(),
        P(),
        P(),
    )
    return jax.shard_map(
        shards,
        mesh=mesh,
        in_specs=placed,
        out_specs=(P(None, "lat", "lon"), P("lat", "lon", None, None), P(), P(), P()),
        check_vma=False,
    )
```

```python
import functools
import math

import jax
import jax.numpy as jnp
import numpy as np
from jax import lax
from jax.experimental import pallas as pl
from jax.experimental.pallas import tpu as pltpu
from jax.sharding import PartitionSpec as P

NLAT = 512
NLON = 1024
L = 128
M = 128
REACH = 2
NQ = 64


root_half = 0.7071067811865476
root_two_pi = 2.5066282746310002


def padded_2(block, sides, width):
    for axis, dim in sides:
        count = lax.axis_size(axis)
        forward = [(i, i + 1) for i in range(count - 1)]
        forward.append((count - 1, 0))
        backward = [(target, source) for source, target in forward]
        low = lax.ppermute(
            lax.slice_in_dim(block, block.shape[dim] - width, None, axis=dim), axis, forward
        )
        high = lax.ppermute(lax.slice_in_dim(block, 0, width, axis=dim), axis, backward)
        block = jnp.concatenate([low, block, high], axis=dim)
    return block


def gelu_value(value):
    return value * 0.5 * (1.0 + lax.erf(value * root_half))


def gelu_slope(value):
    return (
        0.5 * (1.0 + lax.erf(value * root_half))
        + value * jnp.exp(-0.5 * value * value) / root_two_pi
    )


def legendre_tables():
    degree = np.arange(L)[:, None] * 1.0
    order = np.arange(M)[None, :] * 1.0
    upper = np.where(
        degree > order,
        np.sqrt(
            np.maximum(4.0 * degree * degree - 1.0, 0.0)
            / np.maximum(degree * degree - order * order, 1.0)
        ),
        0.0,
    )
    lower = np.where(
        degree > order + 1.0,
        np.sqrt(
            np.maximum((degree - 1.0) ** 2 - order * order, 0.0)
            / np.maximum(4.0 * (degree - 1.0) ** 2 - 1.0, 1.0)
        ),
        0.0,
    )
    counter = np.arange(1, M) * 1.0
    diagonal_log = np.concatenate(
        [np.zeros(1), np.cumsum(0.5 * np.log((2.0 * counter + 1.0) / (2.0 * counter)))]
    ) - 0.5 * np.log(2.0)
    return (upper, lower, diagonal_log)


def legendre_rows(theta):
    upper, lower, diagonal_log = legendre_tables()
    float_type = theta.dtype
    cosine = jnp.cos(theta)[:, None]
    sine = jnp.sin(theta)
    orders = jnp.arange(M, dtype=jnp.int32)
    start_value = jnp.exp(
        jnp.asarray(diagonal_log, float_type)[None, :]
        + orders.astype(float_type)[None, :] * jnp.log(sine)[:, None]
    )

    def advance(carry, inputs):
        previous, before = carry
        degree, coef_up, coef_low = inputs
        fresh = jnp.where(
            (orders == degree)[None, :],
            start_value,
            coef_up[None, :] * (cosine * previous - coef_low[None, :] * before),
        )
        return ((fresh, previous), fresh)

    empty = jnp.zeros_like(start_value)
    final, table = lax.scan(
        advance,
        (empty, empty),
        (
            jnp.arange(L, dtype=jnp.int32),
            jnp.asarray(upper, float_type),
            jnp.asarray(lower, float_type),
        ),
    )
    weight = jnp.sqrt(sine * (math.pi / NLAT))
    return table * weight[None, :, None]


def forward_table():
    column = jnp.arange(NLON, dtype=jnp.int32)[:, None]
    order = jnp.arange(M, dtype=jnp.int32)[None, :]
    angle = (column * order % NLON).astype(jnp.float32) * (2.0 * math.pi / NLON)
    factor = jnp.where(order == 0, 1.0, 2.0).astype(jnp.float32) / math.sqrt(NLON)
    return jnp.concatenate([factor * jnp.cos(angle), -factor * jnp.sin(angle)], axis=1).astype(
        jnp.bfloat16
    )


def inverse_table():
    order = jnp.arange(M, dtype=jnp.int32)[:, None]
    column = jnp.arange(NLON, dtype=jnp.int32)[None, :]
    angle = (column * order % NLON).astype(jnp.float32) * (2.0 * math.pi / NLON)
    return (jnp.concatenate([jnp.cos(angle), -jnp.sin(angle)], axis=0) / math.sqrt(NLON)).astype(
        jnp.bfloat16
    )


def disco_kernel(quad_weights, lat_offsets, lon_offsets, weight_index):
    span = jnp.arange(-REACH, REACH + 1, dtype=jnp.int32)
    slots = jnp.arange(NQ, dtype=jnp.int32)
    values = jnp.sum(
        jnp.where(
            weight_index[:, :, None] == slots[None, None, :], quad_weights[None, None, :], 0.0
        ),
        axis=2,
    )
    north = (lat_offsets[:, :, None] == span[None, None, :]).astype(quad_weights.dtype)
    east = (lon_offsets[:, :, None] == span[None, None, :]).astype(quad_weights.dtype)
    return jnp.sum(values[:, :, None, None] * north[:, :, :, None] * east[:, :, None, :], axis=1)


def disco_apply(padded, kernel):
    height = kernel.shape[0]
    width = padded.shape[2] - 2 * REACH
    total = jnp.zeros((padded.shape[0], height, width), kernel.dtype)
    for north in range(2 * REACH + 1):
        for east in range(2 * REACH + 1):
            total = (
                total
                + kernel[None, :, north, east, None]
                * padded[:, north : north + height, east : east + width]
            )
    return total


def disco_adjoint(padded, kernel_rim):
    height = kernel_rim.shape[0] - 2 * REACH
    width = padded.shape[2] - 2 * REACH
    total = jnp.zeros((padded.shape[0], height, width), kernel_rim.dtype)
    for north in range(2 * REACH + 1):
        for east in range(2 * REACH + 1):
            row_shift = 2 * REACH - north
            col_shift = 2 * REACH - east
            total = (
                total
                + kernel_rim[None, row_shift : row_shift + height, north, east, None]
                * padded[:, row_shift : row_shift + height, col_shift : col_shift + width]
            )
    return total


def inside_rows(padded, first_row):
    height = padded.shape[1]
    latitude = first_row - REACH + jnp.arange(height, dtype=jnp.int32)
    keep = (latitude >= 0) & (latitude < NLAT)
    return jnp.where(keep[None, :, None], padded, jnp.zeros((), padded.dtype))


def shards_general(
    cotangent,
    block_input,
    filtered,
    spectral_saved,
    spectral_gain,
    w_in,
    w_out,
    w_disco,
    quad_weights,
    lat_offsets,
    lon_offsets,
    weight_index,
):
    channels, rows, columns = cotangent.shape
    lat_count = lax.axis_size("lat")
    first_row = lax.axis_index("lat") * rows
    cells = rows * columns
    flat_in = filtered.reshape(channels, cells)
    flat_cot = cotangent.reshape(channels, cells)
    hidden_pre = lax.dot_general(
        w_in, flat_in, (((0,), (0,)), ((), ())), preferred_element_type=jnp.float32
    )
    activation = gelu_value(hidden_pre).astype(jnp.bfloat16)
    grad_act = jnp.dot(w_out, flat_cot, preferred_element_type=jnp.float32)
    grad_pre = (grad_act * gelu_slope(hidden_pre)).astype(jnp.bfloat16)
    grad_in_part = lax.dot_general(
        flat_in, grad_pre, (((1,), (1,)), ((), ())), preferred_element_type=jnp.float32
    )
    grad_out_part = lax.dot_general(
        activation, flat_cot, (((1,), (1,)), ((), ())), preferred_element_type=jnp.float32
    )
    grad_flat = jnp.dot(w_in, grad_pre, preferred_element_type=jnp.float32).astype(jnp.bfloat16)
    grad_filtered = grad_flat.reshape(channels, rows, columns)
    spread = lax.all_to_all(grad_filtered, "lon", split_axis=0, concat_axis=2, tiled=True)
    local_channels = spread.shape[0]
    coeffs = (
        jnp.dot(
            spread.reshape(local_channels * rows, NLON),
            forward_table(),
            preferred_element_type=jnp.float32,
        )
        .astype(jnp.bfloat16)
        .reshape(local_channels, rows, 2, M)
    )
    theta_rows = ((first_row + jnp.arange(rows, dtype=jnp.int32)).astype(jnp.float32) + 0.5) * (
        math.pi / NLAT
    )
    legendre = legendre_rows(theta_rows).astype(jnp.bfloat16)
    owned_count = L // lat_count
    weights = lax.slice_in_dim(legendre, 0, owned_count * lax.axis_size("lat"), axis=0)
    owned = lax.psum_scatter(
        jnp.einsum("ljm,cjrm->lcrm", weights, coeffs, preferred_element_type=jnp.float32),
        "lat",
        scatter_dimension=0,
        tiled=True,
    )
    real_part = owned[:, :, 0]
    imag_part = owned[:, :, 1]
    grad_gain = jnp.stack(
        [
            real_part * spectral_saved[:, :, 0] + imag_part * spectral_saved[:, :, 1],
            imag_part * spectral_saved[:, :, 0] - real_part * spectral_saved[:, :, 1],
        ],
        axis=2,
    )
    scaled = jnp.stack(
        [
            spectral_gain[:, :, 0] * real_part + spectral_gain[:, :, 1] * imag_part,
            spectral_gain[:, :, 0] * imag_part - spectral_gain[:, :, 1] * real_part,
        ],
        axis=2,
    ).astype(jnp.bfloat16)
    piece = lax.all_gather(scaled, "lat", axis=0, tiled=True)
    weights = lax.slice_in_dim(legendre, 0, piece.shape[0], axis=0)
    synthesis = (
        jnp.zeros((local_channels, rows, 2, M), jnp.float32)
        + jnp.einsum("ljm,lcrm->cjrm", weights, piece, preferred_element_type=jnp.float32)
    ).astype(jnp.bfloat16)
    grid_rows = jnp.dot(
        synthesis.reshape(local_channels * rows, 2 * M),
        inverse_table(),
        preferred_element_type=jnp.float32,
    ).reshape(local_channels, rows, NLON)
    spectral_grad = lax.all_to_all(grid_rows, "lon", split_axis=2, concat_axis=0, tiled=True)
    kernel = disco_kernel(quad_weights, lat_offsets, lon_offsets, weight_index)
    kernel_pad = jnp.pad(kernel, ((REACH, REACH), (0, 0), (0, 0)))
    kernel_rim = lax.dynamic_slice_in_dim(kernel_pad, first_row, rows + 2 * REACH, 0)
    stacked_rims = padded_2(
        jnp.stack((block_input, grad_filtered)), (("lat", 2), ("lon", 3)), REACH
    )
    input_pad = inside_rows(stacked_rims[0], first_row)
    grad_source = inside_rows(stacked_rims[1], first_row)
    grad_pad = lax.dot_general(
        w_disco, grad_source, (((1,), (0,)), ((), ())), preferred_element_type=jnp.float32
    ).astype(jnp.bfloat16)
    mixed = disco_apply(input_pad, kernel_rim[REACH : REACH + rows]).astype(jnp.bfloat16)
    grad_disco_part = lax.dot_general(
        mixed.reshape(channels, cells),
        grad_flat,
        (((1,), (1,)), ((), ())),
        preferred_element_type=jnp.float32,
    )
    disco_grad = disco_adjoint(grad_pad, kernel_rim)
    grad_input = (spectral_grad + disco_grad).astype(jnp.bfloat16)
    total_in, total_out, total_disco = lax.psum(
        (grad_in_part, grad_out_part, grad_disco_part), ("lat", "lon")
    )
    scale = 1.0 / math.sqrt(NLAT * NLON)
    return (grad_input, grad_gain, total_in * scale, total_out * scale, total_disco * scale)


BAND = 16
LANES = 128
MIB = 1024 * 1024


def mm(a, b):
    return jnp.dot(a, b, preferred_element_type=jnp.float32)


def mm_nt(a, b):
    return lax.dot_general(a, b, (((1,), (1,)), ((), ())), preferred_element_type=jnp.float32)


def mm_tn(a, b):
    return lax.dot_general(a, b, (((0,), (0,)), ((), ())), preferred_element_type=jnp.float32)


def params(mib):
    return pltpu.CompilerParams(vmem_limit_bytes=mib * MIB)


def whole_block(shape):
    return pl.BlockSpec(shape, lambda *_: (0,) * len(shape))


def rows_first(block, stage, flat, width):
    channels = block.shape[0]
    for tile in range(width // LANES):
        stage[tile] = (
            block[:, :, tile * LANES : (tile + 1) * LANES]
            .astype(jnp.float32)
            .reshape(channels * BAND, LANES)
        )
    for row in range(BAND):
        for tile in range(width // LANES):
            start = row * width + tile * LANES
            flat[:, start : start + LANES] = stage[
                tile, pl.ds(row, channels, stride=BAND), :
            ].astype(jnp.bfloat16)


def gelu_both(value):
    decay = jnp.exp(value * value * -0.5)
    base = 1.0 + (0.3275911 * root_half) * jnp.abs(value)
    inverse = pl.reciprocal(base, approx=True)
    inverse = inverse * (2.0 - base * inverse)
    poly = 0.5 * 1.061405429
    for term in (-1.453152027, 1.421413741, -0.284496736, 0.254829592):
        poly = poly * inverse + 0.5 * term
    tail = poly * inverse * decay
    chance = jnp.where(value >= 0.0, 1.0 - tail, tail)
    return chance, decay


def mlp_kernel(
    side, x_ref, ct_ref, win_t, win, wout, table,
    gf_ref, own_ref, send_ref, edge_ref, halo_ref, gin_ref, gout_ref,
    stage, xs, cs, low, high,
    *, steps, width, chunk, halo,
):
    step = pl.program_id(0)

    @pl.when(step == 0)
    def _():
        gin_ref[...] = jnp.zeros_like(gin_ref)
        gout_ref[...] = jnp.zeros_like(gout_ref)

    rows_first(x_ref, stage, xs, width)
    rows_first(ct_ref, stage, cs, width)
    column = pl.multiple_of(step * width, width)
    per = chunk // width

    def body(index, carry):
        cells = pl.ds(pl.multiple_of(index * chunk, chunk), chunk)
        x = xs[:, cells]
        c = cs[:, cells]
        pre = mm(win_t[...], x)
        grad = mm(wout[...], c)
        chance, decay = gelu_both(pre)
        act = (pre * chance).astype(jnp.bfloat16)
        gp = (grad * (chance + pre * decay * (1.0 / root_two_pi))).astype(jnp.bfloat16)
        gf = mm(win[...], gp).astype(jnp.bfloat16)
        for part in range(per):
            gf_ref[index * per + part, :, pl.ds(column, width)] = gf[
                :, part * width : (part + 1) * width
            ]
        gin_ref[...] += mm_nt(x, gp)
        gout_ref[...] += mm_nt(act, c)
        return carry

    lax.fori_loop(0, BAND * width // chunk, body, 0, unroll=2)

    @pl.when(step == steps - 1)
    def _():
        halo_ref[...] = gf_ref[halo : halo + REACH]
        orders = low.shape[0] // BAND

        def transform(row, carry):
            out = mm_nt(table[...], gf_ref[row])
            low[pl.ds(row, orders, stride=BAND), :] = out[:orders, :LANES]
            high[pl.ds(row, orders, stride=BAND), :] = out[:orders, LANES:]
            edge_ref[row] = out[orders:].astype(jnp.bfloat16)
            return carry

        lax.fori_loop(0, BAND, transform, 0, unroll=2)
        first = side[0] == 0
        shape = own_ref.shape

        @pl.when(first)
        def _():
            own_ref[...] = low[...].astype(jnp.bfloat16).reshape(shape)
            send_ref[...] = high[...].astype(jnp.bfloat16).reshape(shape)

        @pl.when(jnp.logical_not(first))
        def _():
            own_ref[...] = high[...].astype(jnp.bfloat16).reshape(shape)
            send_ref[...] = low[...].astype(jnp.bfloat16).reshape(shape)


def mlp_call(band, side, filtered, cotangent, win_t, win, wout, table):
    channels, rows, columns = filtered.shape
    hidden = wout.shape[0]
    width = LANES
    steps = columns // width
    chunk = 4 * width
    orders = table.shape[0] - 16
    block = pl.BlockSpec((channels, BAND, width), lambda i: (0, band, i))
    cells = BAND * columns
    return pl.pallas_call(
        functools.partial(
            mlp_kernel, steps=steps, width=width, chunk=chunk, halo=band * (BAND - REACH)
        ),
        grid=(steps,),
        in_specs=[
            pl.BlockSpec(memory_space=pltpu.SMEM),
            block,
            block,
            whole_block(win_t.shape),
            whole_block(win.shape),
            whole_block(wout.shape),
            whole_block(table.shape),
        ],
        out_specs=[
            whole_block((BAND, channels, columns)),
            whole_block((orders, BAND, LANES)),
            whole_block((orders, BAND, LANES)),
            whole_block((BAND, 16, channels)),
            whole_block((REACH, channels, columns)),
            whole_block((channels, hidden)),
            whole_block((hidden, channels)),
        ],
        out_shape=[
            jax.ShapeDtypeStruct((BAND, channels, columns), jnp.bfloat16),
            jax.ShapeDtypeStruct((orders, BAND, LANES), jnp.bfloat16),
            jax.ShapeDtypeStruct((orders, BAND, LANES), jnp.bfloat16),
            jax.ShapeDtypeStruct((BAND, 16, channels), jnp.bfloat16),
            jax.ShapeDtypeStruct((REACH, channels, columns), jnp.bfloat16),
            jax.ShapeDtypeStruct((channels, hidden), jnp.float32),
            jax.ShapeDtypeStruct((hidden, channels), jnp.float32),
        ],
        scratch_shapes=[
            pltpu.VMEM((width // LANES, channels * BAND, LANES), jnp.float32),
            pltpu.VMEM((channels, BAND * width), jnp.bfloat16),
            pltpu.VMEM((channels, BAND * width), jnp.bfloat16),
            pltpu.VMEM((orders * BAND, LANES), jnp.float32),
            pltpu.VMEM((orders * BAND, LANES), jnp.float32),
        ],
        compiler_params=params(56),
        cost_estimate=pl.CostEstimate(
            flops=2 * cells * channels * (5 * hidden + orders),
            bytes_accessed=6 * channels * cells,
            transcendentals=2 * hidden * cells,
        ),
        name="mlp",
    )(side, filtered, cotangent, win_t, win, wout, table)


def stencil_kernel(taps, before, rows, after, edges, place, q_ref, field, rim, *, first):
    channels, columns = field.shape[1:]
    field[0:REACH] = before[...]
    field[REACH : REACH + BAND] = rows[...]
    field[REACH + BAND :] = after[...]

    def spread(row, carry):
        rim[row] = mm_tn(edges[row], place[...]).astype(jnp.bfloat16)
        return carry

    lax.fori_loop(0, BAND + 2 * REACH, spread, 0, unroll=5)
    lane = lax.broadcasted_iota(jnp.int32, (16, LANES), 1)
    span = 2 * REACH + 1

    def row_body(row, carry):
        weights = {}
        for north in range(span):
            source = row + 2 * REACH - north
            for east in range(span):
                weights[north, east] = taps[((first + source) * span + north) * span + east].astype(
                    jnp.bfloat16
                )

        def tile_body(tile, inner):
            part = pl.ds(pl.multiple_of(tile * 16, 16), 16)
            sums = [None] * span
            for north in range(span):
                source = row + 2 * REACH - north
                here = field[source, part, :]
                ends = rim[source, part, :]
                for east in range(span):
                    past = east - REACH
                    shifted = here
                    if past < 0:
                        rim_tile = jnp.where(lane < -past, ends, here[:, :LANES])
                        shifted = jnp.concatenate([rim_tile, here[:, LANES:]], axis=1)
                    if past > 0:
                        rim_tile = jnp.where(lane >= LANES - past, ends, here[:, -LANES:])
                        shifted = jnp.concatenate([here[:, :-LANES], rim_tile], axis=1)
                    term = shifted * weights[north, east]
                    sums[east] = term if sums[east] is None else sums[east] + term
            total = sums[REACH].astype(jnp.float32)
            for east in range(span):
                if east != REACH:
                    moved = pltpu.roll(sums[east], (east - REACH) % columns, 1)
                    total = total + moved.astype(jnp.float32)
            q_ref[row, part, :] = total.astype(jnp.bfloat16)
            return inner

        return lax.fori_loop(0, channels // 16, tile_body, carry, unroll=4)

    lax.fori_loop(0, BAND, row_body, 0)


def stencil_call(band, taps, before, rows, after, edges, place):
    _, channels, columns = rows.shape

    def pair(index):
        return pl.BlockSpec((REACH, channels, columns), lambda i: (index, 0, 0))

    return pl.pallas_call(
        functools.partial(stencil_kernel, first=band * BAND),
        grid=(1,),
        in_specs=[
            pl.BlockSpec(memory_space=pltpu.SMEM),
            pair(before[1]),
            whole_block(rows.shape),
            pair(after[1]),
            whole_block(edges.shape),
            whole_block(place.shape),
        ],
        out_specs=whole_block(rows.shape),
        out_shape=jax.ShapeDtypeStruct(rows.shape, jnp.bfloat16),
        scratch_shapes=[
            pltpu.VMEM((BAND + 2 * REACH, channels, columns), jnp.bfloat16),
            pltpu.VMEM((BAND + 2 * REACH, channels, LANES), jnp.bfloat16),
        ],
        compiler_params=params(48),
        cost_estimate=pl.CostEstimate(
            flops=60 * channels * BAND * columns,
            bytes_accessed=4 * channels * BAND * columns,
            transcendentals=0,
        ),
        name="stencil",
    )(taps, before[0], rows, after[0], edges, place)


def disco_kernel_grad(bi_ref, q_ref, gd_ref, stage, flat):
    columns = q_ref.shape[2]
    gd_ref[...] = jnp.zeros_like(gd_ref)
    rows_first(bi_ref, stage, flat, columns)

    def body(row, carry):
        cells = pl.ds(pl.multiple_of(row * columns, columns), columns)
        gd_ref[...] += mm_nt(flat[:, cells], q_ref[row])
        return carry

    lax.fori_loop(0, BAND, body, 0, unroll=4)


def disco_grad_call(band, block_input, q):
    channels, _, columns = block_input.shape
    return pl.pallas_call(
        disco_kernel_grad,
        grid=(1,),
        in_specs=[
            pl.BlockSpec((channels, BAND, columns), lambda i: (0, band, 0)),
            whole_block(q.shape),
        ],
        out_specs=whole_block((channels, channels)),
        out_shape=jax.ShapeDtypeStruct((channels, channels), jnp.float32),
        scratch_shapes=[
            pltpu.VMEM((columns // LANES, channels * BAND, LANES), jnp.float32),
            pltpu.VMEM((channels, BAND * columns), jnp.bfloat16),
        ],
        compiler_params=params(48),
        cost_estimate=pl.CostEstimate(
            flops=2 * channels * channels * BAND * columns,
            bytes_accessed=4 * channels * BAND * columns,
            transcendentals=0,
        ),
        name="disco_weight",
    )(block_input, q)


def legendre_kernel(leg, r0, r1, gain, owned_ref, s0, s1, stage, *, steps, block):
    order = pl.program_id(0)
    degrees = leg.shape[1]
    half = leg.shape[2] // 2
    total = None
    for band, ref in enumerate((r0, r1)):
        pair = jnp.concatenate(
            [ref[:, r].reshape(half, LANES) for r in range(2)], axis=1
        )
        term = mm(leg[0, :, band * half : (band + 1) * half], pair)
        total = term if total is None else total + term
    real = total[:, :LANES]
    imag = total[:, LANES:]
    owned_ref[:, 0, 0] = real.reshape(owned_ref.shape[0], -1, LANES)
    owned_ref[:, 0, 1] = imag.reshape(owned_ref.shape[0], -1, LANES)
    g = gain[:, 0, 0].reshape(degrees, LANES)
    k = gain[:, 0, 1].reshape(degrees, LANES)
    scaled = jnp.concatenate([g * real + k * imag, g * imag - k * real], axis=1).astype(
        jnp.bfloat16
    )
    synth = mm_tn(leg[0], scaled)
    for r in range(2):
        stage[pl.ds(r * steps + order, 2 * half, stride=block), :] = synth[
            :, r * LANES : (r + 1) * LANES
        ]

    @pl.when(order == steps - 1)
    def _():
        s0[...] = stage[: half * block].astype(jnp.bfloat16).reshape(s0.shape)
        s1[...] = stage[half * block :].astype(jnp.bfloat16).reshape(s1.shape)


def legendre_call(leg, r0, r1, gain):
    owners, _, steps, band, lanes = r0.shape
    degrees = leg.shape[1]
    block = 2 * steps
    r_spec = pl.BlockSpec((owners, 2, None, band, lanes), lambda m: (0, 0, m, 0, 0))
    g_shape = (owners, 1, 2, degrees // owners, lanes)
    g_spec = pl.BlockSpec(g_shape, lambda m: (0, m, 0, 0, 0))
    out = (owners, band, block, lanes)
    return pl.pallas_call(
        functools.partial(legendre_kernel, steps=steps, block=block),
        grid=(steps,),
        in_specs=[
            pl.BlockSpec((1, degrees, leg.shape[2]), lambda m: (m, 0, 0)),
            r_spec,
            r_spec,
            g_spec,
        ],
        out_specs=[g_spec, whole_block(out), whole_block(out)],
        out_shape=[
            jax.ShapeDtypeStruct(gain.shape, jnp.float32),
            jax.ShapeDtypeStruct(out, jnp.bfloat16),
            jax.ShapeDtypeStruct(out, jnp.bfloat16),
        ],
        scratch_shapes=[pltpu.VMEM((2 * owners * band * block, lanes), jnp.float32)],
        compiler_params=params(48),
        cost_estimate=pl.CostEstimate(
            flops=8 * steps * degrees * leg.shape[2] * 256,
            bytes_accessed=7 * MIB,
            transcendentals=0,
        ),
        name="legendre",
    )(leg, r0, r1, gain)


def final_kernel(side, q_ref, own, other, table, wd, *rest):
    out_ref, stage = rest[-2:]
    width = q_ref.shape[2]
    orders = table.shape[0]
    channels = out_ref.shape[0]
    first = side[0] == 0

    def body(row, carry):
        mine = own[:, row].reshape(orders, LANES)
        theirs = other[:, row].reshape(orders, LANES)
        synth = jnp.concatenate(
            [jnp.where(first, mine, theirs), jnp.where(first, theirs, mine)], axis=1
        )
        out = mm_tn(synth, table[...]) + mm(wd[...], q_ref[row])
        for tile in range(width // LANES):
            stage[tile, pl.ds(row, channels, stride=BAND), :] = out[
                :, tile * LANES : (tile + 1) * LANES
            ]
        return carry

    lax.fori_loop(0, BAND, body, 0, unroll=2)
    for tile in range(width // LANES):
        out_ref[:, :, tile * LANES : (tile + 1) * LANES] = (
            stage[tile].astype(jnp.bfloat16).reshape(channels, BAND, LANES)
        )


def final_call(band, rows, side, q, own, other, table, wd, previous):
    _, channels, columns = q.shape
    width = 2 * LANES
    cells = BAND * columns
    extra = [] if previous is None else [previous]
    return pl.pallas_call(
        final_kernel,
        grid=(columns // width,),
        in_specs=[
            pl.BlockSpec(memory_space=pltpu.SMEM),
            pl.BlockSpec((BAND, channels, width), lambda i: (0, 0, i)),
            whole_block(own.shape),
            whole_block(other.shape),
            pl.BlockSpec((table.shape[0], width), lambda i: (0, i)),
            whole_block(wd.shape),
        ]
        + [pl.BlockSpec(memory_space=pl.ANY)] * len(extra),
        out_specs=pl.BlockSpec((channels, BAND, width), lambda i: (0, band, i)),
        out_shape=jax.ShapeDtypeStruct((channels, rows, columns), jnp.bfloat16),
        scratch_shapes=[pltpu.VMEM((width // LANES, channels * BAND, LANES), jnp.float32)],
        input_output_aliases={6: 0} if extra else {},
        compiler_params=params(48),
        cost_estimate=pl.CostEstimate(
            flops=2 * cells * channels * (channels + table.shape[0]),
            bytes_accessed=5 * channels * cells,
            transcendentals=0,
        ),
        name="final",
    )(side, q, own, other, table, wd, *extra)


def gain_kernel(gain, out, *, degrees):
    for degree in range(degrees):
        for r in range(2):
            part = gain[pl.ds(degree * 2 * LANES + r, LANES, stride=2), :]
            out[pl.ds(r * degrees + degree, LANES, stride=2 * degrees), :] = part.T


def gain_call(gain):
    degrees, channels, _, orders = gain.shape
    flat = gain.reshape(degrees * channels * 2, orders)
    return pl.pallas_call(
        functools.partial(gain_kernel, degrees=degrees),
        out_shape=jax.ShapeDtypeStruct((orders * 2 * degrees, channels), jnp.float32),
        name="gain",
    )(flat)


def grad_gain_kernel(owned, saved, out, *, degrees):
    for degree in range(degrees):
        real = owned[pl.ds(degree, LANES, stride=2 * degrees), :].T
        imag = owned[pl.ds(degrees + degree, LANES, stride=2 * degrees), :].T
        start = degree * 2 * LANES
        s = saved[pl.ds(start, LANES, stride=2), :]
        t = saved[pl.ds(start + 1, LANES, stride=2), :]
        out[pl.ds(start, LANES, stride=2), :] = real * s + imag * t
        out[pl.ds(start + 1, LANES, stride=2), :] = imag * s - real * t


def grad_gain_call(owned, saved):
    degrees, channels, _, orders = saved.shape
    flat = saved.reshape(degrees * channels * 2, orders)
    out = pl.pallas_call(
        functools.partial(grad_gain_kernel, degrees=degrees),
        out_shape=jax.ShapeDtypeStruct(flat.shape, jnp.float32),
        name="grad_gain",
    )(owned, flat)
    return out.reshape(saved.shape)


def legendre_whole():
    upper, lower, diagonal_log = legendre_tables()
    theta = (np.arange(NLAT) + 0.5) * (math.pi / NLAT)
    sine, cosine = np.sin(theta)[None], np.cos(theta)[None]
    orders = np.arange(M)
    start = np.exp(diagonal_log[:, None] + orders[:, None] * np.log(sine))
    table = np.zeros((M, L, NLAT))
    previous = before = np.zeros((M, NLAT))
    for degree in range(L):
        fresh = np.where(
            (orders == degree)[:, None],
            start,
            upper[degree][:, None] * (cosine * previous - lower[degree][:, None] * before),
        )
        table[:, degree] = fresh
        previous, before = fresh, previous
    return table * np.sqrt(sine * (math.pi / NLAT))[None]


def host_tables(lat_count, lon_count):
    columns, rows, own = NLON // lon_count, NLAT // lat_count, M // lat_count
    angle = (np.arange(M)[:, None] * np.arange(NLON)[None, :] % NLON) * (2.0 * math.pi / NLON)
    waves = np.stack([np.cos(angle), -np.sin(angle)]) / math.sqrt(NLON)
    factor = np.where(np.arange(M) == 0, 1.0, 2.0)[None, :, None]

    def arrange(table):
        table = table.reshape(2, lat_count, own, lon_count, columns)
        return table.transpose(3, 1, 0, 2, 4).reshape(lon_count, 2 * M, columns)

    pick = np.zeros((lon_count, 16, columns))
    for row, column in enumerate((0, 1, columns - 2, columns - 1)):
        pick[:, row, column] = 1.0
    forward = np.concatenate([arrange(waves * factor), pick], axis=1)
    legendre = legendre_whole().reshape(M, L, lat_count, rows // BAND, BAND)
    legendre = legendre.transpose(0, 1, 3, 2, 4).reshape(M, L, NLAT)
    kind = jnp.bfloat16
    return forward.astype(kind), arrange(waves).astype(kind), legendre.astype(kind)


def shards_banded(
    cotangent,
    block_input,
    filtered,
    spectral_saved,
    spectral_gain,
    w_in,
    w_out,
    w_disco,
    quad_weights,
    lat_offsets,
    lon_offsets,
    weight_index,
):
    channels, rows, columns = cotangent.shape
    lat_count = lax.axis_size("lat")
    lon_count = lax.axis_size("lon")
    lat_index = lax.axis_index("lat")
    lon_index = lax.axis_index("lon")
    own = M // lat_count
    degrees = L // lat_count
    side = lon_index.reshape(1).astype(jnp.int32)
    forward, inverse, legendre = host_tables(lat_count, lon_count)
    forward = lax.dynamic_index_in_dim(jnp.asarray(forward), lon_index, 0, keepdims=False)
    inverse = lax.dynamic_index_in_dim(jnp.asarray(inverse), lon_index, 0, keepdims=False)
    legendre = lax.dynamic_slice_in_dim(jnp.asarray(legendre), lat_index * own, own, 0)
    swap = [(i, (i + 1) % lon_count) for i in range(lon_count)]
    exchange = functools.partial(lax.all_to_all, axis_name="lat", split_axis=0, concat_axis=0, tiled=True)

    kernel = disco_kernel(quad_weights, lat_offsets, lon_offsets, weight_index)
    kernel_pad = jnp.pad(kernel, ((REACH, REACH), (0, 0), (0, 0)))
    kernel_rim = lax.dynamic_slice_in_dim(kernel_pad, lat_index * rows, rows + 2 * REACH, 0)
    taps = kernel_rim.reshape(-1)
    place = np.zeros((16, LANES), np.float32)
    for row, lane in enumerate((0, 1, LANES - 2, LANES - 1)):
        place[row, lane] = 1.0
    place = jnp.asarray(place, jnp.bfloat16)
    w_in_t = w_in.T

    down = [(i, (i + 1) % lat_count) for i in range(lat_count)]
    up = [(target, source) for source, target in down]

    def across(moves):
        return [
            (a * lon_count + i, b * lon_count + j) for a, b in moves for i, j in swap
        ]

    def summed(kept, arrived):
        total = (kept.astype(jnp.float32) + arrived.astype(jnp.float32)).astype(jnp.bfloat16)
        return total.reshape(lat_count, 2, own, BAND, LANES)

    gain = gain_call(spectral_gain).reshape(lat_count, own, 2, degrees, LANES)
    gain = exchange(gain)
    gf0, kept0, sent0, ends0, head, gin0, gout0 = mlp_call(
        0, side, filtered, cotangent, w_in_t, w_in, w_out, forward
    )
    arrived0 = lax.ppermute(sent0, "lon", swap)
    bottom = lax.ppermute(head, "lat", up)
    sides0 = lax.ppermute(ends0, "lon", swap)
    bottom_side = lax.ppermute(ends0[:REACH], ("lat", "lon"), across(up))
    gain, w_in_t = lax.optimization_barrier((gain, w_in_t))
    gf1, kept1, sent1, ends1, tail, gin1, gout1 = mlp_call(
        1, side, filtered, cotangent, w_in_t, w_in, w_out, forward
    )
    sides1 = lax.ppermute(ends1, "lon", swap)
    top = lax.ppermute(tail, "lat", down)
    top_side = lax.ppermute(ends1[BAND - REACH :], ("lat", "lon"), across(down))
    sent1, sides1 = lax.optimization_barrier((sent1, sides1))
    arrived1 = lax.ppermute(sent1, "lon", swap)
    edges1 = jnp.concatenate([sides0[BAND - REACH :], sides1, bottom_side], axis=0)
    sum0, edges1 = lax.optimization_barrier((summed(kept0, arrived0), edges1))
    received0 = exchange(sum0)
    q1 = stencil_call(1, taps, (gf0, BAND // REACH - 1), gf1, (bottom, 0), edges1, place)
    arrived1, q1 = lax.optimization_barrier((arrived1, q1))
    received1 = exchange(summed(kept1, arrived1))
    edges0 = jnp.concatenate([top_side, sides0, sides1[:REACH]], axis=0)
    q0 = stencil_call(0, taps, (top, 0), gf0, (gf1, 0), edges0, place)
    received0, received1, q0 = lax.optimization_barrier((received0, received1, q0))
    owned, s0, s1 = legendre_call(legendre, received0, received1, gain)
    local0 = exchange(s0)
    q1, owned = lax.optimization_barrier((q1, owned))
    disco1 = disco_grad_call(1, block_input, q1)
    local0, disco1, s1, q0 = lax.optimization_barrier((local0, disco1, s1, q0))
    local1 = exchange(s1)
    disco0 = disco_grad_call(0, block_input, q0)
    other0 = lax.ppermute(local0, "lon", swap)
    everyone = functools.partial(
        lax.all_to_all, axis_name=("lat", "lon"), split_axis=0, concat_axis=0, tiled=True
    )
    count = lat_count * lon_count
    half = w_in.shape[1] // 2
    gin = gin0 + gin1
    parts = (gin[:, :half], gin[:, half:], gout0 + gout1, disco0 + disco1)
    stacked = jnp.concatenate(parts, axis=0).astype(jnp.bfloat16)
    stacked, local1 = lax.optimization_barrier((stacked, local1))
    shares = everyone(stacked.reshape(count, -1, channels)).astype(jnp.float32).sum(axis=0)
    shares = jnp.broadcast_to(shares.astype(jnp.bfloat16)[None], (count,) + shares.shape)
    shares, owned = lax.optimization_barrier((shares, owned))
    totals = everyone(shares).reshape(-1, channels).astype(jnp.float32)
    total_in = jnp.concatenate([totals[:channels], totals[channels : 2 * channels]], axis=1)
    total_out, total_disco = jnp.split(totals[2 * channels :], (2 * half,), axis=0)
    other1 = lax.ppermute(local1, "lon", swap)
    owned = exchange(owned).reshape(M * 2 * degrees, LANES)
    result = final_call(0, rows, side, q0, local0, other0, inverse, w_disco, None)
    result = final_call(1, rows, side, q1, local1, other1, inverse, w_disco, result)
    grad_gain = grad_gain_call(owned, spectral_saved)
    scale = 1.0 / math.sqrt(NLAT * NLON)
    return (result, grad_gain, total_in * scale, total_out * scale, total_disco * scale)


def shards(*arrays):
    channels, rows, columns = arrays[0].shape
    lat_count = lax.axis_size("lat")
    lon_count = lax.axis_size("lon")
    fits = (
        rows == 2 * BAND
        and lon_count == 2
        and channels == lon_count * LANES
        and columns % (2 * LANES) == 0
        and M == LANES
        and M // lat_count == 8
        and L // lat_count == 8
    )
    return shards_banded(*arrays) if fits else shards_general(*arrays)


def solution(mesh):
    placed = (
        P(None, "lat", "lon"),
        P(None, "lat", "lon"),
        P(None, "lat", "lon"),
        P("lat", "lon", None, None),
        P("lat", "lon", None, None),
        P(),
        P(),
        P(),
        P(),
        P(),
        P(),
        P(),
    )
    return jax.shard_map(
        shards,
        mesh=mesh,
        in_specs=placed,
        out_specs=(P(None, "lat", "lon"), P("lat", "lon", None, None), P(), P(), P()),
        check_vma=False,
    )
```

```python
import functools
import math

import jax
import jax.numpy as jnp
import numpy as np
from jax import lax
from jax.experimental import pallas as pl
from jax.experimental.pallas import tpu as pltpu
from jax.sharding import PartitionSpec as P

NLAT = 512
NLON = 1024
L = 128
M = 128
REACH = 2
NQ = 64


root_half = 0.7071067811865476
root_two_pi = 2.5066282746310002


def padded_2(block, sides, width):
    for axis, dim in sides:
        count = lax.axis_size(axis)
        forward = [(i, i + 1) for i in range(count - 1)]
        forward.append((count - 1, 0))
        backward = [(target, source) for source, target in forward]
        low = lax.ppermute(
            lax.slice_in_dim(block, block.shape[dim] - width, None, axis=dim), axis, forward
        )
        high = lax.ppermute(lax.slice_in_dim(block, 0, width, axis=dim), axis, backward)
        block = jnp.concatenate([low, block, high], axis=dim)
    return block


def gelu_value(value):
    return value * 0.5 * (1.0 + lax.erf(value * root_half))


def gelu_slope(value):
    return (
        0.5 * (1.0 + lax.erf(value * root_half))
        + value * jnp.exp(-0.5 * value * value) / root_two_pi
    )


def legendre_tables():
    degree = np.arange(L)[:, None] * 1.0
    order = np.arange(M)[None, :] * 1.0
    upper = np.where(
        degree > order,
        np.sqrt(
            np.maximum(4.0 * degree * degree - 1.0, 0.0)
            / np.maximum(degree * degree - order * order, 1.0)
        ),
        0.0,
    )
    lower = np.where(
        degree > order + 1.0,
        np.sqrt(
            np.maximum((degree - 1.0) ** 2 - order * order, 0.0)
            / np.maximum(4.0 * (degree - 1.0) ** 2 - 1.0, 1.0)
        ),
        0.0,
    )
    counter = np.arange(1, M) * 1.0
    diagonal_log = np.concatenate(
        [np.zeros(1), np.cumsum(0.5 * np.log((2.0 * counter + 1.0) / (2.0 * counter)))]
    ) - 0.5 * np.log(2.0)
    return (upper, lower, diagonal_log)


def legendre_rows(theta):
    upper, lower, diagonal_log = legendre_tables()
    float_type = theta.dtype
    cosine = jnp.cos(theta)[:, None]
    sine = jnp.sin(theta)
    orders = jnp.arange(M, dtype=jnp.int32)
    start_value = jnp.exp(
        jnp.asarray(diagonal_log, float_type)[None, :]
        + orders.astype(float_type)[None, :] * jnp.log(sine)[:, None]
    )

    def advance(carry, inputs):
        previous, before = carry
        degree, coef_up, coef_low = inputs
        fresh = jnp.where(
            (orders == degree)[None, :],
            start_value,
            coef_up[None, :] * (cosine * previous - coef_low[None, :] * before),
        )
        return ((fresh, previous), fresh)

    empty = jnp.zeros_like(start_value)
    final, table = lax.scan(
        advance,
        (empty, empty),
        (
            jnp.arange(L, dtype=jnp.int32),
            jnp.asarray(upper, float_type),
            jnp.asarray(lower, float_type),
        ),
    )
    weight = jnp.sqrt(sine * (math.pi / NLAT))
    return table * weight[None, :, None]


def forward_table():
    column = jnp.arange(NLON, dtype=jnp.int32)[:, None]
    order = jnp.arange(M, dtype=jnp.int32)[None, :]
    angle = (column * order % NLON).astype(jnp.float32) * (2.0 * math.pi / NLON)
    factor = jnp.where(order == 0, 1.0, 2.0).astype(jnp.float32) / math.sqrt(NLON)
    return jnp.concatenate([factor * jnp.cos(angle), -factor * jnp.sin(angle)], axis=1).astype(
        jnp.bfloat16
    )


def inverse_table():
    order = jnp.arange(M, dtype=jnp.int32)[:, None]
    column = jnp.arange(NLON, dtype=jnp.int32)[None, :]
    angle = (column * order % NLON).astype(jnp.float32) * (2.0 * math.pi / NLON)
    return (jnp.concatenate([jnp.cos(angle), -jnp.sin(angle)], axis=0) / math.sqrt(NLON)).astype(
        jnp.bfloat16
    )


def disco_kernel(quad_weights, lat_offsets, lon_offsets, weight_index):
    span = jnp.arange(-REACH, REACH + 1, dtype=jnp.int32)
    slots = jnp.arange(NQ, dtype=jnp.int32)
    values = jnp.sum(
        jnp.where(
            weight_index[:, :, None] == slots[None, None, :], quad_weights[None, None, :], 0.0
        ),
        axis=2,
    )
    north = (lat_offsets[:, :, None] == span[None, None, :]).astype(quad_weights.dtype)
    east = (lon_offsets[:, :, None] == span[None, None, :]).astype(quad_weights.dtype)
    return jnp.sum(values[:, :, None, None] * north[:, :, :, None] * east[:, :, None, :], axis=1)


def disco_apply(padded, kernel):
    height = kernel.shape[0]
    width = padded.shape[2] - 2 * REACH
    total = jnp.zeros((padded.shape[0], height, width), kernel.dtype)
    for north in range(2 * REACH + 1):
        for east in range(2 * REACH + 1):
            total = (
                total
                + kernel[None, :, north, east, None]
                * padded[:, north : north + height, east : east + width]
            )
    return total


def disco_adjoint(padded, kernel_rim):
    height = kernel_rim.shape[0] - 2 * REACH
    width = padded.shape[2] - 2 * REACH
    total = jnp.zeros((padded.shape[0], height, width), kernel_rim.dtype)
    for north in range(2 * REACH + 1):
        for east in range(2 * REACH + 1):
            row_shift = 2 * REACH - north
            col_shift = 2 * REACH - east
            total = (
                total
                + kernel_rim[None, row_shift : row_shift + height, north, east, None]
                * padded[:, row_shift : row_shift + height, col_shift : col_shift + width]
            )
    return total


def inside_rows(padded, first_row):
    height = padded.shape[1]
    latitude = first_row - REACH + jnp.arange(height, dtype=jnp.int32)
    keep = (latitude >= 0) & (latitude < NLAT)
    return jnp.where(keep[None, :, None], padded, jnp.zeros((), padded.dtype))


def shards_general(
    cotangent,
    block_input,
    filtered,
    spectral_saved,
    spectral_gain,
    w_in,
    w_out,
    w_disco,
    quad_weights,
    lat_offsets,
    lon_offsets,
    weight_index,
):
    channels, rows, columns = cotangent.shape
    lat_count = lax.axis_size("lat")
    first_row = lax.axis_index("lat") * rows
    cells = rows * columns
    flat_in = filtered.reshape(channels, cells)
    flat_cot = cotangent.reshape(channels, cells)
    hidden_pre = lax.dot_general(
        w_in, flat_in, (((0,), (0,)), ((), ())), preferred_element_type=jnp.float32
    )
    activation = gelu_value(hidden_pre).astype(jnp.bfloat16)
    grad_act = jnp.dot(w_out, flat_cot, preferred_element_type=jnp.float32)
    grad_pre = (grad_act * gelu_slope(hidden_pre)).astype(jnp.bfloat16)
    grad_in_part = lax.dot_general(
        flat_in, grad_pre, (((1,), (1,)), ((), ())), preferred_element_type=jnp.float32
    )
    grad_out_part = lax.dot_general(
        activation, flat_cot, (((1,), (1,)), ((), ())), preferred_element_type=jnp.float32
    )
    grad_flat = jnp.dot(w_in, grad_pre, preferred_element_type=jnp.float32).astype(jnp.bfloat16)
    grad_filtered = grad_flat.reshape(channels, rows, columns)
    spread = lax.all_to_all(grad_filtered, "lon", split_axis=0, concat_axis=2, tiled=True)
    local_channels = spread.shape[0]
    coeffs = (
        jnp.dot(
            spread.reshape(local_channels * rows, NLON),
            forward_table(),
            preferred_element_type=jnp.float32,
        )
        .astype(jnp.bfloat16)
        .reshape(local_channels, rows, 2, M)
    )
    theta_rows = ((first_row + jnp.arange(rows, dtype=jnp.int32)).astype(jnp.float32) + 0.5) * (
        math.pi / NLAT
    )
    legendre = legendre_rows(theta_rows).astype(jnp.bfloat16)
    owned_count = L // lat_count
    weights = lax.slice_in_dim(legendre, 0, owned_count * lax.axis_size("lat"), axis=0)
    owned = lax.psum_scatter(
        jnp.einsum("ljm,cjrm->lcrm", weights, coeffs, preferred_element_type=jnp.float32),
        "lat",
        scatter_dimension=0,
        tiled=True,
    )
    real_part = owned[:, :, 0]
    imag_part = owned[:, :, 1]
    grad_gain = jnp.stack(
        [
            real_part * spectral_saved[:, :, 0] + imag_part * spectral_saved[:, :, 1],
            imag_part * spectral_saved[:, :, 0] - real_part * spectral_saved[:, :, 1],
        ],
        axis=2,
    )
    scaled = jnp.stack(
        [
            spectral_gain[:, :, 0] * real_part + spectral_gain[:, :, 1] * imag_part,
            spectral_gain[:, :, 0] * imag_part - spectral_gain[:, :, 1] * real_part,
        ],
        axis=2,
    ).astype(jnp.bfloat16)
    piece = lax.all_gather(scaled, "lat", axis=0, tiled=True)
    weights = lax.slice_in_dim(legendre, 0, piece.shape[0], axis=0)
    synthesis = (
        jnp.zeros((local_channels, rows, 2, M), jnp.float32)
        + jnp.einsum("ljm,lcrm->cjrm", weights, piece, preferred_element_type=jnp.float32)
    ).astype(jnp.bfloat16)
    grid_rows = jnp.dot(
        synthesis.reshape(local_channels * rows, 2 * M),
        inverse_table(),
        preferred_element_type=jnp.float32,
    ).reshape(local_channels, rows, NLON)
    spectral_grad = lax.all_to_all(grid_rows, "lon", split_axis=2, concat_axis=0, tiled=True)
    kernel = disco_kernel(quad_weights, lat_offsets, lon_offsets, weight_index)
    kernel_pad = jnp.pad(kernel, ((REACH, REACH), (0, 0), (0, 0)))
    kernel_rim = lax.dynamic_slice_in_dim(kernel_pad, first_row, rows + 2 * REACH, 0)
    stacked_rims = padded_2(
        jnp.stack((block_input, grad_filtered)), (("lat", 2), ("lon", 3)), REACH
    )
    input_pad = inside_rows(stacked_rims[0], first_row)
    grad_source = inside_rows(stacked_rims[1], first_row)
    grad_pad = lax.dot_general(
        w_disco, grad_source, (((1,), (0,)), ((), ())), preferred_element_type=jnp.float32
    ).astype(jnp.bfloat16)
    mixed = disco_apply(input_pad, kernel_rim[REACH : REACH + rows]).astype(jnp.bfloat16)
    grad_disco_part = lax.dot_general(
        mixed.reshape(channels, cells),
        grad_flat,
        (((1,), (1,)), ((), ())),
        preferred_element_type=jnp.float32,
    )
    disco_grad = disco_adjoint(grad_pad, kernel_rim)
    grad_input = (spectral_grad + disco_grad).astype(jnp.bfloat16)
    total_in, total_out, total_disco = lax.psum(
        (grad_in_part, grad_out_part, grad_disco_part), ("lat", "lon")
    )
    scale = 1.0 / math.sqrt(NLAT * NLON)
    return (grad_input, grad_gain, total_in * scale, total_out * scale, total_disco * scale)


BAND = 16
LANES = 128
MIB = 1024 * 1024


def mm(a, b):
    return jnp.dot(a, b, preferred_element_type=jnp.float32)


def mm_nt(a, b):
    return lax.dot_general(a, b, (((1,), (1,)), ((), ())), preferred_element_type=jnp.float32)


def mm_tn(a, b):
    return lax.dot_general(a, b, (((0,), (0,)), ((), ())), preferred_element_type=jnp.float32)


def params(mib):
    return pltpu.CompilerParams(vmem_limit_bytes=mib * MIB)


def whole_block(shape):
    return pl.BlockSpec(shape, lambda *_: (0,) * len(shape))


def rows_first(block, stage, flat, width):
    channels = block.shape[0]
    for tile in range(width // LANES):
        stage[tile] = (
            block[:, :, tile * LANES : (tile + 1) * LANES]
            .astype(jnp.float32)
            .reshape(channels * BAND, LANES)
        )
    for row in range(BAND):
        for tile in range(width // LANES):
            start = row * width + tile * LANES
            flat[:, start : start + LANES] = stage[
                tile, pl.ds(row, channels, stride=BAND), :
            ].astype(jnp.bfloat16)


def gelu_both(value):
    decay = jnp.exp(value * value * -0.5)
    base = 1.0 + (0.3275911 * root_half) * jnp.abs(value)
    inverse = pl.reciprocal(base, approx=True)
    inverse = inverse * (2.0 - base * inverse)
    poly = 0.5 * 1.061405429
    for term in (-1.453152027, 1.421413741, -0.284496736, 0.254829592):
        poly = poly * inverse + 0.5 * term
    tail = poly * inverse * decay
    chance = jnp.where(value >= 0.0, 1.0 - tail, tail)
    return chance, decay


def mlp_kernel(
    side, x_ref, ct_ref, win_t, win, wout, table, earlier,
    gf_ref, own_ref, send_ref, edge_ref, halo_ref, gin_ref, gout_ref,
    stage, xs, cs, low, high, *slots, steps, width, chunk, halo,
):
    step = pl.program_id(0)

    @pl.when(step == 0)
    def _():
        gin_ref[...] = jnp.zeros_like(gin_ref)
        gout_ref[...] = jnp.zeros_like(gout_ref)

    rows_first(x_ref, stage, xs, width)
    rows_first(ct_ref, stage, cs, width)
    column = pl.multiple_of(step * width, width)
    per = chunk // width

    even, odd = slots[:4], slots[4:]

    def cells(index):
        return pl.ds(pl.multiple_of(index * chunk, chunk), chunk)

    def project(index, slot):
        slot[0][...] = mm(win_t[...], xs[:, cells(index)])
        slot[1][...] = mm(wout[...], cs[:, cells(index)])

    def activate(slot):
        pre = slot[0][...]
        chance, decay = gelu_both(pre)
        slot[2][...] = (pre * chance).astype(jnp.bfloat16)
        slope = chance + pre * decay * (1.0 / root_two_pi)
        slot[3][...] = (slot[1][...] * slope).astype(jnp.bfloat16)

    def reduce(index, slot):
        gp = slot[3][...]
        gf = mm(win[...], gp).astype(jnp.bfloat16)
        for part in range(per):
            gf_ref[index * per + part, :, pl.ds(column, width)] = gf[
                :, part * width : (part + 1) * width
            ]
        gin_ref[...] += mm_nt(xs[:, cells(index)], gp)
        gout_ref[...] += mm_nt(slot[2][...], cs[:, cells(index)])

    chunks = BAND * width // chunk
    project(0, even)
    activate(even)
    project(1, odd)

    def body(pair, carry):
        index = 2 * pair
        reduce(index, even)
        activate(odd)
        project(index + 2, even)
        reduce(index + 1, odd)
        activate(even)
        project(index + 3, odd)
        return carry

    lax.fori_loop(0, chunks // 2 - 1, body, 0)
    reduce(chunks - 2, even)
    activate(odd)
    reduce(chunks - 1, odd)

    @pl.when(step == steps - 1)
    def _():
        halo_ref[...] = gf_ref[halo : halo + REACH]
        orders = low.shape[0] // BAND

        def transform(row, carry):
            out = mm_nt(table[...], gf_ref[row])
            low[pl.ds(row, orders, stride=BAND), :] = out[:orders, :LANES]
            high[pl.ds(row, orders, stride=BAND), :] = out[:orders, LANES:]
            edge_ref[row] = out[orders:].astype(jnp.bfloat16)
            return carry

        lax.fori_loop(0, BAND, transform, 0, unroll=2)
        first = side[0] == 0
        shape = own_ref.shape

        @pl.when(first)
        def _():
            own_ref[...] = low[...].astype(jnp.bfloat16).reshape(shape)
            send_ref[...] = high[...].astype(jnp.bfloat16).reshape(shape)

        @pl.when(jnp.logical_not(first))
        def _():
            own_ref[...] = high[...].astype(jnp.bfloat16).reshape(shape)
            send_ref[...] = low[...].astype(jnp.bfloat16).reshape(shape)


def mlp_call(band, side, filtered, cotangent, win_t, win, wout, table, earlier):
    channels, rows, columns = filtered.shape
    hidden = wout.shape[0]
    width = 2 * LANES
    steps = columns // width
    chunk = 2 * width
    orders = table.shape[0] - 16
    block = pl.BlockSpec((channels, BAND, width), lambda i: (0, band, i))
    cells = BAND * columns
    return pl.pallas_call(
        functools.partial(
            mlp_kernel, steps=steps, width=width, chunk=chunk, halo=band * (BAND - REACH)
        ),
        grid=(steps,),
        in_specs=[
            pl.BlockSpec(memory_space=pltpu.SMEM),
            block,
            block,
            whole_block(win_t.shape),
            whole_block(win.shape),
            whole_block(wout.shape),
            whole_block(table.shape),
            pl.BlockSpec(memory_space=pl.ANY),
        ],
        out_specs=[
            whole_block((BAND, channels, columns)),
            whole_block((orders, BAND, LANES)),
            whole_block((orders, BAND, LANES)),
            whole_block((BAND, 16, channels)),
            whole_block((REACH, channels, columns)),
            whole_block((channels, hidden)),
            whole_block((hidden, channels)),
        ],
        out_shape=[
            jax.ShapeDtypeStruct((BAND, channels, columns), jnp.bfloat16),
            jax.ShapeDtypeStruct((orders, BAND, LANES), jnp.bfloat16),
            jax.ShapeDtypeStruct((orders, BAND, LANES), jnp.bfloat16),
            jax.ShapeDtypeStruct((BAND, 16, channels), jnp.bfloat16),
            jax.ShapeDtypeStruct((REACH, channels, columns), jnp.bfloat16),
            jax.ShapeDtypeStruct((channels, hidden), jnp.float32),
            jax.ShapeDtypeStruct((hidden, channels), jnp.float32),
        ],
        scratch_shapes=[
            pltpu.VMEM((width // LANES, channels * BAND, LANES), jnp.float32),
            pltpu.VMEM((channels, BAND * width), jnp.bfloat16),
            pltpu.VMEM((channels, BAND * width), jnp.bfloat16),
            pltpu.VMEM((orders * BAND, LANES), jnp.float32),
            pltpu.VMEM((orders * BAND, LANES), jnp.float32),
        ]
        + [
            pltpu.VMEM((hidden, chunk), kind)
            for kind in (jnp.float32, jnp.float32, jnp.bfloat16, jnp.bfloat16) * 2
        ],
        compiler_params=params(60),
        cost_estimate=pl.CostEstimate(
            flops=2 * cells * channels * (5 * hidden + orders),
            bytes_accessed=6 * channels * cells,
            transcendentals=2 * hidden * cells,
        ),
        name="mlp",
    )(side, filtered, cotangent, win_t, win, wout, table, earlier)


def stencil_kernel(taps, before, rows, after, edges, place, earlier, q_ref, field, rim, *, first):
    channels, columns = field.shape[1:]
    field[0:REACH] = before[...]
    field[REACH : REACH + BAND] = rows[...]
    field[REACH + BAND :] = after[...]

    def spread(row, carry):
        rim[row] = mm_tn(edges[row], place[...]).astype(jnp.bfloat16)
        return carry

    lax.fori_loop(0, BAND + 2 * REACH, spread, 0, unroll=5)
    lane = lax.broadcasted_iota(jnp.int32, (16, LANES), 1)
    span = 2 * REACH + 1

    def row_body(row, carry):
        weights = {}
        for north in range(span):
            source = row + 2 * REACH - north
            for east in range(span):
                weights[north, east] = taps[((first + source) * span + north) * span + east].astype(
                    jnp.bfloat16
                )

        def tile_body(tile, inner):
            part = pl.ds(pl.multiple_of(tile * 16, 16), 16)
            sums = [None] * span
            for north in range(span):
                source = row + 2 * REACH - north
                here = field[source, part, :]
                ends = rim[source, part, :]
                for east in range(span):
                    past = east - REACH
                    shifted = here
                    if past < 0:
                        rim_tile = jnp.where(lane < -past, ends, here[:, :LANES])
                        shifted = jnp.concatenate([rim_tile, here[:, LANES:]], axis=1)
                    if past > 0:
                        rim_tile = jnp.where(lane >= LANES - past, ends, here[:, -LANES:])
                        shifted = jnp.concatenate([here[:, :-LANES], rim_tile], axis=1)
                    term = shifted * weights[north, east]
                    sums[east] = term if sums[east] is None else sums[east] + term
            total = sums[REACH].astype(jnp.float32)
            for east in range(span):
                if east != REACH:
                    moved = pltpu.roll(sums[east], (east - REACH) % columns, 1)
                    total = total + moved.astype(jnp.float32)
            q_ref[row, part, :] = total.astype(jnp.bfloat16)
            return inner

        return lax.fori_loop(0, channels // 16, tile_body, carry, unroll=4)

    lax.fori_loop(0, BAND, row_body, 0)


def stencil_call(band, taps, before, rows, after, edges, place, earlier):
    _, channels, columns = rows.shape

    def pair(index):
        return pl.BlockSpec((REACH, channels, columns), lambda i: (index, 0, 0))

    return pl.pallas_call(
        functools.partial(stencil_kernel, first=band * BAND),
        grid=(1,),
        in_specs=[
            pl.BlockSpec(memory_space=pltpu.SMEM),
            pair(before[1]),
            whole_block(rows.shape),
            pair(after[1]),
            whole_block(edges.shape),
            whole_block(place.shape),
            pl.BlockSpec(memory_space=pl.ANY),
        ],
        out_specs=whole_block(rows.shape),
        out_shape=jax.ShapeDtypeStruct(rows.shape, jnp.bfloat16),
        scratch_shapes=[
            pltpu.VMEM((BAND + 2 * REACH, channels, columns), jnp.bfloat16),
            pltpu.VMEM((BAND + 2 * REACH, channels, LANES), jnp.bfloat16),
        ],
        compiler_params=params(48),
        cost_estimate=pl.CostEstimate(
            flops=60 * channels * BAND * columns,
            bytes_accessed=4 * channels * BAND * columns,
            transcendentals=0,
        ),
        name="stencil",
    )(taps, before[0], rows, after[0], edges, place, earlier)


def disco_kernel_grad(bi_ref, q_ref, gd_ref, stage, flat):
    columns = q_ref.shape[2]
    gd_ref[...] = jnp.zeros_like(gd_ref)
    rows_first(bi_ref, stage, flat, columns)

    def body(row, carry):
        cells = pl.ds(pl.multiple_of(row * columns, columns), columns)
        gd_ref[...] += mm_nt(flat[:, cells], q_ref[row])
        return carry

    lax.fori_loop(0, BAND, body, 0, unroll=4)


def disco_grad_call(band, block_input, q):
    channels, _, columns = block_input.shape
    return pl.pallas_call(
        disco_kernel_grad,
        grid=(1,),
        in_specs=[
            pl.BlockSpec((channels, BAND, columns), lambda i: (0, band, 0)),
            whole_block(q.shape),
        ],
        out_specs=whole_block((channels, channels)),
        out_shape=jax.ShapeDtypeStruct((channels, channels), jnp.float32),
        scratch_shapes=[
            pltpu.VMEM((columns // LANES, channels * BAND, LANES), jnp.float32),
            pltpu.VMEM((channels, BAND * columns), jnp.bfloat16),
        ],
        compiler_params=params(48),
        cost_estimate=pl.CostEstimate(
            flops=2 * channels * channels * BAND * columns,
            bytes_accessed=4 * channels * BAND * columns,
            transcendentals=0,
        ),
        name="disco_weight",
    )(block_input, q)


def legendre_kernel(leg, p0, t0, p1, t1, gain, s0, s1, stage, *, steps, block):
    order = pl.program_id(0)
    degrees = leg.shape[1]
    half = leg.shape[2] // 2
    total = None
    for band, refs in enumerate(((p0, t0), (p1, t1))):
        pair = jnp.concatenate([ref[...].reshape(half, LANES) for ref in refs], axis=1)
        term = mm(leg[0, :, band * half : (band + 1) * half], pair)
        total = term if total is None else total + term
    real = total[:, :LANES]
    imag = total[:, LANES:]
    owners, band = s0.shape[:2]
    shape = (owners, -1, LANES)
    s1[:, band + order] = jnp.concatenate(
        [real.reshape(shape), imag.reshape(shape)], axis=1
    ).astype(jnp.bfloat16)
    g = gain[:, 0, 0].reshape(degrees, LANES)
    k = gain[:, 0, 1].reshape(degrees, LANES)
    scaled = jnp.concatenate([g * real + k * imag, g * imag - k * real], axis=1).astype(
        jnp.bfloat16
    )
    synth = mm_tn(leg[0], scaled)
    for r in range(2):
        stage[pl.ds(r * steps + order, 2 * half, stride=block), :] = synth[
            :, r * LANES : (r + 1) * LANES
        ]

    @pl.when(order == steps - 1)
    def _():
        s0[...] = stage[: half * block].astype(jnp.bfloat16).reshape(s0.shape)
        s1[:, :band] = stage[half * block :].astype(jnp.bfloat16).reshape(s0.shape)


def legendre_call(leg, r0, r1, gain):
    owners, block, band, lanes = r0.shape
    degrees = leg.shape[1]
    steps = block // 2
    real = pl.BlockSpec((owners, None, band, lanes), lambda m: (0, m, 0, 0))
    imag = pl.BlockSpec((owners, None, band, lanes), lambda m: (0, m + steps, 0, 0))
    g_shape = (owners, 1, 2, degrees // owners, lanes)
    g_spec = pl.BlockSpec(g_shape, lambda m: (0, m, 0, 0, 0))
    out = (owners, band, block, lanes)
    more = (owners, band + steps + 1, block, lanes)
    return pl.pallas_call(
        functools.partial(legendre_kernel, steps=steps, block=block),
        grid=(steps,),
        in_specs=[
            pl.BlockSpec((1, degrees, leg.shape[2]), lambda m: (m, 0, 0)),
            real,
            imag,
            real,
            imag,
            g_spec,
        ],
        out_specs=[whole_block(out), whole_block(more)],
        out_shape=[
            jax.ShapeDtypeStruct(out, jnp.bfloat16),
            jax.ShapeDtypeStruct(more, jnp.bfloat16),
        ],
        scratch_shapes=[pltpu.VMEM((2 * owners * band * block, lanes), jnp.float32)],
        compiler_params=params(48),
        cost_estimate=pl.CostEstimate(
            flops=8 * steps * degrees * leg.shape[2] * 256,
            bytes_accessed=7 * MIB,
            transcendentals=0,
        ),
        name="legendre",
    )(leg, r0, r0, r1, r1, gain)


def pair_sum_kernel(kept, arrived, *rest):
    out = rest[-1]
    block = kept.shape[0] // out.shape[0]
    total = kept[...].astype(jnp.float32) + arrived[...].astype(jnp.float32)
    out[:, :block] = total.astype(jnp.bfloat16).reshape(-1, block, *kept.shape[1:])
    if out.shape[1] > block:
        total = rest[0][...].astype(jnp.float32) + rest[1][...].astype(jnp.float32)
        out[:, block:] = total.astype(jnp.bfloat16)


def pair_sum_call(owners, kept, arrived, more, earlier):
    orders, band, lanes = kept.shape
    extra = more[0].shape[1] if more else 0
    shape = (owners, orders // owners + extra, band, lanes)
    return pl.pallas_call(
        pair_sum_kernel,
        grid=(1,),
        in_specs=[whole_block(array.shape) for array in (kept, arrived, *more)]
        + [pl.BlockSpec(memory_space=pl.ANY)] * len(earlier),
        out_specs=whole_block(shape),
        out_shape=jax.ShapeDtypeStruct(shape, jnp.bfloat16),
        compiler_params=params(32),
        name="pair_sum",
    )(kept, arrived, *more, *earlier)


def share_kernel(kept, arrived, before, out):
    total = kept[...].astype(jnp.float32) + arrived[...].astype(jnp.float32)
    out[...] = total.astype(jnp.bfloat16).reshape(out.shape)


def share_call(kept, arrived, parcel):
    owners, blocks, band, lanes = parcel.shape
    return pl.pallas_call(
        share_kernel,
        grid=(1,),
        in_specs=[whole_block(kept.shape)] * 2 + [pl.BlockSpec(memory_space=pl.ANY)],
        out_specs=pl.BlockSpec((owners, 1, band, lanes), lambda i: (0, blocks - 1, 0, 0)),
        out_shape=jax.ShapeDtypeStruct(parcel.shape, jnp.bfloat16),
        input_output_aliases={2: 0},
        name="share",
    )(kept, arrived, parcel)


def split_kernel(parcel, shares, earlier, synth, owned, totals):
    band = synth.shape[1]
    degrees = owned.shape[1]
    synth[...] = parcel[:, :band]
    owned[...] = parcel[:, band : band + degrees].astype(jnp.float32)
    blocks = totals.shape[1] - 1
    first = shares[...].astype(jnp.float32).sum(axis=0).astype(jnp.bfloat16)
    last = parcel[:, band + degrees :].astype(jnp.float32).sum(axis=0).astype(jnp.bfloat16)
    totals[:, :blocks] = jnp.broadcast_to(first[None], (totals.shape[0],) + first.shape)
    totals[:, blocks:] = jnp.broadcast_to(last[None], (totals.shape[0],) + last.shape)


def split_call(count, degrees, parcel, shares, earlier):
    owners, blocks, band, lanes = parcel.shape
    more = shares.shape[1] - band
    shapes = (
        ((owners, band, band, lanes), jnp.bfloat16),
        ((owners, degrees, band, lanes), jnp.float32),
        ((count, more + 1, band, lanes), jnp.bfloat16),
    )
    return pl.pallas_call(
        split_kernel,
        grid=(1,),
        in_specs=[
            whole_block(parcel.shape),
            pl.BlockSpec((owners, more, band, lanes), lambda i: (0, band // more, 0, 0)),
            pl.BlockSpec(memory_space=pl.ANY),
        ],
        out_specs=[whole_block(shape) for shape, _ in shapes],
        out_shape=[jax.ShapeDtypeStruct(shape, kind) for shape, kind in shapes],
        compiler_params=params(32),
        name="split",
    )(parcel, shares, earlier)


def final_kernel(side, q_ref, own, other, table, wd, *rest):
    out_ref, stage = rest[-2:]
    width = q_ref.shape[2]
    orders = table.shape[0]
    channels = out_ref.shape[0]
    first = side[0] == 0

    def body(row, carry):
        mine = own[:, row].reshape(orders, LANES)
        theirs = other[:, row].reshape(orders, LANES)
        synth = jnp.concatenate(
            [jnp.where(first, mine, theirs), jnp.where(first, theirs, mine)], axis=1
        )
        out = mm_tn(synth, table[...]) + mm(wd[...], q_ref[row])
        for tile in range(width // LANES):
            stage[tile, pl.ds(row, channels, stride=BAND), :] = out[
                :, tile * LANES : (tile + 1) * LANES
            ]
        return carry

    lax.fori_loop(0, BAND, body, 0, unroll=2)
    for tile in range(width // LANES):
        out_ref[:, :, tile * LANES : (tile + 1) * LANES] = (
            stage[tile].astype(jnp.bfloat16).reshape(channels, BAND, LANES)
        )


def final_call(band, rows, side, q, own, other, table, wd, previous):
    _, channels, columns = q.shape
    width = 2 * LANES
    cells = BAND * columns
    extra = [] if previous is None else [previous]
    return pl.pallas_call(
        final_kernel,
        grid=(columns // width,),
        in_specs=[
            pl.BlockSpec(memory_space=pltpu.SMEM),
            pl.BlockSpec((BAND, channels, width), lambda i: (0, 0, i)),
            whole_block(other.shape),
            whole_block(other.shape),
            pl.BlockSpec((table.shape[0], width), lambda i: (0, i)),
            whole_block(wd.shape),
        ]
        + [pl.BlockSpec(memory_space=pl.ANY)] * len(extra),
        out_specs=pl.BlockSpec((channels, BAND, width), lambda i: (0, band, i)),
        out_shape=jax.ShapeDtypeStruct((channels, rows, columns), jnp.bfloat16),
        scratch_shapes=[pltpu.VMEM((width // LANES, channels * BAND, LANES), jnp.float32)],
        input_output_aliases={6: 0} if extra else {},
        compiler_params=params(48),
        cost_estimate=pl.CostEstimate(
            flops=2 * cells * channels * (channels + table.shape[0]),
            bytes_accessed=5 * channels * cells,
            transcendentals=0,
        ),
        name="final",
    )(side, q, own, other, table, wd, *extra)


def gain_kernel(gain, out, *, degrees):
    for degree in range(degrees):
        for r in range(2):
            part = gain[pl.ds(degree * 2 * LANES + r, LANES, stride=2), :]
            out[pl.ds(r * degrees + degree, LANES, stride=2 * degrees), :] = part.T


def gain_call(gain):
    degrees, channels, _, orders = gain.shape
    flat = gain.reshape(degrees * channels * 2, orders)
    return pl.pallas_call(
        functools.partial(gain_kernel, degrees=degrees),
        out_shape=jax.ShapeDtypeStruct((orders * 2 * degrees, channels), jnp.float32),
        name="gain",
    )(flat)


def grad_gain_kernel(owned, saved, out, *, degrees):
    for degree in range(degrees):
        real = owned[pl.ds(degree, LANES, stride=2 * degrees), :].T
        imag = owned[pl.ds(degrees + degree, LANES, stride=2 * degrees), :].T
        start = degree * 2 * LANES
        s = saved[pl.ds(start, LANES, stride=2), :]
        t = saved[pl.ds(start + 1, LANES, stride=2), :]
        out[pl.ds(start, LANES, stride=2), :] = real * s + imag * t
        out[pl.ds(start + 1, LANES, stride=2), :] = imag * s - real * t


def grad_gain_call(owned, saved):
    degrees, channels, _, orders = saved.shape
    flat = saved.reshape(degrees * channels * 2, orders)
    out = pl.pallas_call(
        functools.partial(grad_gain_kernel, degrees=degrees),
        out_shape=jax.ShapeDtypeStruct(flat.shape, jnp.float32),
        name="grad_gain",
    )(owned, flat)
    return out.reshape(saved.shape)


def legendre_whole():
    upper, lower, diagonal_log = legendre_tables()
    theta = (np.arange(NLAT) + 0.5) * (math.pi / NLAT)
    sine, cosine = np.sin(theta)[None], np.cos(theta)[None]
    orders = np.arange(M)
    start = np.exp(diagonal_log[:, None] + orders[:, None] * np.log(sine))
    table = np.zeros((M, L, NLAT))
    previous = before = np.zeros((M, NLAT))
    for degree in range(L):
        fresh = np.where(
            (orders == degree)[:, None],
            start,
            upper[degree][:, None] * (cosine * previous - lower[degree][:, None] * before),
        )
        table[:, degree] = fresh
        previous, before = fresh, previous
    return table * np.sqrt(sine * (math.pi / NLAT))[None]


def host_tables(lat_count, lon_count):
    columns, rows, own = NLON // lon_count, NLAT // lat_count, M // lat_count
    angle = (np.arange(M)[:, None] * np.arange(NLON)[None, :] % NLON) * (2.0 * math.pi / NLON)
    waves = np.stack([np.cos(angle), -np.sin(angle)]) / math.sqrt(NLON)
    factor = np.where(np.arange(M) == 0, 1.0, 2.0)[None, :, None]

    def arrange(table):
        table = table.reshape(2, lat_count, own, lon_count, columns)
        return table.transpose(3, 1, 0, 2, 4).reshape(lon_count, 2 * M, columns)

    pick = np.zeros((lon_count, 16, columns))
    for row, column in enumerate((0, 1, columns - 2, columns - 1)):
        pick[:, row, column] = 1.0
    forward = np.concatenate([arrange(waves * factor), pick], axis=1)
    legendre = legendre_whole().reshape(M, L, lat_count, rows // BAND, BAND)
    legendre = legendre.transpose(0, 1, 3, 2, 4).reshape(M, L, NLAT)
    kind = jnp.bfloat16
    return forward.astype(kind), arrange(waves).astype(kind), legendre.astype(kind)


def shards_banded(
    cotangent,
    block_input,
    filtered,
    spectral_saved,
    spectral_gain,
    w_in,
    w_out,
    w_disco,
    quad_weights,
    lat_offsets,
    lon_offsets,
    weight_index,
):
    channels, rows, columns = cotangent.shape
    lat_count = lax.axis_size("lat")
    lon_count = lax.axis_size("lon")
    lat_index = lax.axis_index("lat")
    lon_index = lax.axis_index("lon")
    own = M // lat_count
    degrees = L // lat_count
    side = lon_index.reshape(1).astype(jnp.int32)
    forward, inverse, legendre = host_tables(lat_count, lon_count)
    forward = lax.dynamic_index_in_dim(jnp.asarray(forward), lon_index, 0, keepdims=False)
    inverse = lax.dynamic_index_in_dim(jnp.asarray(inverse), lon_index, 0, keepdims=False)
    legendre = lax.dynamic_slice_in_dim(jnp.asarray(legendre), lat_index * own, own, 0)
    swap = [(i, (i + 1) % lon_count) for i in range(lon_count)]
    exchange = functools.partial(lax.all_to_all, axis_name="lat", split_axis=0, concat_axis=0, tiled=True)

    kernel = disco_kernel(quad_weights, lat_offsets, lon_offsets, weight_index)
    kernel_pad = jnp.pad(kernel, ((REACH, REACH), (0, 0), (0, 0)))
    kernel_rim = lax.dynamic_slice_in_dim(kernel_pad, lat_index * rows, rows + 2 * REACH, 0)
    taps = kernel_rim.reshape(-1)
    place = np.zeros((16, LANES), np.float32)
    for row, lane in enumerate((0, 1, LANES - 2, LANES - 1)):
        place[row, lane] = 1.0
    place = jnp.asarray(place, jnp.bfloat16)
    w_in_t = w_in.T

    down = [(i, (i + 1) % lat_count) for i in range(lat_count)]
    up = [(target, source) for source, target in down]

    def across(moves):
        return [
            (a * lon_count + i, b * lon_count + j) for a, b in moves for i, j in swap
        ]

    def dealt(array):
        blocks = array.astype(jnp.bfloat16).reshape(lat_count, lon_count, -1, BAND, LANES)
        half = functools.partial(lax.dynamic_index_in_dim, blocks, axis=1, keepdims=False)
        return half(lon_index), lax.ppermute(half(1 - lon_index), "lon", swap)

    gain = gain_call(spectral_gain).reshape(lat_count, own, 2, degrees, LANES)
    gf0, kept0, sent0, ends0, head, gin0, gout0 = mlp_call(
        0, side, filtered, cotangent, w_in_t, w_in, w_out, forward, gain
    )
    gain = exchange(gain)
    arrived0 = lax.ppermute(sent0, "lon", swap)
    bottom = lax.ppermute(head, "lat", up)
    sides0 = lax.ppermute(ends0, "lon", swap)
    bottom_side = lax.ppermute(ends0[:REACH], ("lat", "lon"), across(up))
    gf1, kept1, sent1, ends1, tail, gin1, gout1 = mlp_call(
        1, side, filtered, cotangent, w_in_t, w_in, w_out, forward, gain
    )
    sides1 = lax.ppermute(ends1, "lon", swap)
    top = lax.ppermute(tail, "lat", down)
    top_side = lax.ppermute(ends1[BAND - REACH :], ("lat", "lon"), across(down))
    arrived1 = lax.ppermute(sent1, "lon", swap)
    half = w_in.shape[1] // 2
    gin = gin0 + gin1
    weights = jnp.concatenate([gin[:, :half], gin[:, half:], gout0 + gout1], axis=0)
    sum0 = pair_sum_call(
        lat_count, kept0, arrived0, (), (bottom, bottom_side, sides0, top, top_side)
    )
    received0 = exchange(sum0)
    edges1 = jnp.concatenate([sides0[BAND - REACH :], sides1, bottom_side], axis=0)
    q1 = stencil_call(1, taps, (gf0, BAND // REACH - 1), gf1, (bottom, 0), edges1, place, sum0)
    received1 = exchange(pair_sum_call(lat_count, kept1, arrived1, dealt(weights), (q1,)))
    edges0 = jnp.concatenate([top_side, sides0, sides1[:REACH]], axis=0)
    q0 = stencil_call(0, taps, (top, 0), gf0, (gf1, 0), edges0, place, q1)
    disco1 = disco_grad_call(1, block_input, q1)
    disco0 = disco_grad_call(0, block_input, q0)
    s0, s1 = legendre_call(legendre, received0, received1, gain)
    local0 = exchange(s0)
    other0 = lax.ppermute(local0, "lon", swap)
    parcel = exchange(share_call(*dealt(disco0 + disco1), s1))
    result = final_call(0, rows, side, q0, local0, other0, inverse, w_disco, None)
    count = lat_count * lon_count
    synth1, owned, totals = split_call(count, degrees, parcel, received1, result)
    other1 = lax.ppermute(synth1, "lon", swap)
    totals = lax.all_to_all(totals, ("lat", "lon"), split_axis=0, concat_axis=0, tiled=True)
    grad_gain = grad_gain_call(owned.reshape(M * 2 * degrees, LANES), spectral_saved)
    result = final_call(1, rows, side, q1, synth1, other1, inverse, w_disco, result)
    totals = totals.astype(jnp.float32)
    total_disco = totals[:, -1].reshape(channels, channels)
    totals = totals[:, :-1].reshape(-1, channels)
    total_in = jnp.concatenate([totals[:channels], totals[channels : 2 * channels]], axis=1)
    total_out = totals[2 * channels :]
    scale = 1.0 / math.sqrt(NLAT * NLON)
    return (result, grad_gain, total_in * scale, total_out * scale, total_disco * scale)


def shards(*arrays):
    channels, rows, columns = arrays[0].shape
    lat_count = lax.axis_size("lat")
    lon_count = lax.axis_size("lon")
    fits = (
        rows == 2 * BAND
        and lon_count == 2
        and channels == lon_count * LANES
        and columns % (2 * LANES) == 0
        and M == LANES
        and M // lat_count == 8
        and L // lat_count == 8
    )
    return shards_banded(*arrays) if fits else shards_general(*arrays)


def solution(mesh):
    placed = (
        P(None, "lat", "lon"),
        P(None, "lat", "lon"),
        P(None, "lat", "lon"),
        P("lat", "lon", None, None),
        P("lat", "lon", None, None),
        P(),
        P(),
        P(),
        P(),
        P(),
        P(),
        P(),
    )
    return jax.shard_map(
        shards,
        mesh=mesh,
        in_specs=placed,
        out_specs=(P(None, "lat", "lon"), P("lat", "lon", None, None), P(), P(), P()),
        check_vma=False,
    )
```

```python
import functools
import math

import jax
import jax.numpy as jnp
import numpy as np
from jax import lax
from jax.experimental import pallas as pl
from jax.experimental.pallas import tpu as pltpu
from jax.sharding import PartitionSpec as P

NLAT = 512
NLON = 1024
L = 128
M = 128
REACH = 2
NQ = 64


root_half = 0.7071067811865476
root_two_pi = 2.5066282746310002


def padded_2(block, sides, width):
    for axis, dim in sides:
        count = lax.axis_size(axis)
        forward = [(i, i + 1) for i in range(count - 1)]
        forward.append((count - 1, 0))
        backward = [(target, source) for source, target in forward]
        low = lax.ppermute(
            lax.slice_in_dim(block, block.shape[dim] - width, None, axis=dim), axis, forward
        )
        high = lax.ppermute(lax.slice_in_dim(block, 0, width, axis=dim), axis, backward)
        block = jnp.concatenate([low, block, high], axis=dim)
    return block


def gelu_value(value):
    return value * 0.5 * (1.0 + lax.erf(value * root_half))


def gelu_slope(value):
    return (
        0.5 * (1.0 + lax.erf(value * root_half))
        + value * jnp.exp(-0.5 * value * value) / root_two_pi
    )


def legendre_tables():
    degree = np.arange(L)[:, None] * 1.0
    order = np.arange(M)[None, :] * 1.0
    upper = np.where(
        degree > order,
        np.sqrt(
            np.maximum(4.0 * degree * degree - 1.0, 0.0)
            / np.maximum(degree * degree - order * order, 1.0)
        ),
        0.0,
    )
    lower = np.where(
        degree > order + 1.0,
        np.sqrt(
            np.maximum((degree - 1.0) ** 2 - order * order, 0.0)
            / np.maximum(4.0 * (degree - 1.0) ** 2 - 1.0, 1.0)
        ),
        0.0,
    )
    counter = np.arange(1, M) * 1.0
    diagonal_log = np.concatenate(
        [np.zeros(1), np.cumsum(0.5 * np.log((2.0 * counter + 1.0) / (2.0 * counter)))]
    ) - 0.5 * np.log(2.0)
    return (upper, lower, diagonal_log)


def legendre_rows(theta):
    upper, lower, diagonal_log = legendre_tables()
    float_type = theta.dtype
    cosine = jnp.cos(theta)[:, None]
    sine = jnp.sin(theta)
    orders = jnp.arange(M, dtype=jnp.int32)
    start_value = jnp.exp(
        jnp.asarray(diagonal_log, float_type)[None, :]
        + orders.astype(float_type)[None, :] * jnp.log(sine)[:, None]
    )

    def advance(carry, inputs):
        previous, before = carry
        degree, coef_up, coef_low = inputs
        fresh = jnp.where(
            (orders == degree)[None, :],
            start_value,
            coef_up[None, :] * (cosine * previous - coef_low[None, :] * before),
        )
        return ((fresh, previous), fresh)

    empty = jnp.zeros_like(start_value)
    final, table = lax.scan(
        advance,
        (empty, empty),
        (
            jnp.arange(L, dtype=jnp.int32),
            jnp.asarray(upper, float_type),
            jnp.asarray(lower, float_type),
        ),
    )
    weight = jnp.sqrt(sine * (math.pi / NLAT))
    return table * weight[None, :, None]


def forward_table():
    column = jnp.arange(NLON, dtype=jnp.int32)[:, None]
    order = jnp.arange(M, dtype=jnp.int32)[None, :]
    angle = (column * order % NLON).astype(jnp.float32) * (2.0 * math.pi / NLON)
    factor = jnp.where(order == 0, 1.0, 2.0).astype(jnp.float32) / math.sqrt(NLON)
    return jnp.concatenate([factor * jnp.cos(angle), -factor * jnp.sin(angle)], axis=1).astype(
        jnp.bfloat16
    )


def inverse_table():
    order = jnp.arange(M, dtype=jnp.int32)[:, None]
    column = jnp.arange(NLON, dtype=jnp.int32)[None, :]
    angle = (column * order % NLON).astype(jnp.float32) * (2.0 * math.pi / NLON)
    return (jnp.concatenate([jnp.cos(angle), -jnp.sin(angle)], axis=0) / math.sqrt(NLON)).astype(
        jnp.bfloat16
    )


def disco_kernel(quad_weights, lat_offsets, lon_offsets, weight_index):
    span = jnp.arange(-REACH, REACH + 1, dtype=jnp.int32)
    slots = jnp.arange(NQ, dtype=jnp.int32)
    values = jnp.sum(
        jnp.where(
            weight_index[:, :, None] == slots[None, None, :], quad_weights[None, None, :], 0.0
        ),
        axis=2,
    )
    north = (lat_offsets[:, :, None] == span[None, None, :]).astype(quad_weights.dtype)
    east = (lon_offsets[:, :, None] == span[None, None, :]).astype(quad_weights.dtype)
    return jnp.sum(values[:, :, None, None] * north[:, :, :, None] * east[:, :, None, :], axis=1)


def disco_apply(padded, kernel):
    height = kernel.shape[0]
    width = padded.shape[2] - 2 * REACH
    total = jnp.zeros((padded.shape[0], height, width), kernel.dtype)
    for north in range(2 * REACH + 1):
        for east in range(2 * REACH + 1):
            total = (
                total
                + kernel[None, :, north, east, None]
                * padded[:, north : north + height, east : east + width]
            )
    return total


def disco_adjoint(padded, kernel_rim):
    height = kernel_rim.shape[0] - 2 * REACH
    width = padded.shape[2] - 2 * REACH
    total = jnp.zeros((padded.shape[0], height, width), kernel_rim.dtype)
    for north in range(2 * REACH + 1):
        for east in range(2 * REACH + 1):
            row_shift = 2 * REACH - north
            col_shift = 2 * REACH - east
            total = (
                total
                + kernel_rim[None, row_shift : row_shift + height, north, east, None]
                * padded[:, row_shift : row_shift + height, col_shift : col_shift + width]
            )
    return total


def inside_rows(padded, first_row):
    height = padded.shape[1]
    latitude = first_row - REACH + jnp.arange(height, dtype=jnp.int32)
    keep = (latitude >= 0) & (latitude < NLAT)
    return jnp.where(keep[None, :, None], padded, jnp.zeros((), padded.dtype))


def shards_general(
    cotangent,
    block_input,
    filtered,
    spectral_saved,
    spectral_gain,
    w_in,
    w_out,
    w_disco,
    quad_weights,
    lat_offsets,
    lon_offsets,
    weight_index,
):
    channels, rows, columns = cotangent.shape
    lat_count = lax.axis_size("lat")
    first_row = lax.axis_index("lat") * rows
    cells = rows * columns
    flat_in = filtered.reshape(channels, cells)
    flat_cot = cotangent.reshape(channels, cells)
    hidden_pre = lax.dot_general(
        w_in, flat_in, (((0,), (0,)), ((), ())), preferred_element_type=jnp.float32
    )
    activation = gelu_value(hidden_pre).astype(jnp.bfloat16)
    grad_act = jnp.dot(w_out, flat_cot, preferred_element_type=jnp.float32)
    grad_pre = (grad_act * gelu_slope(hidden_pre)).astype(jnp.bfloat16)
    grad_in_part = lax.dot_general(
        flat_in, grad_pre, (((1,), (1,)), ((), ())), preferred_element_type=jnp.float32
    )
    grad_out_part = lax.dot_general(
        activation, flat_cot, (((1,), (1,)), ((), ())), preferred_element_type=jnp.float32
    )
    grad_flat = jnp.dot(w_in, grad_pre, preferred_element_type=jnp.float32).astype(jnp.bfloat16)
    grad_filtered = grad_flat.reshape(channels, rows, columns)
    spread = lax.all_to_all(grad_filtered, "lon", split_axis=0, concat_axis=2, tiled=True)
    local_channels = spread.shape[0]
    coeffs = (
        jnp.dot(
            spread.reshape(local_channels * rows, NLON),
            forward_table(),
            preferred_element_type=jnp.float32,
        )
        .astype(jnp.bfloat16)
        .reshape(local_channels, rows, 2, M)
    )
    theta_rows = ((first_row + jnp.arange(rows, dtype=jnp.int32)).astype(jnp.float32) + 0.5) * (
        math.pi / NLAT
    )
    legendre = legendre_rows(theta_rows).astype(jnp.bfloat16)
    owned_count = L // lat_count
    weights = lax.slice_in_dim(legendre, 0, owned_count * lax.axis_size("lat"), axis=0)
    owned = lax.psum_scatter(
        jnp.einsum("ljm,cjrm->lcrm", weights, coeffs, preferred_element_type=jnp.float32),
        "lat",
        scatter_dimension=0,
        tiled=True,
    )
    real_part = owned[:, :, 0]
    imag_part = owned[:, :, 1]
    grad_gain = jnp.stack(
        [
            real_part * spectral_saved[:, :, 0] + imag_part * spectral_saved[:, :, 1],
            imag_part * spectral_saved[:, :, 0] - real_part * spectral_saved[:, :, 1],
        ],
        axis=2,
    )
    scaled = jnp.stack(
        [
            spectral_gain[:, :, 0] * real_part + spectral_gain[:, :, 1] * imag_part,
            spectral_gain[:, :, 0] * imag_part - spectral_gain[:, :, 1] * real_part,
        ],
        axis=2,
    ).astype(jnp.bfloat16)
    piece = lax.all_gather(scaled, "lat", axis=0, tiled=True)
    weights = lax.slice_in_dim(legendre, 0, piece.shape[0], axis=0)
    synthesis = (
        jnp.zeros((local_channels, rows, 2, M), jnp.float32)
        + jnp.einsum("ljm,lcrm->cjrm", weights, piece, preferred_element_type=jnp.float32)
    ).astype(jnp.bfloat16)
    grid_rows = jnp.dot(
        synthesis.reshape(local_channels * rows, 2 * M),
        inverse_table(),
        preferred_element_type=jnp.float32,
    ).reshape(local_channels, rows, NLON)
    spectral_grad = lax.all_to_all(grid_rows, "lon", split_axis=2, concat_axis=0, tiled=True)
    kernel = disco_kernel(quad_weights, lat_offsets, lon_offsets, weight_index)
    kernel_pad = jnp.pad(kernel, ((REACH, REACH), (0, 0), (0, 0)))
    kernel_rim = lax.dynamic_slice_in_dim(kernel_pad, first_row, rows + 2 * REACH, 0)
    stacked_rims = padded_2(
        jnp.stack((block_input, grad_filtered)), (("lat", 2), ("lon", 3)), REACH
    )
    input_pad = inside_rows(stacked_rims[0], first_row)
    grad_source = inside_rows(stacked_rims[1], first_row)
    grad_pad = lax.dot_general(
        w_disco, grad_source, (((1,), (0,)), ((), ())), preferred_element_type=jnp.float32
    ).astype(jnp.bfloat16)
    mixed = disco_apply(input_pad, kernel_rim[REACH : REACH + rows]).astype(jnp.bfloat16)
    grad_disco_part = lax.dot_general(
        mixed.reshape(channels, cells),
        grad_flat,
        (((1,), (1,)), ((), ())),
        preferred_element_type=jnp.float32,
    )
    disco_grad = disco_adjoint(grad_pad, kernel_rim)
    grad_input = (spectral_grad + disco_grad).astype(jnp.bfloat16)
    total_in, total_out, total_disco = lax.psum(
        (grad_in_part, grad_out_part, grad_disco_part), ("lat", "lon")
    )
    scale = 1.0 / math.sqrt(NLAT * NLON)
    return (grad_input, grad_gain, total_in * scale, total_out * scale, total_disco * scale)


BAND = 16
LANES = 128
MIB = 1024 * 1024
MLP_CHUNK = 512


def mm(a, b):
    return jnp.dot(a, b, preferred_element_type=jnp.float32)


def mm_nt(a, b):
    return lax.dot_general(a, b, (((1,), (1,)), ((), ())), preferred_element_type=jnp.float32)


def mm_tn(a, b):
    return lax.dot_general(a, b, (((0,), (0,)), ((), ())), preferred_element_type=jnp.float32)


def params(mib):
    return pltpu.CompilerParams(vmem_limit_bytes=mib * MIB)


def whole_block(shape):
    return pl.BlockSpec(shape, lambda *_: (0,) * len(shape))


def rows_first(block, stage, flat, width):
    channels = block.shape[0]
    for tile in range(width // LANES):
        stage[tile] = (
            block[:, :, tile * LANES : (tile + 1) * LANES]
            .astype(jnp.float32)
            .reshape(channels * BAND, LANES)
        )
    for row in range(BAND):
        for tile in range(width // LANES):
            start = row * width + tile * LANES
            flat[:, start : start + LANES] = stage[
                tile, pl.ds(row, channels, stride=BAND), :
            ].astype(jnp.bfloat16)


def gelu_both(value):
    decay = jnp.exp(value * value * -0.5)
    base = 1.0 + (0.3275911 * root_half) * jnp.abs(value)
    inverse = pl.reciprocal(base, approx=True)
    inverse = inverse * (2.0 - base * inverse)
    poly = 0.5 * 1.061405429
    for term in (-1.453152027, 1.421413741, -0.284496736, 0.254829592):
        poly = poly * inverse + 0.5 * term
    tail = poly * inverse * decay
    chance = jnp.where(value >= 0.0, 1.0 - tail, tail)
    return chance, decay


def mlp_kernel(
    side, x_ref, ct_ref, win_t, win, wout, *rest, steps, width, chunk, halo, pieces,
):
    left = rest[: max(pieces - 1, 0)]
    table = rest[len(left)] if pieces else None
    rest = rest[pieces + 1 :]
    if pieces:
        gf_ref, own_ref, send_ref, edge_ref, halo_ref, gin_ref, gout_ref = rest[:7]
        stage, xs, cs, low, high = rest[7:]
    else:
        gf_ref, gin_ref, gout_ref, stage, xs, cs = rest
    step = pl.program_id(0)

    @pl.when(step == 0)
    def _():
        gin_ref[...] = jnp.zeros_like(gin_ref)
        gout_ref[...] = jnp.zeros_like(gout_ref)

    rows_first(x_ref, stage, xs, width)
    rows_first(ct_ref, stage, cs, width)
    column = pl.multiple_of(step * width, width)
    per = chunk // width

    def body(index, carry):
        cells = pl.ds(pl.multiple_of(index * chunk, chunk), chunk)
        x = xs[:, cells]
        c = cs[:, cells]
        pre = mm(win_t[...], x)
        grad = mm(wout[...], c)
        chance, decay = gelu_both(pre)
        act = (pre * chance).astype(jnp.bfloat16)
        gp = (grad * (chance + pre * decay * (1.0 / root_two_pi))).astype(jnp.bfloat16)
        gf = mm(win[...], gp).astype(jnp.bfloat16)
        for part in range(per):
            gf_ref[index * per + part, :, pl.ds(column, width)] = gf[
                :, part * width : (part + 1) * width
            ]
        gin_ref[...] += mm_nt(x, gp)
        gout_ref[...] += mm_nt(act, c)
        return carry

    lax.fori_loop(0, BAND * width // chunk, body, 0, unroll=2)
    if not pieces:
        return

    @pl.when(step == steps - 1)
    def _():
        parts = [*left, gf_ref]
        spans = []
        for ref in parts:
            start = spans[-1][1] if spans else 0
            spans.append((start, start + ref.shape[2]))
        for ref, (start, stop) in zip(parts, spans):
            halo_ref[:, :, start:stop] = ref[halo : halo + REACH]
        orders = low.shape[0] // BAND

        def transform(row, carry):
            out = None
            for ref, (start, stop) in zip(parts, spans):
                term = mm_nt(table[:, start:stop], ref[row])
                out = term if out is None else out + term
            low[pl.ds(row, orders, stride=BAND), :] = out[:orders, :LANES]
            high[pl.ds(row, orders, stride=BAND), :] = out[:orders, LANES:]
            edge_ref[row] = out[orders:].astype(jnp.bfloat16)
            return carry

        lax.fori_loop(0, BAND, transform, 0, unroll=2)
        first = side[0] == 0
        shape = own_ref.shape

        @pl.when(first)
        def _():
            own_ref[...] = low[...].astype(jnp.bfloat16).reshape(shape)
            send_ref[...] = high[...].astype(jnp.bfloat16).reshape(shape)

        @pl.when(jnp.logical_not(first))
        def _():
            own_ref[...] = high[...].astype(jnp.bfloat16).reshape(shape)
            send_ref[...] = low[...].astype(jnp.bfloat16).reshape(shape)


def mlp_call(band, span, side, filtered, cotangent, win_t, win, wout, left, table, earlier):
    channels, rows, columns = filtered.shape
    hidden = wout.shape[0]
    width = LANES
    offset = span[0] // width
    steps = (span[1] - span[0]) // width
    chunk = MLP_CHUNK
    orders = table.shape[0] - 16
    last = span[1] == columns
    pieces = len(left) + 1 if last else 0
    block = pl.BlockSpec((channels, BAND, width), lambda i: (0, band, offset + i))
    cells = BAND * (span[1] - span[0])
    outs = [((BAND, channels, span[1] - span[0]), jnp.bfloat16)]
    if last:
        outs += [
            ((orders, BAND, LANES), jnp.bfloat16),
            ((orders, BAND, LANES), jnp.bfloat16),
            ((BAND, 16, channels), jnp.bfloat16),
            ((REACH, channels, columns), jnp.bfloat16),
        ]
    outs += [((channels, hidden), jnp.float32), ((hidden, channels), jnp.float32)]
    tables = [*left, table] if last else []
    return pl.pallas_call(
        functools.partial(
            mlp_kernel,
            steps=steps,
            width=width,
            chunk=chunk,
            halo=band * (BAND - REACH),
            pieces=pieces,
        ),
        grid=(steps,),
        in_specs=[
            pl.BlockSpec(memory_space=pltpu.SMEM),
            block,
            block,
            whole_block(win_t.shape),
            whole_block(win.shape),
            whole_block(wout.shape),
        ]
        + [whole_block(array.shape) for array in tables]
        + [pl.BlockSpec(memory_space=pl.ANY)],
        out_specs=[whole_block(shape) for shape, _ in outs],
        out_shape=[jax.ShapeDtypeStruct(shape, kind) for shape, kind in outs],
        scratch_shapes=[
            pltpu.VMEM((width // LANES, channels * BAND, LANES), jnp.float32),
            pltpu.VMEM((channels, BAND * width), jnp.bfloat16),
            pltpu.VMEM((channels, BAND * width), jnp.bfloat16),
        ]
        + [pltpu.VMEM((orders * BAND, LANES), jnp.float32)] * (2 if last else 0),
        compiler_params=params(60),
        cost_estimate=pl.CostEstimate(
            flops=2 * cells * channels * (5 * hidden + orders),
            bytes_accessed=6 * channels * cells,
            transcendentals=2 * hidden * cells,
        ),
        name="mlp",
    )(side, filtered, cotangent, win_t, win, wout, *tables, earlier)


def stencil_kernel(taps, *rest, first, counts):
    edges, place, _, q_ref, field, rim = rest[sum(counts) :]
    channels, columns = field.shape[1:]
    pieces = iter(rest)
    low = 0
    for count, height in zip(counts, (REACH, BAND, REACH)):
        start = 0
        for _ in range(count):
            piece = next(pieces)
            stop = start + piece.shape[2]
            field[low : low + height, :, start:stop] = piece[...]
            start = stop
        low += height

    def spread(row, carry):
        rim[row] = mm_tn(edges[row], place[...]).astype(jnp.bfloat16)
        return carry

    lax.fori_loop(0, BAND + 2 * REACH, spread, 0, unroll=5)
    lane = lax.broadcasted_iota(jnp.int32, (16, LANES), 1)
    span = 2 * REACH + 1

    def row_body(row, carry):
        weights = {}
        for north in range(span):
            source = row + 2 * REACH - north
            for east in range(span):
                weights[north, east] = taps[((first + source) * span + north) * span + east].astype(
                    jnp.bfloat16
                )

        def tile_body(tile, inner):
            part = pl.ds(pl.multiple_of(tile * 16, 16), 16)
            sums = [None] * span
            for north in range(span):
                source = row + 2 * REACH - north
                here = field[source, part, :]
                ends = rim[source, part, :]
                for east in range(span):
                    past = east - REACH
                    shifted = here
                    if past < 0:
                        rim_tile = jnp.where(lane < -past, ends, here[:, :LANES])
                        shifted = jnp.concatenate([rim_tile, here[:, LANES:]], axis=1)
                    if past > 0:
                        rim_tile = jnp.where(lane >= LANES - past, ends, here[:, -LANES:])
                        shifted = jnp.concatenate([here[:, :-LANES], rim_tile], axis=1)
                    term = shifted * weights[north, east]
                    sums[east] = term if sums[east] is None else sums[east] + term
            total = sums[REACH].astype(jnp.float32)
            for east in range(span):
                if east != REACH:
                    moved = pltpu.roll(sums[east], (east - REACH) % columns, 1)
                    total = total + moved.astype(jnp.float32)
            q_ref[row, part, :] = total.astype(jnp.bfloat16)
            return inner

        return lax.fori_loop(0, channels // 16, tile_body, carry, unroll=4)

    lax.fori_loop(0, BAND, row_body, 0)


def stencil_call(band, taps, before, rows, after, edges, place, earlier):
    sources = (before, rows, after)
    channels = rows[0][0].shape[1]
    columns = sum(piece.shape[2] for piece in rows[0])
    shape = (BAND, channels, columns)

    def piece_spec(piece, height, index):
        return pl.BlockSpec((height, channels, piece.shape[2]), lambda i: (index, 0, 0))

    return pl.pallas_call(
        functools.partial(
            stencil_kernel, first=band * BAND, counts=[len(pieces) for pieces, _ in sources]
        ),
        grid=(1,),
        in_specs=[pl.BlockSpec(memory_space=pltpu.SMEM)]
        + [
            piece_spec(piece, height, index)
            for (pieces, index), height in zip(sources, (REACH, BAND, REACH))
            for piece in pieces
        ]
        + [
            whole_block(edges.shape),
            whole_block(place.shape),
            pl.BlockSpec(memory_space=pl.ANY),
        ],
        out_specs=whole_block(shape),
        out_shape=jax.ShapeDtypeStruct(shape, jnp.bfloat16),
        scratch_shapes=[
            pltpu.VMEM((BAND + 2 * REACH, channels, columns), jnp.bfloat16),
            pltpu.VMEM((BAND + 2 * REACH, channels, LANES), jnp.bfloat16),
        ],
        compiler_params=params(48),
        cost_estimate=pl.CostEstimate(
            flops=60 * channels * BAND * columns,
            bytes_accessed=4 * channels * BAND * columns,
            transcendentals=0,
        ),
        name="stencil",
    )(taps, *before[0], *rows[0], *after[0], edges, place, earlier)


def disco_kernel_grad(bi_ref, q_ref, gd_ref, stage, flat):
    columns = q_ref.shape[2]
    gd_ref[...] = jnp.zeros_like(gd_ref)
    rows_first(bi_ref, stage, flat, columns)

    def body(row, carry):
        cells = pl.ds(pl.multiple_of(row * columns, columns), columns)
        gd_ref[...] += mm_nt(flat[:, cells], q_ref[row])
        return carry

    lax.fori_loop(0, BAND, body, 0, unroll=4)


def disco_grad_call(band, block_input, q):
    channels, _, columns = block_input.shape
    return pl.pallas_call(
        disco_kernel_grad,
        grid=(1,),
        in_specs=[
            pl.BlockSpec((channels, BAND, columns), lambda i: (0, band, 0)),
            whole_block(q.shape),
        ],
        out_specs=whole_block((channels, channels)),
        out_shape=jax.ShapeDtypeStruct((channels, channels), jnp.float32),
        scratch_shapes=[
            pltpu.VMEM((columns // LANES, channels * BAND, LANES), jnp.float32),
            pltpu.VMEM((channels, BAND * columns), jnp.bfloat16),
        ],
        compiler_params=params(48),
        cost_estimate=pl.CostEstimate(
            flops=2 * channels * channels * BAND * columns,
            bytes_accessed=4 * channels * BAND * columns,
            transcendentals=0,
        ),
        name="disco_weight",
    )(block_input, q)


def legendre_kernel(leg, p0, t0, p1, t1, gain, _, __, s0, s1, stage, *, steps, block):
    order = pl.program_id(0)
    degrees = leg.shape[1]
    half = leg.shape[2] // 2
    total = None
    for band, refs in enumerate(((p0, t0), (p1, t1))):
        pair = jnp.concatenate([ref[...].reshape(half, LANES) for ref in refs], axis=1)
        term = mm(leg[0, :, band * half : (band + 1) * half], pair)
        total = term if total is None else total + term
    real = total[:, :LANES]
    imag = total[:, LANES:]
    owners, band = s0.shape[:2]
    shape = (owners, -1, LANES)
    s1[:, band + order] = jnp.concatenate(
        [real.reshape(shape), imag.reshape(shape)], axis=1
    ).astype(jnp.bfloat16)
    g = gain[:, 0, 0].reshape(degrees, LANES)
    k = gain[:, 0, 1].reshape(degrees, LANES)
    scaled = jnp.concatenate([g * real + k * imag, g * imag - k * real], axis=1).astype(
        jnp.bfloat16
    )
    synth = mm_tn(leg[0], scaled)
    for r in range(2):
        stage[pl.ds(r * steps + order, 2 * half, stride=block), :] = synth[
            :, r * LANES : (r + 1) * LANES
        ]

    @pl.when(order == steps - 1)
    def _():
        s0[...] = stage[: half * block].astype(jnp.bfloat16).reshape(s0.shape)
        s1[:, :band] = stage[half * block :].astype(jnp.bfloat16).reshape(s0.shape)


def legendre_call(leg, r0, r1, gain, earlier):
    owners, block, band, lanes = r0.shape
    degrees = leg.shape[1]
    steps = block // 2
    real = pl.BlockSpec((owners, None, band, lanes), lambda m: (0, m, 0, 0))
    imag = pl.BlockSpec((owners, None, band, lanes), lambda m: (0, m + steps, 0, 0))
    g_shape = (owners, 1, 2, degrees // owners, lanes)
    g_spec = pl.BlockSpec(g_shape, lambda m: (0, m, 0, 0, 0))
    out = (owners, band, block, lanes)
    more = (owners, band + steps + 1, block, lanes)
    return pl.pallas_call(
        functools.partial(legendre_kernel, steps=steps, block=block),
        grid=(steps,),
        in_specs=[
            pl.BlockSpec((1, degrees, leg.shape[2]), lambda m: (m, 0, 0)),
            real,
            imag,
            real,
            imag,
            g_spec,
        ]
        + [pl.BlockSpec(memory_space=pl.ANY)] * 2,
        out_specs=[whole_block(out), whole_block(more)],
        out_shape=[
            jax.ShapeDtypeStruct(out, jnp.bfloat16),
            jax.ShapeDtypeStruct(more, jnp.bfloat16),
        ],
        scratch_shapes=[pltpu.VMEM((2 * owners * band * block, lanes), jnp.float32)],
        compiler_params=params(48),
        cost_estimate=pl.CostEstimate(
            flops=8 * steps * degrees * leg.shape[2] * 256,
            bytes_accessed=7 * MIB,
            transcendentals=0,
        ),
        name="legendre",
    )(leg, r0, r0, r1, r1, gain, *earlier)


def pair_sum_kernel(kept, arrived, *rest):
    out = rest[-1]
    block = kept.shape[0] // out.shape[0]
    total = kept[...].astype(jnp.float32) + arrived[...].astype(jnp.float32)
    out[:, :block] = total.astype(jnp.bfloat16).reshape(-1, block, *kept.shape[1:])
    if out.shape[1] > block:
        total = rest[0][...].astype(jnp.float32) + rest[1][...].astype(jnp.float32)
        out[:, block:] = total.astype(jnp.bfloat16)


def pair_sum_call(owners, kept, arrived, more, earlier):
    orders, band, lanes = kept.shape
    extra = more[0].shape[1] if more else 0
    shape = (owners, orders // owners + extra, band, lanes)
    return pl.pallas_call(
        pair_sum_kernel,
        grid=(1,),
        in_specs=[whole_block(array.shape) for array in (kept, arrived, *more)]
        + [pl.BlockSpec(memory_space=pl.ANY)] * len(earlier),
        out_specs=whole_block(shape),
        out_shape=jax.ShapeDtypeStruct(shape, jnp.bfloat16),
        compiler_params=params(32),
        name="pair_sum",
    )(kept, arrived, *more, *earlier)


def share_kernel(kept, arrived, before, out):
    total = kept[...].astype(jnp.float32) + arrived[...].astype(jnp.float32)
    out[...] = total.astype(jnp.bfloat16).reshape(out.shape)


def share_call(kept, arrived, parcel):
    owners, blocks, band, lanes = parcel.shape
    return pl.pallas_call(
        share_kernel,
        grid=(1,),
        in_specs=[whole_block(kept.shape)] * 2 + [pl.BlockSpec(memory_space=pl.ANY)],
        out_specs=pl.BlockSpec((owners, 1, band, lanes), lambda i: (0, blocks - 1, 0, 0)),
        out_shape=jax.ShapeDtypeStruct(parcel.shape, jnp.bfloat16),
        input_output_aliases={2: 0},
        name="share",
    )(kept, arrived, parcel)


def split_kernel(parcel, shares, earlier, synth, owned, totals):
    band = synth.shape[1]
    degrees = owned.shape[1]
    synth[...] = parcel[:, :band]
    owned[...] = parcel[:, band : band + degrees].astype(jnp.float32)
    blocks = totals.shape[1] - 1
    first = shares[...].astype(jnp.float32).sum(axis=0).astype(jnp.bfloat16)
    last = parcel[:, band + degrees :].astype(jnp.float32).sum(axis=0).astype(jnp.bfloat16)
    totals[:, :blocks] = jnp.broadcast_to(first[None], (totals.shape[0],) + first.shape)
    totals[:, blocks:] = jnp.broadcast_to(last[None], (totals.shape[0],) + last.shape)


def split_call(count, degrees, parcel, shares, earlier):
    owners, blocks, band, lanes = parcel.shape
    more = shares.shape[1] - band
    shapes = (
        ((owners, band, band, lanes), jnp.bfloat16),
        ((owners, degrees, band, lanes), jnp.float32),
        ((count, more + 1, band, lanes), jnp.bfloat16),
    )
    return pl.pallas_call(
        split_kernel,
        grid=(1,),
        in_specs=[
            whole_block(parcel.shape),
            pl.BlockSpec((owners, more, band, lanes), lambda i: (0, band // more, 0, 0)),
            pl.BlockSpec(memory_space=pl.ANY),
        ],
        out_specs=[whole_block(shape) for shape, _ in shapes],
        out_shape=[jax.ShapeDtypeStruct(shape, kind) for shape, kind in shapes],
        compiler_params=params(32),
        name="split",
    )(parcel, shares, earlier)


def final_kernel(side, q_ref, own, other, table, wd, *rest):
    out_ref, stage = rest[-2:]
    width = q_ref.shape[2]
    orders = table.shape[0]
    channels = out_ref.shape[0]
    first = side[0] == 0

    def body(row, carry):
        mine = own[:, row].reshape(orders, LANES)
        theirs = other[:, row].reshape(orders, LANES)
        synth = jnp.concatenate(
            [jnp.where(first, mine, theirs), jnp.where(first, theirs, mine)], axis=1
        )
        out = mm_tn(synth, table[...]) + mm(wd[...], q_ref[row])
        for tile in range(width // LANES):
            stage[tile, pl.ds(row, channels, stride=BAND), :] = out[
                :, tile * LANES : (tile + 1) * LANES
            ]
        return carry

    lax.fori_loop(0, BAND, body, 0, unroll=2)
    for tile in range(width // LANES):
        out_ref[:, :, tile * LANES : (tile + 1) * LANES] = (
            stage[tile].astype(jnp.bfloat16).reshape(channels, BAND, LANES)
        )


def final_call(band, rows, side, q, own, other, table, wd, previous):
    _, channels, columns = q.shape
    width = 2 * LANES
    cells = BAND * columns
    extra = [] if previous is None else [previous]
    return pl.pallas_call(
        final_kernel,
        grid=(columns // width,),
        in_specs=[
            pl.BlockSpec(memory_space=pltpu.SMEM),
            pl.BlockSpec((BAND, channels, width), lambda i: (0, 0, i)),
            whole_block(other.shape),
            whole_block(other.shape),
            pl.BlockSpec((table.shape[0], width), lambda i: (0, i)),
            whole_block(wd.shape),
        ]
        + [pl.BlockSpec(memory_space=pl.ANY)] * len(extra),
        out_specs=pl.BlockSpec((channels, BAND, width), lambda i: (0, band, i)),
        out_shape=jax.ShapeDtypeStruct((channels, rows, columns), jnp.bfloat16),
        scratch_shapes=[pltpu.VMEM((width // LANES, channels * BAND, LANES), jnp.float32)],
        input_output_aliases={6: 0} if extra else {},
        compiler_params=params(48),
        cost_estimate=pl.CostEstimate(
            flops=2 * cells * channels * (channels + table.shape[0]),
            bytes_accessed=5 * channels * cells,
            transcendentals=0,
        ),
        name="final",
    )(side, q, own, other, table, wd, *extra)


def gain_kernel(gain, out, *, degrees):
    for degree in range(degrees):
        for r in range(2):
            part = gain[pl.ds(degree * 2 * LANES + r, LANES, stride=2), :]
            out[pl.ds(r * degrees + degree, LANES, stride=2 * degrees), :] = part.T


def gain_call(gain):
    degrees, channels, _, orders = gain.shape
    flat = gain.reshape(degrees * channels * 2, orders)
    return pl.pallas_call(
        functools.partial(gain_kernel, degrees=degrees),
        out_shape=jax.ShapeDtypeStruct((orders * 2 * degrees, channels), jnp.float32),
        name="gain",
    )(flat)


def grad_gain_kernel(owned, saved, out, *, degrees):
    for degree in range(degrees):
        real = owned[pl.ds(degree, LANES, stride=2 * degrees), :].T
        imag = owned[pl.ds(degrees + degree, LANES, stride=2 * degrees), :].T
        start = degree * 2 * LANES
        s = saved[pl.ds(start, LANES, stride=2), :]
        t = saved[pl.ds(start + 1, LANES, stride=2), :]
        out[pl.ds(start, LANES, stride=2), :] = real * s + imag * t
        out[pl.ds(start + 1, LANES, stride=2), :] = imag * s - real * t


def grad_gain_call(owned, saved):
    degrees, channels, _, orders = saved.shape
    flat = saved.reshape(degrees * channels * 2, orders)
    out = pl.pallas_call(
        functools.partial(grad_gain_kernel, degrees=degrees),
        out_shape=jax.ShapeDtypeStruct(flat.shape, jnp.float32),
        name="grad_gain",
    )(owned, flat)
    return out.reshape(saved.shape)


def legendre_whole():
    upper, lower, diagonal_log = legendre_tables()
    theta = (np.arange(NLAT) + 0.5) * (math.pi / NLAT)
    sine, cosine = np.sin(theta)[None], np.cos(theta)[None]
    orders = np.arange(M)
    start = np.exp(diagonal_log[:, None] + orders[:, None] * np.log(sine))
    table = np.zeros((M, L, NLAT))
    previous = before = np.zeros((M, NLAT))
    for degree in range(L):
        fresh = np.where(
            (orders == degree)[:, None],
            start,
            upper[degree][:, None] * (cosine * previous - lower[degree][:, None] * before),
        )
        table[:, degree] = fresh
        previous, before = fresh, previous
    return table * np.sqrt(sine * (math.pi / NLAT))[None]


def host_tables(lat_count, lon_count):
    columns, rows, own = NLON // lon_count, NLAT // lat_count, M // lat_count
    angle = (np.arange(M)[:, None] * np.arange(NLON)[None, :] % NLON) * (2.0 * math.pi / NLON)
    waves = np.stack([np.cos(angle), -np.sin(angle)]) / math.sqrt(NLON)
    factor = np.where(np.arange(M) == 0, 1.0, 2.0)[None, :, None]

    def arrange(table):
        table = table.reshape(2, lat_count, own, lon_count, columns)
        return table.transpose(3, 1, 0, 2, 4).reshape(lon_count, 2 * M, columns)

    pick = np.zeros((lon_count, 16, columns))
    for row, column in enumerate((0, 1, columns - 2, columns - 1)):
        pick[:, row, column] = 1.0
    forward = np.concatenate([arrange(waves * factor), pick], axis=1)
    legendre = legendre_whole().reshape(M, L, lat_count, rows // BAND, BAND)
    legendre = legendre.transpose(0, 1, 3, 2, 4).reshape(M, L, NLAT)
    kind = jnp.bfloat16
    return forward.astype(kind), arrange(waves).astype(kind), legendre.astype(kind)


def shards_banded(
    cotangent,
    block_input,
    filtered,
    spectral_saved,
    spectral_gain,
    w_in,
    w_out,
    w_disco,
    quad_weights,
    lat_offsets,
    lon_offsets,
    weight_index,
):
    channels, rows, columns = cotangent.shape
    lat_count = lax.axis_size("lat")
    lon_count = lax.axis_size("lon")
    lat_index = lax.axis_index("lat")
    lon_index = lax.axis_index("lon")
    own = M // lat_count
    degrees = L // lat_count
    side = lon_index.reshape(1).astype(jnp.int32)
    forward, inverse, legendre = host_tables(lat_count, lon_count)
    forward = lax.dynamic_index_in_dim(jnp.asarray(forward), lon_index, 0, keepdims=False)
    inverse = lax.dynamic_index_in_dim(jnp.asarray(inverse), lon_index, 0, keepdims=False)
    legendre = lax.dynamic_slice_in_dim(jnp.asarray(legendre), lat_index * own, own, 0)
    swap = [(i, (i + 1) % lon_count) for i in range(lon_count)]
    exchange = functools.partial(lax.all_to_all, axis_name="lat", split_axis=0, concat_axis=0, tiled=True)

    kernel = disco_kernel(quad_weights, lat_offsets, lon_offsets, weight_index)
    kernel_pad = jnp.pad(kernel, ((REACH, REACH), (0, 0), (0, 0)))
    kernel_rim = lax.dynamic_slice_in_dim(kernel_pad, lat_index * rows, rows + 2 * REACH, 0)
    taps = kernel_rim.reshape(-1)
    place = np.zeros((16, LANES), np.float32)
    for row, lane in enumerate((0, 1, LANES - 2, LANES - 1)):
        place[row, lane] = 1.0
    place = jnp.asarray(place, jnp.bfloat16)
    w_in_t = w_in.T

    down = [(i, (i + 1) % lat_count) for i in range(lat_count)]
    up = [(target, source) for source, target in down]

    def across(moves):
        return [
            (a * lon_count + i, b * lon_count + j) for a, b in moves for i, j in swap
        ]

    def dealt(array):
        blocks = array.astype(jnp.bfloat16).reshape(lat_count, lon_count, -1, BAND, LANES)
        half = functools.partial(lax.dynamic_index_in_dim, blocks, axis=1, keepdims=False)
        return half(lon_index), lax.ppermute(half(1 - lon_index), "lon", swap)

    gain = gain_call(spectral_gain).reshape(lat_count, own, 2, degrees, LANES)
    gf0, kept0, sent0, ends0, head, gin0, gout0 = mlp_call(
        0, (0, columns), side, filtered, cotangent, w_in_t, w_in, w_out, (), forward, gain
    )
    gain = exchange(gain)
    arrived0 = lax.ppermute(sent0, "lon", swap)
    bottom = lax.ppermute(head, "lat", up)
    sides0 = lax.ppermute(ends0, "lon", swap)
    bottom_side = lax.ppermute(ends0[:REACH], ("lat", "lon"), across(up))
    middle = columns // 2
    left1, gin1, gout1 = mlp_call(
        1, (0, middle), side, filtered, cotangent, w_in_t, w_in, w_out, (), forward, gain
    )
    sum0 = pair_sum_call(lat_count, kept0, arrived0, (), (bottom, bottom_side, sides0, gin1))
    received0 = exchange(sum0)
    right1, kept1, sent1, ends1, tail, gin2, gout2 = mlp_call(
        1, (middle, columns), side, filtered, cotangent, w_in_t, w_in, w_out, (left1,), forward, sum0
    )
    gf1 = (left1, right1)
    sides1 = lax.ppermute(ends1, "lon", swap)
    top = lax.ppermute(tail, "lat", down)
    top_side = lax.ppermute(ends1[BAND - REACH :], ("lat", "lon"), across(down))
    arrived1 = lax.ppermute(sent1, "lon", swap)
    half = w_in.shape[1] // 2
    gin = gin0 + gin1 + gin2
    weights = jnp.concatenate([gin[:, :half], gin[:, half:], gout0 + gout1 + gout2], axis=0)
    edges1 = jnp.concatenate([sides0[BAND - REACH :], sides1, bottom_side], axis=0)
    q1 = stencil_call(
        1, taps, ((gf0,), BAND // REACH - 1), (gf1, 0), ((bottom,), 0), edges1, place, received0
    )
    received1 = exchange(
        pair_sum_call(lat_count, kept1, arrived1, dealt(weights), (q1, top, top_side))
    )
    edges0 = jnp.concatenate([top_side, sides0, sides1[:REACH]], axis=0)
    q0 = stencil_call(0, taps, ((top,), 0), ((gf0,), 0), (gf1, 0), edges0, place, q1)
    disco1 = disco_grad_call(1, block_input, q1)
    disco0 = disco_grad_call(0, block_input, q0)
    s0, s1 = legendre_call(legendre, received0, received1, gain, (q0, disco1))
    local0 = exchange(s0)
    other0 = lax.ppermute(local0, "lon", swap)
    parcel = exchange(share_call(*dealt(disco0 + disco1), s1))
    result = final_call(0, rows, side, q0, local0, other0, inverse, w_disco, None)
    count = lat_count * lon_count
    synth1, owned, totals = split_call(count, degrees, parcel, received1, result)
    other1 = lax.ppermute(synth1, "lon", swap)
    totals = lax.all_to_all(totals, ("lat", "lon"), split_axis=0, concat_axis=0, tiled=True)
    grad_gain = grad_gain_call(owned.reshape(M * 2 * degrees, LANES), spectral_saved)
    result = final_call(1, rows, side, q1, synth1, other1, inverse, w_disco, result)
    totals = totals.astype(jnp.float32)
    total_disco = totals[:, -1].reshape(channels, channels)
    totals = totals[:, :-1].reshape(-1, channels)
    total_in = jnp.concatenate([totals[:channels], totals[channels : 2 * channels]], axis=1)
    total_out = totals[2 * channels :]
    scale = 1.0 / math.sqrt(NLAT * NLON)
    return (result, grad_gain, total_in * scale, total_out * scale, total_disco * scale)


def shards(*arrays):
    channels, rows, columns = arrays[0].shape
    lat_count = lax.axis_size("lat")
    lon_count = lax.axis_size("lon")
    fits = (
        rows == 2 * BAND
        and lon_count == 2
        and channels == lon_count * LANES
        and columns % (2 * LANES) == 0
        and M == LANES
        and M // lat_count == 8
        and L // lat_count == 8
    )
    return shards_banded(*arrays) if fits else shards_general(*arrays)


def solution(mesh):
    placed = (
        P(None, "lat", "lon"),
        P(None, "lat", "lon"),
        P(None, "lat", "lon"),
        P("lat", "lon", None, None),
        P("lat", "lon", None, None),
        P(),
        P(),
        P(),
        P(),
        P(),
        P(),
        P(),
    )
    return jax.shard_map(
        shards,
        mesh=mesh,
        in_specs=placed,
        out_specs=(P(None, "lat", "lon"), P("lat", "lon", None, None), P(), P(), P()),
        check_vma=False,
    )
```

```python
import functools
import math

import jax
import jax.numpy as jnp
import numpy as np
from jax import lax
from jax.experimental import pallas as pl
from jax.experimental.pallas import tpu as pltpu
from jax.sharding import PartitionSpec as P

NLAT = 512
NLON = 1024
L = 128
M = 128
REACH = 2
NQ = 64


root_half = 0.7071067811865476
root_two_pi = 2.5066282746310002


def padded_2(block, sides, width):
    for axis, dim in sides:
        count = lax.axis_size(axis)
        forward = [(i, i + 1) for i in range(count - 1)]
        forward.append((count - 1, 0))
        backward = [(target, source) for source, target in forward]
        low = lax.ppermute(
            lax.slice_in_dim(block, block.shape[dim] - width, None, axis=dim), axis, forward
        )
        high = lax.ppermute(lax.slice_in_dim(block, 0, width, axis=dim), axis, backward)
        block = jnp.concatenate([low, block, high], axis=dim)
    return block


def gelu_value(value):
    return value * 0.5 * (1.0 + lax.erf(value * root_half))


def gelu_slope(value):
    return (
        0.5 * (1.0 + lax.erf(value * root_half))
        + value * jnp.exp(-0.5 * value * value) / root_two_pi
    )


def legendre_tables():
    degree = np.arange(L)[:, None] * 1.0
    order = np.arange(M)[None, :] * 1.0
    upper = np.where(
        degree > order,
        np.sqrt(
            np.maximum(4.0 * degree * degree - 1.0, 0.0)
            / np.maximum(degree * degree - order * order, 1.0)
        ),
        0.0,
    )
    lower = np.where(
        degree > order + 1.0,
        np.sqrt(
            np.maximum((degree - 1.0) ** 2 - order * order, 0.0)
            / np.maximum(4.0 * (degree - 1.0) ** 2 - 1.0, 1.0)
        ),
        0.0,
    )
    counter = np.arange(1, M) * 1.0
    diagonal_log = np.concatenate(
        [np.zeros(1), np.cumsum(0.5 * np.log((2.0 * counter + 1.0) / (2.0 * counter)))]
    ) - 0.5 * np.log(2.0)
    return (upper, lower, diagonal_log)


def legendre_rows(theta):
    upper, lower, diagonal_log = legendre_tables()
    float_type = theta.dtype
    cosine = jnp.cos(theta)[:, None]
    sine = jnp.sin(theta)
    orders = jnp.arange(M, dtype=jnp.int32)
    start_value = jnp.exp(
        jnp.asarray(diagonal_log, float_type)[None, :]
        + orders.astype(float_type)[None, :] * jnp.log(sine)[:, None]
    )

    def advance(carry, inputs):
        previous, before = carry
        degree, coef_up, coef_low = inputs
        fresh = jnp.where(
            (orders == degree)[None, :],
            start_value,
            coef_up[None, :] * (cosine * previous - coef_low[None, :] * before),
        )
        return ((fresh, previous), fresh)

    empty = jnp.zeros_like(start_value)
    final, table = lax.scan(
        advance,
        (empty, empty),
        (
            jnp.arange(L, dtype=jnp.int32),
            jnp.asarray(upper, float_type),
            jnp.asarray(lower, float_type),
        ),
    )
    weight = jnp.sqrt(sine * (math.pi / NLAT))
    return table * weight[None, :, None]


def forward_table():
    column = jnp.arange(NLON, dtype=jnp.int32)[:, None]
    order = jnp.arange(M, dtype=jnp.int32)[None, :]
    angle = (column * order % NLON).astype(jnp.float32) * (2.0 * math.pi / NLON)
    factor = jnp.where(order == 0, 1.0, 2.0).astype(jnp.float32) / math.sqrt(NLON)
    return jnp.concatenate([factor * jnp.cos(angle), -factor * jnp.sin(angle)], axis=1).astype(
        jnp.bfloat16
    )


def inverse_table():
    order = jnp.arange(M, dtype=jnp.int32)[:, None]
    column = jnp.arange(NLON, dtype=jnp.int32)[None, :]
    angle = (column * order % NLON).astype(jnp.float32) * (2.0 * math.pi / NLON)
    return (jnp.concatenate([jnp.cos(angle), -jnp.sin(angle)], axis=0) / math.sqrt(NLON)).astype(
        jnp.bfloat16
    )


def disco_kernel(quad_weights, lat_offsets, lon_offsets, weight_index):
    span = jnp.arange(-REACH, REACH + 1, dtype=jnp.int32)
    slots = jnp.arange(NQ, dtype=jnp.int32)
    values = jnp.sum(
        jnp.where(
            weight_index[:, :, None] == slots[None, None, :], quad_weights[None, None, :], 0.0
        ),
        axis=2,
    )
    north = (lat_offsets[:, :, None] == span[None, None, :]).astype(quad_weights.dtype)
    east = (lon_offsets[:, :, None] == span[None, None, :]).astype(quad_weights.dtype)
    return jnp.sum(values[:, :, None, None] * north[:, :, :, None] * east[:, :, None, :], axis=1)


def disco_apply(padded, kernel):
    height = kernel.shape[0]
    width = padded.shape[2] - 2 * REACH
    total = jnp.zeros((padded.shape[0], height, width), kernel.dtype)
    for north in range(2 * REACH + 1):
        for east in range(2 * REACH + 1):
            total = (
                total
                + kernel[None, :, north, east, None]
                * padded[:, north : north + height, east : east + width]
            )
    return total


def disco_adjoint(padded, kernel_rim):
    height = kernel_rim.shape[0] - 2 * REACH
    width = padded.shape[2] - 2 * REACH
    total = jnp.zeros((padded.shape[0], height, width), kernel_rim.dtype)
    for north in range(2 * REACH + 1):
        for east in range(2 * REACH + 1):
            row_shift = 2 * REACH - north
            col_shift = 2 * REACH - east
            total = (
                total
                + kernel_rim[None, row_shift : row_shift + height, north, east, None]
                * padded[:, row_shift : row_shift + height, col_shift : col_shift + width]
            )
    return total


def inside_rows(padded, first_row):
    height = padded.shape[1]
    latitude = first_row - REACH + jnp.arange(height, dtype=jnp.int32)
    keep = (latitude >= 0) & (latitude < NLAT)
    return jnp.where(keep[None, :, None], padded, jnp.zeros((), padded.dtype))


def shards_general(
    cotangent,
    block_input,
    filtered,
    spectral_saved,
    spectral_gain,
    w_in,
    w_out,
    w_disco,
    quad_weights,
    lat_offsets,
    lon_offsets,
    weight_index,
):
    channels, rows, columns = cotangent.shape
    lat_count = lax.axis_size("lat")
    first_row = lax.axis_index("lat") * rows
    cells = rows * columns
    flat_in = filtered.reshape(channels, cells)
    flat_cot = cotangent.reshape(channels, cells)
    hidden_pre = lax.dot_general(
        w_in, flat_in, (((0,), (0,)), ((), ())), preferred_element_type=jnp.float32
    )
    activation = gelu_value(hidden_pre).astype(jnp.bfloat16)
    grad_act = jnp.dot(w_out, flat_cot, preferred_element_type=jnp.float32)
    grad_pre = (grad_act * gelu_slope(hidden_pre)).astype(jnp.bfloat16)
    grad_in_part = lax.dot_general(
        flat_in, grad_pre, (((1,), (1,)), ((), ())), preferred_element_type=jnp.float32
    )
    grad_out_part = lax.dot_general(
        activation, flat_cot, (((1,), (1,)), ((), ())), preferred_element_type=jnp.float32
    )
    grad_flat = jnp.dot(w_in, grad_pre, preferred_element_type=jnp.float32).astype(jnp.bfloat16)
    grad_filtered = grad_flat.reshape(channels, rows, columns)
    spread = lax.all_to_all(grad_filtered, "lon", split_axis=0, concat_axis=2, tiled=True)
    local_channels = spread.shape[0]
    coeffs = (
        jnp.dot(
            spread.reshape(local_channels * rows, NLON),
            forward_table(),
            preferred_element_type=jnp.float32,
        )
        .astype(jnp.bfloat16)
        .reshape(local_channels, rows, 2, M)
    )
    theta_rows = ((first_row + jnp.arange(rows, dtype=jnp.int32)).astype(jnp.float32) + 0.5) * (
        math.pi / NLAT
    )
    legendre = legendre_rows(theta_rows).astype(jnp.bfloat16)
    owned_count = L // lat_count
    weights = lax.slice_in_dim(legendre, 0, owned_count * lax.axis_size("lat"), axis=0)
    owned = lax.psum_scatter(
        jnp.einsum("ljm,cjrm->lcrm", weights, coeffs, preferred_element_type=jnp.float32),
        "lat",
        scatter_dimension=0,
        tiled=True,
    )
    real_part = owned[:, :, 0]
    imag_part = owned[:, :, 1]
    grad_gain = jnp.stack(
        [
            real_part * spectral_saved[:, :, 0] + imag_part * spectral_saved[:, :, 1],
            imag_part * spectral_saved[:, :, 0] - real_part * spectral_saved[:, :, 1],
        ],
        axis=2,
    )
    scaled = jnp.stack(
        [
            spectral_gain[:, :, 0] * real_part + spectral_gain[:, :, 1] * imag_part,
            spectral_gain[:, :, 0] * imag_part - spectral_gain[:, :, 1] * real_part,
        ],
        axis=2,
    ).astype(jnp.bfloat16)
    piece = lax.all_gather(scaled, "lat", axis=0, tiled=True)
    weights = lax.slice_in_dim(legendre, 0, piece.shape[0], axis=0)
    synthesis = (
        jnp.zeros((local_channels, rows, 2, M), jnp.float32)
        + jnp.einsum("ljm,lcrm->cjrm", weights, piece, preferred_element_type=jnp.float32)
    ).astype(jnp.bfloat16)
    grid_rows = jnp.dot(
        synthesis.reshape(local_channels * rows, 2 * M),
        inverse_table(),
        preferred_element_type=jnp.float32,
    ).reshape(local_channels, rows, NLON)
    spectral_grad = lax.all_to_all(grid_rows, "lon", split_axis=2, concat_axis=0, tiled=True)
    kernel = disco_kernel(quad_weights, lat_offsets, lon_offsets, weight_index)
    kernel_pad = jnp.pad(kernel, ((REACH, REACH), (0, 0), (0, 0)))
    kernel_rim = lax.dynamic_slice_in_dim(kernel_pad, first_row, rows + 2 * REACH, 0)
    stacked_rims = padded_2(
        jnp.stack((block_input, grad_filtered)), (("lat", 2), ("lon", 3)), REACH
    )
    input_pad = inside_rows(stacked_rims[0], first_row)
    grad_source = inside_rows(stacked_rims[1], first_row)
    grad_pad = lax.dot_general(
        w_disco, grad_source, (((1,), (0,)), ((), ())), preferred_element_type=jnp.float32
    ).astype(jnp.bfloat16)
    mixed = disco_apply(input_pad, kernel_rim[REACH : REACH + rows]).astype(jnp.bfloat16)
    grad_disco_part = lax.dot_general(
        mixed.reshape(channels, cells),
        grad_flat,
        (((1,), (1,)), ((), ())),
        preferred_element_type=jnp.float32,
    )
    disco_grad = disco_adjoint(grad_pad, kernel_rim)
    grad_input = (spectral_grad + disco_grad).astype(jnp.bfloat16)
    total_in, total_out, total_disco = lax.psum(
        (grad_in_part, grad_out_part, grad_disco_part), ("lat", "lon")
    )
    scale = 1.0 / math.sqrt(NLAT * NLON)
    return (grad_input, grad_gain, total_in * scale, total_out * scale, total_disco * scale)


BAND = 16
LANES = 128
MIB = 1024 * 1024
MLP_CHUNK = 512


def mm(a, b):
    return jnp.dot(a, b, preferred_element_type=jnp.float32)


def mm_nt(a, b):
    return lax.dot_general(a, b, (((1,), (1,)), ((), ())), preferred_element_type=jnp.float32)


def mm_tn(a, b):
    return lax.dot_general(a, b, (((0,), (0,)), ((), ())), preferred_element_type=jnp.float32)


def params(mib):
    return pltpu.CompilerParams(vmem_limit_bytes=mib * MIB)


def whole_block(shape):
    return pl.BlockSpec(shape, lambda *_: (0,) * len(shape))


def rows_first(block, stage, flat, width):
    channels = block.shape[0]
    for tile in range(width // LANES):
        stage[tile] = (
            block[:, :, tile * LANES : (tile + 1) * LANES]
            .astype(jnp.float32)
            .reshape(channels * BAND, LANES)
        )
    for row in range(BAND):
        for tile in range(width // LANES):
            start = row * width + tile * LANES
            flat[:, start : start + LANES] = stage[
                tile, pl.ds(row, channels, stride=BAND), :
            ].astype(jnp.bfloat16)


def gelu_both(value):
    decay = jnp.exp(value * value * -0.5)
    base = 1.0 + (0.3275911 * root_half) * jnp.abs(value)
    inverse = pl.reciprocal(base, approx=True)
    inverse = inverse * (2.0 - base * inverse)
    poly = 0.5 * 1.061405429
    for term in (-1.453152027, 1.421413741, -0.284496736, 0.254829592):
        poly = poly * inverse + 0.5 * term
    tail = poly * inverse * decay
    chance = jnp.where(value >= 0.0, 1.0 - tail, tail)
    return chance, decay


def mlp_kernel(
    side, x_ref, ct_ref, win_t, win, wout, *rest,
    steps, width, chunk, halo, pieces, prior, final,
):
    sums = rest[:prior]
    rest = rest[prior:]
    left = rest[: max(pieces - 1, 0)]
    table = rest[len(left)] if pieces else None
    gf_ref, *rest = rest[pieces + 1 :]
    if pieces:
        own_ref, send_ref, edge_ref, halo_ref, *rest = rest
    if final:
        weights_ref, *rest = rest
    gin_ref, gout_ref, stage, xs, cs, *rest = rest
    if pieces:
        low, high = rest
    step = pl.program_id(0)

    @pl.when(step == 0)
    def _():
        gin_ref[...] = sums[0][...] if prior else jnp.zeros_like(gin_ref)
        gout_ref[...] = sums[1][...] if prior else jnp.zeros_like(gout_ref)

    rows_first(x_ref, stage, xs, width)
    rows_first(ct_ref, stage, cs, width)
    column = pl.multiple_of(step * width, width)
    per = chunk // width

    def body(index, carry):
        cells = pl.ds(pl.multiple_of(index * chunk, chunk), chunk)
        x = xs[:, cells]
        c = cs[:, cells]
        pre = mm(win_t[...], x)
        grad = mm(wout[...], c)
        chance, decay = gelu_both(pre)
        act = (pre * chance).astype(jnp.bfloat16)
        gp = (grad * (chance + pre * decay * (1.0 / root_two_pi))).astype(jnp.bfloat16)
        gf = mm(win[...], gp).astype(jnp.bfloat16)
        for part in range(per):
            gf_ref[index * per + part, :, pl.ds(column, width)] = gf[
                :, part * width : (part + 1) * width
            ]
        gin_ref[...] += mm_nt(x, gp)
        gout_ref[...] += mm_nt(act, c)
        return carry

    lax.fori_loop(0, BAND * width // chunk, body, 0, unroll=2)
    if not pieces:
        return

    @pl.when(step == steps - 1)
    def _():
        parts = [*left, gf_ref]
        spans = []
        for ref in parts:
            start = spans[-1][1] if spans else 0
            spans.append((start, start + ref.shape[2]))
        for ref, (start, stop) in zip(parts, spans):
            halo_ref[:, :, start:stop] = ref[halo : halo + REACH]
        orders = low.shape[0] // BAND

        def transform(row, carry):
            out = None
            for ref, (start, stop) in zip(parts, spans):
                term = mm_nt(table[:, start:stop], ref[row])
                out = term if out is None else out + term
            low[pl.ds(row, orders, stride=BAND), :] = out[:orders, :LANES]
            high[pl.ds(row, orders, stride=BAND), :] = out[:orders, LANES:]
            edge_ref[row] = out[orders:].astype(jnp.bfloat16)
            return carry

        lax.fori_loop(0, BAND, transform, 0, unroll=2)
        first = side[0] == 0
        shape = own_ref.shape

        @pl.when(first)
        def _():
            own_ref[...] = low[...].astype(jnp.bfloat16).reshape(shape)
            send_ref[...] = high[...].astype(jnp.bfloat16).reshape(shape)

        @pl.when(jnp.logical_not(first))
        def _():
            own_ref[...] = high[...].astype(jnp.bfloat16).reshape(shape)
            send_ref[...] = low[...].astype(jnp.bfloat16).reshape(shape)

        if final:
            start = 0
            for ref in (gin_ref, gout_ref):
                count, lanes = ref.shape
                for lane in range(0, lanes, LANES):
                    weights_ref[start : start + count] = ref[:, lane : lane + LANES].astype(
                        jnp.bfloat16
                    )
                    start += count


def mlp_call(
    band, span, side, filtered, cotangent, win_t, win, wout, sums, left, table, earlier, final=False
):
    channels, rows, columns = filtered.shape
    hidden = wout.shape[0]
    width = LANES
    offset = span[0] // width
    steps = (span[1] - span[0]) // width
    chunk = MLP_CHUNK
    orders = table.shape[0] - 16
    last = span[1] == columns
    pieces = len(left) + 1 if last else 0
    block = pl.BlockSpec((channels, BAND, width), lambda i: (0, band, offset + i))
    cells = BAND * (span[1] - span[0])
    outs = [((BAND, channels, span[1] - span[0]), jnp.bfloat16)]
    if last:
        outs += [
            ((orders, BAND, LANES), jnp.bfloat16),
            ((orders, BAND, LANES), jnp.bfloat16),
            ((BAND, 16, channels), jnp.bfloat16),
            ((REACH, channels, columns), jnp.bfloat16),
        ]
    grads = [((channels, hidden), jnp.float32), ((hidden, channels), jnp.float32)]
    held = [pltpu.VMEM(shape, kind) for shape, kind in grads] if final else []
    outs += [((2 * channels * hidden // LANES, LANES), jnp.bfloat16)] if final else grads
    tables = [*sums, *left, table] if last else list(sums)
    return pl.pallas_call(
        functools.partial(
            mlp_kernel,
            steps=steps,
            width=width,
            chunk=chunk,
            halo=band * (BAND - REACH),
            pieces=pieces,
            prior=len(sums),
            final=final,
        ),
        grid=(steps,),
        in_specs=[
            pl.BlockSpec(memory_space=pltpu.SMEM),
            block,
            block,
            whole_block(win_t.shape),
            whole_block(win.shape),
            whole_block(wout.shape),
        ]
        + [whole_block(array.shape) for array in tables]
        + [pl.BlockSpec(memory_space=pl.ANY)],
        out_specs=[whole_block(shape) for shape, _ in outs],
        out_shape=[jax.ShapeDtypeStruct(shape, kind) for shape, kind in outs],
        scratch_shapes=held
        + [
            pltpu.VMEM((width // LANES, channels * BAND, LANES), jnp.float32),
            pltpu.VMEM((channels, BAND * width), jnp.bfloat16),
            pltpu.VMEM((channels, BAND * width), jnp.bfloat16),
        ]
        + [pltpu.VMEM((orders * BAND, LANES), jnp.float32)] * (2 if last else 0),
        compiler_params=params(60),
        cost_estimate=pl.CostEstimate(
            flops=2 * cells * channels * (5 * hidden + orders),
            bytes_accessed=6 * channels * cells,
            transcendentals=2 * hidden * cells,
        ),
        name="mlp",
    )(side, filtered, cotangent, win_t, win, wout, *tables, earlier)


def stencil_kernel(taps, *rest, first, counts):
    edges, place, _, q_ref, field, rim = rest[sum(counts) :]
    channels, columns = field.shape[1:]
    pieces = iter(rest)
    low = 0
    for count, height in zip(counts, (REACH, BAND, REACH)):
        start = 0
        for _ in range(count):
            piece = next(pieces)
            stop = start + piece.shape[2]
            field[low : low + height, :, start:stop] = piece[...]
            start = stop
        low += height

    def spread(row, carry):
        rim[row] = mm_tn(edges[row], place[...]).astype(jnp.bfloat16)
        return carry

    lax.fori_loop(0, BAND + 2 * REACH, spread, 0, unroll=5)
    lane = lax.broadcasted_iota(jnp.int32, (16, LANES), 1)
    span = 2 * REACH + 1

    def row_body(row, carry):
        weights = {}
        for north in range(span):
            source = row + 2 * REACH - north
            for east in range(span):
                weights[north, east] = taps[((first + source) * span + north) * span + east].astype(
                    jnp.bfloat16
                )

        def tile_body(tile, inner):
            part = pl.ds(pl.multiple_of(tile * 16, 16), 16)
            sums = [None] * span
            for north in range(span):
                source = row + 2 * REACH - north
                here = field[source, part, :]
                ends = rim[source, part, :]
                for east in range(span):
                    past = east - REACH
                    shifted = here
                    if past < 0:
                        rim_tile = jnp.where(lane < -past, ends, here[:, :LANES])
                        shifted = jnp.concatenate([rim_tile, here[:, LANES:]], axis=1)
                    if past > 0:
                        rim_tile = jnp.where(lane >= LANES - past, ends, here[:, -LANES:])
                        shifted = jnp.concatenate([here[:, :-LANES], rim_tile], axis=1)
                    term = shifted * weights[north, east]
                    sums[east] = term if sums[east] is None else sums[east] + term
            total = sums[REACH].astype(jnp.float32)
            for east in range(span):
                if east != REACH:
                    moved = pltpu.roll(sums[east], (east - REACH) % columns, 1)
                    total = total + moved.astype(jnp.float32)
            q_ref[row, part, :] = total.astype(jnp.bfloat16)
            return inner

        return lax.fori_loop(0, channels // 16, tile_body, carry, unroll=4)

    lax.fori_loop(0, BAND, row_body, 0)


def stencil_call(band, taps, before, rows, after, edges, place, earlier):
    sources = (before, rows, after)
    channels = rows[0][0].shape[1]
    columns = sum(piece.shape[2] for piece in rows[0])
    shape = (BAND, channels, columns)

    def piece_spec(piece, height, index):
        return pl.BlockSpec((height, channels, piece.shape[2]), lambda i: (index, 0, 0))

    return pl.pallas_call(
        functools.partial(
            stencil_kernel, first=band * BAND, counts=[len(pieces) for pieces, _ in sources]
        ),
        grid=(1,),
        in_specs=[pl.BlockSpec(memory_space=pltpu.SMEM)]
        + [
            piece_spec(piece, height, index)
            for (pieces, index), height in zip(sources, (REACH, BAND, REACH))
            for piece in pieces
        ]
        + [
            whole_block(edges.shape),
            whole_block(place.shape),
            pl.BlockSpec(memory_space=pl.ANY),
        ],
        out_specs=whole_block(shape),
        out_shape=jax.ShapeDtypeStruct(shape, jnp.bfloat16),
        scratch_shapes=[
            pltpu.VMEM((BAND + 2 * REACH, channels, columns), jnp.bfloat16),
            pltpu.VMEM((BAND + 2 * REACH, channels, LANES), jnp.bfloat16),
        ],
        compiler_params=params(48),
        cost_estimate=pl.CostEstimate(
            flops=60 * channels * BAND * columns,
            bytes_accessed=4 * channels * BAND * columns,
            transcendentals=0,
        ),
        name="stencil",
    )(taps, *before[0], *rows[0], *after[0], edges, place, earlier)


def disco_kernel_grad(bi_ref, q_ref, gd_ref, stage, flat):
    columns = q_ref.shape[2]
    gd_ref[...] = jnp.zeros_like(gd_ref)
    rows_first(bi_ref, stage, flat, columns)

    def body(row, carry):
        cells = pl.ds(pl.multiple_of(row * columns, columns), columns)
        gd_ref[...] += mm_nt(flat[:, cells], q_ref[row])
        return carry

    lax.fori_loop(0, BAND, body, 0, unroll=4)


def disco_grad_call(band, block_input, q):
    channels, _, columns = block_input.shape
    return pl.pallas_call(
        disco_kernel_grad,
        grid=(1,),
        in_specs=[
            pl.BlockSpec((channels, BAND, columns), lambda i: (0, band, 0)),
            whole_block(q.shape),
        ],
        out_specs=whole_block((channels, channels)),
        out_shape=jax.ShapeDtypeStruct((channels, channels), jnp.float32),
        scratch_shapes=[
            pltpu.VMEM((columns // LANES, channels * BAND, LANES), jnp.float32),
            pltpu.VMEM((channels, BAND * columns), jnp.bfloat16),
        ],
        compiler_params=params(48),
        cost_estimate=pl.CostEstimate(
            flops=2 * channels * channels * BAND * columns,
            bytes_accessed=4 * channels * BAND * columns,
            transcendentals=0,
        ),
        name="disco_weight",
    )(block_input, q)


def legendre_kernel(leg, p0, t0, p1, t1, gain, _, __, s0, s1, s2, stage, *, steps, block):
    order = pl.program_id(0)
    degrees = leg.shape[1]
    half = leg.shape[2] // 2
    total = None
    for band, refs in enumerate(((p0, t0), (p1, t1))):
        pair = jnp.concatenate([ref[...].reshape(half, LANES) for ref in refs], axis=1)
        term = mm(leg[0, :, band * half : (band + 1) * half], pair)
        total = term if total is None else total + term
    real = total[:, :LANES]
    imag = total[:, LANES:]
    owners, band = s0.shape[:2]
    shape = (owners, -1, LANES)
    s2[:, order] = jnp.concatenate(
        [real.reshape(shape), imag.reshape(shape)], axis=1
    ).astype(jnp.bfloat16)
    g = gain[:, 0, 0].reshape(degrees, LANES)
    k = gain[:, 0, 1].reshape(degrees, LANES)
    scaled = jnp.concatenate([g * real + k * imag, g * imag - k * real], axis=1).astype(
        jnp.bfloat16
    )
    synth = mm_tn(leg[0], scaled)
    for r in range(2):
        stage[pl.ds(r * steps + order, 2 * half, stride=block), :] = synth[
            :, r * LANES : (r + 1) * LANES
        ]

    @pl.when(order == steps - 1)
    def _():
        s0[...] = stage[: half * block].astype(jnp.bfloat16).reshape(s0.shape)
        s1[:, :band] = stage[half * block :].astype(jnp.bfloat16).reshape(s0.shape)


def legendre_call(leg, r0, r1, gain, earlier):
    owners, block, band, lanes = r0.shape
    degrees = leg.shape[1]
    steps = block // 2
    real = pl.BlockSpec((owners, None, band, lanes), lambda m: (0, m, 0, 0))
    imag = pl.BlockSpec((owners, None, band, lanes), lambda m: (0, m + steps, 0, 0))
    g_shape = (owners, 1, 2, degrees // owners, lanes)
    g_spec = pl.BlockSpec(g_shape, lambda m: (0, m, 0, 0, 0))
    out = (owners, band, block, lanes)
    more = (owners, band + 1, block, lanes)
    owned = (owners, steps, block, lanes)
    return pl.pallas_call(
        functools.partial(legendre_kernel, steps=steps, block=block),
        grid=(steps,),
        in_specs=[
            pl.BlockSpec((1, degrees, leg.shape[2]), lambda m: (m, 0, 0)),
            real,
            imag,
            real,
            imag,
            g_spec,
        ]
        + [pl.BlockSpec(memory_space=pl.ANY)] * 2,
        out_specs=[whole_block(out), whole_block(more), whole_block(owned)],
        out_shape=[
            jax.ShapeDtypeStruct(out, jnp.bfloat16),
            jax.ShapeDtypeStruct(more, jnp.bfloat16),
            jax.ShapeDtypeStruct(owned, jnp.bfloat16),
        ],
        scratch_shapes=[pltpu.VMEM((2 * owners * band * block, lanes), jnp.float32)],
        compiler_params=params(48),
        cost_estimate=pl.CostEstimate(
            flops=8 * steps * degrees * leg.shape[2] * 256,
            bytes_accessed=7 * MIB,
            transcendentals=0,
        ),
        name="legendre",
    )(leg, r0, r0, r1, r1, gain, *earlier)


def pair_sum_kernel(kept, arrived, *rest):
    out, token = rest[-2:]
    token[...] = jnp.zeros_like(token)
    block = kept.shape[0] // out.shape[0]
    total = kept[...].astype(jnp.float32) + arrived[...].astype(jnp.float32)
    out[:, :block] = total.astype(jnp.bfloat16).reshape(-1, block, *kept.shape[1:])
    if out.shape[1] > block:
        total = rest[0][...].astype(jnp.float32) + rest[1][...].astype(jnp.float32)
        out[:, block:] = total.astype(jnp.bfloat16)


def pair_sum_call(owners, kept, arrived, more, earlier):
    orders, band, lanes = kept.shape
    extra = more[0].shape[1] if more else 0
    shape = (owners, orders // owners + extra, band, lanes)
    return pl.pallas_call(
        pair_sum_kernel,
        grid=(1,),
        in_specs=[whole_block(array.shape) for array in (kept, arrived, *more)]
        + [pl.BlockSpec(memory_space=pl.ANY)] * len(earlier),
        out_specs=[whole_block(shape), whole_block((8, lanes))],
        out_shape=[
            jax.ShapeDtypeStruct(shape, jnp.bfloat16),
            jax.ShapeDtypeStruct((8, lanes), jnp.float32),
        ],
        compiler_params=params(32),
        name="pair_sum",
    )(kept, arrived, *more, *earlier)


def share_kernel(kept, arrived, before, out):
    total = kept[...].astype(jnp.float32) + arrived[...].astype(jnp.float32)
    out[...] = total.astype(jnp.bfloat16).reshape(out.shape)


def share_call(kept, arrived, parcel):
    owners, blocks, band, lanes = parcel.shape
    return pl.pallas_call(
        share_kernel,
        grid=(1,),
        in_specs=[whole_block(kept.shape)] * 2 + [pl.BlockSpec(memory_space=pl.ANY)],
        out_specs=pl.BlockSpec((owners, 1, band, lanes), lambda i: (0, blocks - 1, 0, 0)),
        out_shape=jax.ShapeDtypeStruct(parcel.shape, jnp.bfloat16),
        input_output_aliases={2: 0},
        name="share",
    )(kept, arrived, parcel)


def split_kernel(parcel, shares, owned, earlier, synth, sent, totals):
    band = synth.shape[1]
    synth[...] = parcel[:, :band]
    sent[...] = owned[...]
    blocks = totals.shape[1] - 1
    first = shares[...].astype(jnp.float32).sum(axis=0).astype(jnp.bfloat16)
    last = parcel[:, band:].astype(jnp.float32).sum(axis=0).astype(jnp.bfloat16)
    totals[:, :blocks] = jnp.broadcast_to(first[None], (totals.shape[0],) + first.shape)
    totals[:, blocks:] = jnp.broadcast_to(last[None], (totals.shape[0],) + last.shape)


def split_call(count, parcel, shares, owned, earlier):
    owners, _, band, lanes = parcel.shape
    more = shares.shape[1] - band
    shapes = ((owners, band, band, lanes), owned.shape, (count, more + 1, band, lanes))
    return pl.pallas_call(
        split_kernel,
        grid=(1,),
        in_specs=[
            whole_block(parcel.shape),
            pl.BlockSpec((owners, more, band, lanes), lambda i: (0, band // more, 0, 0)),
            whole_block(owned.shape),
            pl.BlockSpec(memory_space=pl.ANY),
        ],
        out_specs=[whole_block(shape) for shape in shapes],
        out_shape=[jax.ShapeDtypeStruct(shape, jnp.bfloat16) for shape in shapes],
        compiler_params=params(32),
        name="split",
    )(parcel, shares, owned, earlier)


def final_kernel(side, q_ref, own, other, table, wd, *rest):
    out_ref, stage = rest[-2:]
    width = q_ref.shape[2]
    orders = table.shape[0]
    channels = out_ref.shape[0]
    first = side[0] == 0

    def body(row, carry):
        mine = own[:, row].reshape(orders, LANES)
        theirs = other[:, row].reshape(orders, LANES)
        synth = jnp.concatenate(
            [jnp.where(first, mine, theirs), jnp.where(first, theirs, mine)], axis=1
        )
        out = mm_tn(synth, table[...]) + mm(wd[...], q_ref[row])
        for tile in range(width // LANES):
            stage[tile, pl.ds(row, channels, stride=BAND), :] = out[
                :, tile * LANES : (tile + 1) * LANES
            ]
        return carry

    lax.fori_loop(0, BAND, body, 0, unroll=2)
    for tile in range(width // LANES):
        out_ref[:, :, tile * LANES : (tile + 1) * LANES] = (
            stage[tile].astype(jnp.bfloat16).reshape(channels, BAND, LANES)
        )


def final_call(band, rows, side, q, own, other, table, wd, previous):
    _, channels, columns = q.shape
    width = 2 * LANES
    cells = BAND * columns
    extra = [] if previous is None else [previous]
    return pl.pallas_call(
        final_kernel,
        grid=(columns // width,),
        in_specs=[
            pl.BlockSpec(memory_space=pltpu.SMEM),
            pl.BlockSpec((BAND, channels, width), lambda i: (0, 0, i)),
            whole_block(other.shape),
            whole_block(other.shape),
            pl.BlockSpec((table.shape[0], width), lambda i: (0, i)),
            whole_block(wd.shape),
        ]
        + [pl.BlockSpec(memory_space=pl.ANY)] * len(extra),
        out_specs=pl.BlockSpec((channels, BAND, width), lambda i: (0, band, i)),
        out_shape=jax.ShapeDtypeStruct((channels, rows, columns), jnp.bfloat16),
        scratch_shapes=[pltpu.VMEM((width // LANES, channels * BAND, LANES), jnp.float32)],
        input_output_aliases={6: 0} if extra else {},
        compiler_params=params(48),
        cost_estimate=pl.CostEstimate(
            flops=2 * cells * channels * (channels + table.shape[0]),
            bytes_accessed=5 * channels * cells,
            transcendentals=0,
        ),
        name="final",
    )(side, q, own, other, table, wd, *extra)


def gain_kernel(gain, out, *, degrees):
    for degree in range(degrees):
        for r in range(2):
            part = gain[pl.ds(degree * 2 * LANES + r, LANES, stride=2), :]
            out[pl.ds(r * degrees + degree, LANES, stride=2 * degrees), :] = part.T


def gain_call(gain):
    degrees, channels, _, orders = gain.shape
    flat = gain.reshape(degrees * channels * 2, orders)
    return pl.pallas_call(
        functools.partial(gain_kernel, degrees=degrees),
        out_shape=jax.ShapeDtypeStruct((orders * 2 * degrees, channels), jnp.float32),
        name="gain",
    )(flat)


def grad_gain_kernel(owned, saved, out, *, degrees):
    for degree in range(degrees):
        real = owned[pl.ds(degree, LANES, stride=2 * degrees), :].T
        imag = owned[pl.ds(degrees + degree, LANES, stride=2 * degrees), :].T
        start = degree * 2 * LANES
        s = saved[pl.ds(start, LANES, stride=2), :]
        t = saved[pl.ds(start + 1, LANES, stride=2), :]
        out[pl.ds(start, LANES, stride=2), :] = real * s + imag * t
        out[pl.ds(start + 1, LANES, stride=2), :] = imag * s - real * t


def grad_gain_call(owned, saved):
    degrees, channels, _, orders = saved.shape
    flat = saved.reshape(degrees * channels * 2, orders)
    out = pl.pallas_call(
        functools.partial(grad_gain_kernel, degrees=degrees),
        out_shape=jax.ShapeDtypeStruct(flat.shape, jnp.float32),
        name="grad_gain",
    )(owned, flat)
    return out.reshape(saved.shape)


def legendre_whole():
    upper, lower, diagonal_log = legendre_tables()
    theta = (np.arange(NLAT) + 0.5) * (math.pi / NLAT)
    sine, cosine = np.sin(theta)[None], np.cos(theta)[None]
    orders = np.arange(M)
    start = np.exp(diagonal_log[:, None] + orders[:, None] * np.log(sine))
    table = np.zeros((M, L, NLAT))
    previous = before = np.zeros((M, NLAT))
    for degree in range(L):
        fresh = np.where(
            (orders == degree)[:, None],
            start,
            upper[degree][:, None] * (cosine * previous - lower[degree][:, None] * before),
        )
        table[:, degree] = fresh
        previous, before = fresh, previous
    return table * np.sqrt(sine * (math.pi / NLAT))[None]


def host_tables(lat_count, lon_count):
    columns, rows, own = NLON // lon_count, NLAT // lat_count, M // lat_count
    angle = (np.arange(M)[:, None] * np.arange(NLON)[None, :] % NLON) * (2.0 * math.pi / NLON)
    waves = np.stack([np.cos(angle), -np.sin(angle)]) / math.sqrt(NLON)
    factor = np.where(np.arange(M) == 0, 1.0, 2.0)[None, :, None]

    def arrange(table):
        table = table.reshape(2, lat_count, own, lon_count, columns)
        return table.transpose(3, 1, 0, 2, 4).reshape(lon_count, 2 * M, columns)

    pick = np.zeros((lon_count, 16, columns))
    for row, column in enumerate((0, 1, columns - 2, columns - 1)):
        pick[:, row, column] = 1.0
    forward = np.concatenate([arrange(waves * factor), pick], axis=1)
    legendre = legendre_whole().reshape(M, L, lat_count, rows // BAND, BAND)
    legendre = legendre.transpose(0, 1, 3, 2, 4).reshape(M, L, NLAT)
    kind = jnp.bfloat16
    return forward.astype(kind), arrange(waves).astype(kind), legendre.astype(kind)


def shards_banded(
    cotangent,
    block_input,
    filtered,
    spectral_saved,
    spectral_gain,
    w_in,
    w_out,
    w_disco,
    quad_weights,
    lat_offsets,
    lon_offsets,
    weight_index,
):
    channels, rows, columns = cotangent.shape
    lat_count = lax.axis_size("lat")
    lon_count = lax.axis_size("lon")
    lat_index = lax.axis_index("lat")
    lon_index = lax.axis_index("lon")
    own = M // lat_count
    degrees = L // lat_count
    side = lon_index.reshape(1).astype(jnp.int32)
    forward, inverse, legendre = host_tables(lat_count, lon_count)
    forward = lax.dynamic_index_in_dim(jnp.asarray(forward), lon_index, 0, keepdims=False)
    inverse = lax.dynamic_index_in_dim(jnp.asarray(inverse), lon_index, 0, keepdims=False)
    legendre = lax.dynamic_slice_in_dim(jnp.asarray(legendre), lat_index * own, own, 0)
    swap = [(i, (i + 1) % lon_count) for i in range(lon_count)]
    exchange = functools.partial(lax.all_to_all, axis_name="lat", split_axis=0, concat_axis=0, tiled=True)

    kernel = disco_kernel(quad_weights, lat_offsets, lon_offsets, weight_index)
    kernel_pad = jnp.pad(kernel, ((REACH, REACH), (0, 0), (0, 0)))
    kernel_rim = lax.dynamic_slice_in_dim(kernel_pad, lat_index * rows, rows + 2 * REACH, 0)
    taps = kernel_rim.reshape(-1)
    place = np.zeros((16, LANES), np.float32)
    for row, lane in enumerate((0, 1, LANES - 2, LANES - 1)):
        place[row, lane] = 1.0
    place = jnp.asarray(place, jnp.bfloat16)
    w_in_t = w_in.T

    down = [(i, (i + 1) % lat_count) for i in range(lat_count)]
    up = [(target, source) for source, target in down]

    def across(moves):
        return [
            (a * lon_count + i, b * lon_count + j) for a, b in moves for i, j in swap
        ]

    def dealt(array):
        blocks = array.astype(jnp.bfloat16).reshape(lat_count, lon_count, -1, BAND, LANES)
        half = functools.partial(lax.dynamic_index_in_dim, blocks, axis=1, keepdims=False)
        return half(lon_index), lax.ppermute(half(1 - lon_index), "lon", swap)

    gain = gain_call(spectral_gain).reshape(lat_count, own, 2, degrees, LANES)
    gf0, kept0, sent0, ends0, head, gin0, gout0 = mlp_call(
        0, (0, columns), side, filtered, cotangent, w_in_t, w_in, w_out, (), (), forward, gain
    )
    gain = exchange(gain)
    arrived0 = lax.ppermute(sent0, "lon", swap)
    bottom = lax.ppermute(head, "lat", up)
    sides0 = lax.ppermute(ends0, "lon", swap)
    bottom_side = lax.ppermute(ends0[:REACH], ("lat", "lon"), across(up))
    middle = columns // 2
    left1, gin1, gout1 = mlp_call(
        1, (0, middle), side, filtered, cotangent, w_in_t, w_in, w_out, (gin0, gout0), (), forward, gain
    )
    sum0, token = pair_sum_call(lat_count, kept0, arrived0, (), (bottom,))
    received0 = exchange(sum0)
    right1, kept1, sent1, ends1, tail, weights = mlp_call(
        1, (middle, columns), side, filtered, cotangent, w_in_t, w_in, w_out, (gin1, gout1), (left1,),
        forward, token, final=True,
    )
    gf1 = (left1, right1)
    sides1 = lax.ppermute(ends1, "lon", swap)
    top = lax.ppermute(tail, "lat", down)
    top_side = lax.ppermute(ends1[BAND - REACH :], ("lat", "lon"), across(down))
    arrived1 = lax.ppermute(sent1, "lon", swap)
    edges1 = jnp.concatenate([sides0[BAND - REACH :], sides1, bottom_side], axis=0)
    q1 = stencil_call(
        1, taps, ((gf0,), BAND // REACH - 1), (gf1, 0), ((bottom,), 0), edges1, place, received0
    )
    sum1, _ = pair_sum_call(lat_count, kept1, arrived1, dealt(weights), (q1, top, top_side))
    received1 = exchange(sum1)
    edges0 = jnp.concatenate([top_side, sides0, sides1[:REACH]], axis=0)
    q0 = stencil_call(0, taps, ((top,), 0), ((gf0,), 0), (gf1, 0), edges0, place, q1)
    disco1 = disco_grad_call(1, block_input, q1)
    disco0 = disco_grad_call(0, block_input, q0)
    s0, s1, owned = legendre_call(legendre, received0, received1, gain, (q0, disco1))
    local0 = exchange(s0)
    other0 = lax.ppermute(local0, "lon", swap)
    parcel = exchange(share_call(*dealt(disco0 + disco1), s1))
    result = final_call(0, rows, side, q0, local0, other0, inverse, w_disco, None)
    count = lat_count * lon_count
    synth1, owned, totals = split_call(count, parcel, received1, owned, other0)
    other1 = lax.ppermute(synth1, "lon", swap)
    totals = lax.all_to_all(totals, ("lat", "lon"), split_axis=0, concat_axis=0, tiled=True)
    owned = exchange(owned).astype(jnp.float32).reshape(M * 2 * degrees, LANES)
    grad_gain = grad_gain_call(owned, spectral_saved)
    result = final_call(1, rows, side, q1, synth1, other1, inverse, w_disco, result)
    totals = totals.astype(jnp.float32)
    total_disco = totals[:, -1].reshape(channels, channels)
    totals = totals[:, :-1].reshape(-1, LANES)
    half = totals.shape[0] // 2
    total_in = jnp.concatenate(jnp.split(totals[:half], half // channels), axis=1)
    total_out = jnp.concatenate(jnp.split(totals[half:], channels // LANES), axis=1)
    scale = 1.0 / math.sqrt(NLAT * NLON)
    return (result, grad_gain, total_in * scale, total_out * scale, total_disco * scale)


def shards(*arrays):
    channels, rows, columns = arrays[0].shape
    lat_count = lax.axis_size("lat")
    lon_count = lax.axis_size("lon")
    fits = (
        rows == 2 * BAND
        and lon_count == 2
        and channels == lon_count * LANES
        and columns % (2 * LANES) == 0
        and M == LANES
        and M // lat_count == 8
        and L // lat_count == 8
    )
    return shards_banded(*arrays) if fits else shards_general(*arrays)


def solution(mesh):
    placed = (
        P(None, "lat", "lon"),
        P(None, "lat", "lon"),
        P(None, "lat", "lon"),
        P("lat", "lon", None, None),
        P("lat", "lon", None, None),
        P(),
        P(),
        P(),
        P(),
        P(),
        P(),
        P(),
    )
    return jax.shard_map(
        shards,
        mesh=mesh,
        in_specs=placed,
        out_specs=(P(None, "lat", "lon"), P("lat", "lon", None, None), P(), P(), P()),
        check_vma=False,
    )
```

```python
import functools
import math

import jax
import jax.numpy as jnp
import numpy as np
from jax import lax
from jax.experimental import pallas as pl
from jax.experimental.pallas import tpu as pltpu
from jax.sharding import PartitionSpec as P

NLAT = 512
NLON = 1024
L = 128
M = 128
REACH = 2
NQ = 64


root_half = 0.7071067811865476
root_two_pi = 2.5066282746310002


def padded_2(block, sides, width):
    for axis, dim in sides:
        count = lax.axis_size(axis)
        forward = [(i, i + 1) for i in range(count - 1)]
        forward.append((count - 1, 0))
        backward = [(target, source) for source, target in forward]
        low = lax.ppermute(
            lax.slice_in_dim(block, block.shape[dim] - width, None, axis=dim), axis, forward
        )
        high = lax.ppermute(lax.slice_in_dim(block, 0, width, axis=dim), axis, backward)
        block = jnp.concatenate([low, block, high], axis=dim)
    return block


def gelu_value(value):
    return value * 0.5 * (1.0 + lax.erf(value * root_half))


def gelu_slope(value):
    return (
        0.5 * (1.0 + lax.erf(value * root_half))
        + value * jnp.exp(-0.5 * value * value) / root_two_pi
    )


def legendre_tables():
    degree = np.arange(L)[:, None] * 1.0
    order = np.arange(M)[None, :] * 1.0
    upper = np.where(
        degree > order,
        np.sqrt(
            np.maximum(4.0 * degree * degree - 1.0, 0.0)
            / np.maximum(degree * degree - order * order, 1.0)
        ),
        0.0,
    )
    lower = np.where(
        degree > order + 1.0,
        np.sqrt(
            np.maximum((degree - 1.0) ** 2 - order * order, 0.0)
            / np.maximum(4.0 * (degree - 1.0) ** 2 - 1.0, 1.0)
        ),
        0.0,
    )
    counter = np.arange(1, M) * 1.0
    diagonal_log = np.concatenate(
        [np.zeros(1), np.cumsum(0.5 * np.log((2.0 * counter + 1.0) / (2.0 * counter)))]
    ) - 0.5 * np.log(2.0)
    return (upper, lower, diagonal_log)


def legendre_rows(theta):
    upper, lower, diagonal_log = legendre_tables()
    float_type = theta.dtype
    cosine = jnp.cos(theta)[:, None]
    sine = jnp.sin(theta)
    orders = jnp.arange(M, dtype=jnp.int32)
    start_value = jnp.exp(
        jnp.asarray(diagonal_log, float_type)[None, :]
        + orders.astype(float_type)[None, :] * jnp.log(sine)[:, None]
    )

    def advance(carry, inputs):
        previous, before = carry
        degree, coef_up, coef_low = inputs
        fresh = jnp.where(
            (orders == degree)[None, :],
            start_value,
            coef_up[None, :] * (cosine * previous - coef_low[None, :] * before),
        )
        return ((fresh, previous), fresh)

    empty = jnp.zeros_like(start_value)
    final, table = lax.scan(
        advance,
        (empty, empty),
        (
            jnp.arange(L, dtype=jnp.int32),
            jnp.asarray(upper, float_type),
            jnp.asarray(lower, float_type),
        ),
    )
    weight = jnp.sqrt(sine * (math.pi / NLAT))
    return table * weight[None, :, None]


def forward_table():
    column = jnp.arange(NLON, dtype=jnp.int32)[:, None]
    order = jnp.arange(M, dtype=jnp.int32)[None, :]
    angle = (column * order % NLON).astype(jnp.float32) * (2.0 * math.pi / NLON)
    factor = jnp.where(order == 0, 1.0, 2.0).astype(jnp.float32) / math.sqrt(NLON)
    return jnp.concatenate([factor * jnp.cos(angle), -factor * jnp.sin(angle)], axis=1).astype(
        jnp.bfloat16
    )


def inverse_table():
    order = jnp.arange(M, dtype=jnp.int32)[:, None]
    column = jnp.arange(NLON, dtype=jnp.int32)[None, :]
    angle = (column * order % NLON).astype(jnp.float32) * (2.0 * math.pi / NLON)
    return (jnp.concatenate([jnp.cos(angle), -jnp.sin(angle)], axis=0) / math.sqrt(NLON)).astype(
        jnp.bfloat16
    )


def disco_kernel(quad_weights, lat_offsets, lon_offsets, weight_index):
    span = jnp.arange(-REACH, REACH + 1, dtype=jnp.int32)
    slots = jnp.arange(NQ, dtype=jnp.int32)
    values = jnp.sum(
        jnp.where(
            weight_index[:, :, None] == slots[None, None, :], quad_weights[None, None, :], 0.0
        ),
        axis=2,
    )
    north = (lat_offsets[:, :, None] == span[None, None, :]).astype(quad_weights.dtype)
    east = (lon_offsets[:, :, None] == span[None, None, :]).astype(quad_weights.dtype)
    return jnp.sum(values[:, :, None, None] * north[:, :, :, None] * east[:, :, None, :], axis=1)


def disco_apply(padded, kernel):
    height = kernel.shape[0]
    width = padded.shape[2] - 2 * REACH
    total = jnp.zeros((padded.shape[0], height, width), kernel.dtype)
    for north in range(2 * REACH + 1):
        for east in range(2 * REACH + 1):
            total = (
                total
                + kernel[None, :, north, east, None]
                * padded[:, north : north + height, east : east + width]
            )
    return total


def disco_adjoint(padded, kernel_rim):
    height = kernel_rim.shape[0] - 2 * REACH
    width = padded.shape[2] - 2 * REACH
    total = jnp.zeros((padded.shape[0], height, width), kernel_rim.dtype)
    for north in range(2 * REACH + 1):
        for east in range(2 * REACH + 1):
            row_shift = 2 * REACH - north
            col_shift = 2 * REACH - east
            total = (
                total
                + kernel_rim[None, row_shift : row_shift + height, north, east, None]
                * padded[:, row_shift : row_shift + height, col_shift : col_shift + width]
            )
    return total


def inside_rows(padded, first_row):
    height = padded.shape[1]
    latitude = first_row - REACH + jnp.arange(height, dtype=jnp.int32)
    keep = (latitude >= 0) & (latitude < NLAT)
    return jnp.where(keep[None, :, None], padded, jnp.zeros((), padded.dtype))


def shards_general(
    cotangent,
    block_input,
    filtered,
    spectral_saved,
    spectral_gain,
    w_in,
    w_out,
    w_disco,
    quad_weights,
    lat_offsets,
    lon_offsets,
    weight_index,
):
    channels, rows, columns = cotangent.shape
    lat_count = lax.axis_size("lat")
    first_row = lax.axis_index("lat") * rows
    cells = rows * columns
    flat_in = filtered.reshape(channels, cells)
    flat_cot = cotangent.reshape(channels, cells)
    hidden_pre = lax.dot_general(
        w_in, flat_in, (((0,), (0,)), ((), ())), preferred_element_type=jnp.float32
    )
    activation = gelu_value(hidden_pre).astype(jnp.bfloat16)
    grad_act = jnp.dot(w_out, flat_cot, preferred_element_type=jnp.float32)
    grad_pre = (grad_act * gelu_slope(hidden_pre)).astype(jnp.bfloat16)
    grad_in_part = lax.dot_general(
        flat_in, grad_pre, (((1,), (1,)), ((), ())), preferred_element_type=jnp.float32
    )
    grad_out_part = lax.dot_general(
        activation, flat_cot, (((1,), (1,)), ((), ())), preferred_element_type=jnp.float32
    )
    grad_flat = jnp.dot(w_in, grad_pre, preferred_element_type=jnp.float32).astype(jnp.bfloat16)
    grad_filtered = grad_flat.reshape(channels, rows, columns)
    spread = lax.all_to_all(grad_filtered, "lon", split_axis=0, concat_axis=2, tiled=True)
    local_channels = spread.shape[0]
    coeffs = (
        jnp.dot(
            spread.reshape(local_channels * rows, NLON),
            forward_table(),
            preferred_element_type=jnp.float32,
        )
        .astype(jnp.bfloat16)
        .reshape(local_channels, rows, 2, M)
    )
    theta_rows = ((first_row + jnp.arange(rows, dtype=jnp.int32)).astype(jnp.float32) + 0.5) * (
        math.pi / NLAT
    )
    legendre = legendre_rows(theta_rows).astype(jnp.bfloat16)
    owned_count = L // lat_count
    weights = lax.slice_in_dim(legendre, 0, owned_count * lax.axis_size("lat"), axis=0)
    owned = lax.psum_scatter(
        jnp.einsum("ljm,cjrm->lcrm", weights, coeffs, preferred_element_type=jnp.float32),
        "lat",
        scatter_dimension=0,
        tiled=True,
    )
    real_part = owned[:, :, 0]
    imag_part = owned[:, :, 1]
    grad_gain = jnp.stack(
        [
            real_part * spectral_saved[:, :, 0] + imag_part * spectral_saved[:, :, 1],
            imag_part * spectral_saved[:, :, 0] - real_part * spectral_saved[:, :, 1],
        ],
        axis=2,
    )
    scaled = jnp.stack(
        [
            spectral_gain[:, :, 0] * real_part + spectral_gain[:, :, 1] * imag_part,
            spectral_gain[:, :, 0] * imag_part - spectral_gain[:, :, 1] * real_part,
        ],
        axis=2,
    ).astype(jnp.bfloat16)
    piece = lax.all_gather(scaled, "lat", axis=0, tiled=True)
    weights = lax.slice_in_dim(legendre, 0, piece.shape[0], axis=0)
    synthesis = (
        jnp.zeros((local_channels, rows, 2, M), jnp.float32)
        + jnp.einsum("ljm,lcrm->cjrm", weights, piece, preferred_element_type=jnp.float32)
    ).astype(jnp.bfloat16)
    grid_rows = jnp.dot(
        synthesis.reshape(local_channels * rows, 2 * M),
        inverse_table(),
        preferred_element_type=jnp.float32,
    ).reshape(local_channels, rows, NLON)
    spectral_grad = lax.all_to_all(grid_rows, "lon", split_axis=2, concat_axis=0, tiled=True)
    kernel = disco_kernel(quad_weights, lat_offsets, lon_offsets, weight_index)
    kernel_pad = jnp.pad(kernel, ((REACH, REACH), (0, 0), (0, 0)))
    kernel_rim = lax.dynamic_slice_in_dim(kernel_pad, first_row, rows + 2 * REACH, 0)
    stacked_rims = padded_2(
        jnp.stack((block_input, grad_filtered)), (("lat", 2), ("lon", 3)), REACH
    )
    input_pad = inside_rows(stacked_rims[0], first_row)
    grad_source = inside_rows(stacked_rims[1], first_row)
    grad_pad = lax.dot_general(
        w_disco, grad_source, (((1,), (0,)), ((), ())), preferred_element_type=jnp.float32
    ).astype(jnp.bfloat16)
    mixed = disco_apply(input_pad, kernel_rim[REACH : REACH + rows]).astype(jnp.bfloat16)
    grad_disco_part = lax.dot_general(
        mixed.reshape(channels, cells),
        grad_flat,
        (((1,), (1,)), ((), ())),
        preferred_element_type=jnp.float32,
    )
    disco_grad = disco_adjoint(grad_pad, kernel_rim)
    grad_input = (spectral_grad + disco_grad).astype(jnp.bfloat16)
    total_in, total_out, total_disco = lax.psum(
        (grad_in_part, grad_out_part, grad_disco_part), ("lat", "lon")
    )
    scale = 1.0 / math.sqrt(NLAT * NLON)
    return (grad_input, grad_gain, total_in * scale, total_out * scale, total_disco * scale)


BAND = 16
LANES = 128
MIB = 1024 * 1024
MLP_CHUNK = 512


def mm(a, b):
    return jnp.dot(a, b, preferred_element_type=jnp.float32)


def mm_nt(a, b):
    return lax.dot_general(a, b, (((1,), (1,)), ((), ())), preferred_element_type=jnp.float32)


def mm_tn(a, b):
    return lax.dot_general(a, b, (((0,), (0,)), ((), ())), preferred_element_type=jnp.float32)


def params(mib):
    return pltpu.CompilerParams(vmem_limit_bytes=mib * MIB)


def whole_block(shape):
    return pl.BlockSpec(shape, lambda *_: (0,) * len(shape))


def rows_first(block, stage, flat, width):
    channels = block.shape[0]
    for tile in range(width // LANES):
        stage[tile] = (
            block[:, :, tile * LANES : (tile + 1) * LANES]
            .astype(jnp.float32)
            .reshape(channels * BAND, LANES)
        )
    for row in range(BAND):
        for tile in range(width // LANES):
            start = row * width + tile * LANES
            flat[:, start : start + LANES] = stage[
                tile, pl.ds(row, channels, stride=BAND), :
            ].astype(jnp.bfloat16)


def gelu_both(value):
    decay = jnp.exp(value * value * -0.5)
    base = 1.0 + (0.3275911 * root_half) * jnp.abs(value)
    inverse = pl.reciprocal(base, approx=True)
    inverse = inverse * (2.0 - base * inverse)
    poly = 0.5 * 1.061405429
    for term in (-1.453152027, 1.421413741, -0.284496736, 0.254829592):
        poly = poly * inverse + 0.5 * term
    tail = poly * inverse * decay
    chance = jnp.where(value >= 0.0, 1.0 - tail, tail)
    return chance, decay


def mlp_kernel(
    side, x_ref, ct_ref, win_t, win, wout, *rest, steps, width, chunk, halo, pieces,
):
    left = rest[: max(pieces - 1, 0)]
    table = rest[len(left)] if pieces else None
    rest = rest[pieces + 1 :]
    if pieces:
        gf_ref, own_ref, send_ref, edge_ref, halo_ref, gin_ref, gout_ref = rest[:7]
        stage, xs, cs, low, high = rest[7:]
    else:
        gf_ref, gin_ref, gout_ref, stage, xs, cs = rest
    step = pl.program_id(0)

    @pl.when(step == 0)
    def _():
        gin_ref[...] = jnp.zeros_like(gin_ref)
        gout_ref[...] = jnp.zeros_like(gout_ref)

    rows_first(x_ref, stage, xs, width)
    rows_first(ct_ref, stage, cs, width)
    column = pl.multiple_of(step * width, width)
    per = chunk // width

    def body(index, carry):
        cells = pl.ds(pl.multiple_of(index * chunk, chunk), chunk)
        x = xs[:, cells]
        c = cs[:, cells]
        pre = mm(win_t[...], x)
        grad = mm(wout[...], c)
        chance, decay = gelu_both(pre)
        act = (pre * chance).astype(jnp.bfloat16)
        gp = (grad * (chance + pre * decay * (1.0 / root_two_pi))).astype(jnp.bfloat16)
        gf = mm(win[...], gp).astype(jnp.bfloat16)
        for part in range(per):
            gf_ref[index * per + part, :, pl.ds(column, width)] = gf[
                :, part * width : (part + 1) * width
            ]
        gin_ref[...] += mm_nt(x, gp)
        gout_ref[...] += mm_nt(act, c)
        return carry

    lax.fori_loop(0, BAND * width // chunk, body, 0, unroll=2)
    if not pieces:
        return

    @pl.when(step == steps - 1)
    def _():
        parts = [*left, gf_ref]
        spans = []
        for ref in parts:
            start = spans[-1][1] if spans else 0
            spans.append((start, start + ref.shape[2]))
        for ref, (start, stop) in zip(parts, spans):
            halo_ref[:, :, start:stop] = ref[halo : halo + REACH]
        orders = low.shape[0] // BAND

        def transform(row, carry):
            out = None
            for ref, (start, stop) in zip(parts, spans):
                term = mm_nt(table[:, start:stop], ref[row])
                out = term if out is None else out + term
            low[pl.ds(row, orders, stride=BAND), :] = out[:orders, :LANES]
            high[pl.ds(row, orders, stride=BAND), :] = out[:orders, LANES:]
            edge_ref[row] = out[orders:].astype(jnp.bfloat16)
            return carry

        lax.fori_loop(0, BAND, transform, 0, unroll=2)
        first = side[0] == 0
        shape = own_ref.shape

        @pl.when(first)
        def _():
            own_ref[...] = low[...].astype(jnp.bfloat16).reshape(shape)
            send_ref[...] = high[...].astype(jnp.bfloat16).reshape(shape)

        @pl.when(jnp.logical_not(first))
        def _():
            own_ref[...] = high[...].astype(jnp.bfloat16).reshape(shape)
            send_ref[...] = low[...].astype(jnp.bfloat16).reshape(shape)


def mlp_call(band, span, side, filtered, cotangent, win_t, win, wout, left, table, earlier):
    channels, rows, columns = filtered.shape
    hidden = wout.shape[0]
    width = LANES
    offset = span[0] // width
    steps = (span[1] - span[0]) // width
    chunk = MLP_CHUNK
    orders = table.shape[0] - 16
    last = span[1] == columns
    pieces = len(left) + 1 if last else 0
    block = pl.BlockSpec((channels, BAND, width), lambda i: (0, band, offset + i))
    cells = BAND * (span[1] - span[0])
    outs = [((BAND, channels, span[1] - span[0]), jnp.bfloat16)]
    if last:
        outs += [
            ((orders, BAND, LANES), jnp.bfloat16),
            ((orders, BAND, LANES), jnp.bfloat16),
            ((BAND, 16, channels), jnp.bfloat16),
            ((REACH, channels, columns), jnp.bfloat16),
        ]
    outs += [((channels, hidden), jnp.float32), ((hidden, channels), jnp.float32)]
    tables = [*left, table] if last else []
    return pl.pallas_call(
        functools.partial(
            mlp_kernel,
            steps=steps,
            width=width,
            chunk=chunk,
            halo=band * (BAND - REACH),
            pieces=pieces,
        ),
        grid=(steps,),
        in_specs=[
            pl.BlockSpec(memory_space=pltpu.SMEM),
            block,
            block,
            whole_block(win_t.shape),
            whole_block(win.shape),
            whole_block(wout.shape),
        ]
        + [whole_block(array.shape) for array in tables]
        + [pl.BlockSpec(memory_space=pl.ANY)],
        out_specs=[whole_block(shape) for shape, _ in outs],
        out_shape=[jax.ShapeDtypeStruct(shape, kind) for shape, kind in outs],
        scratch_shapes=[
            pltpu.VMEM((width // LANES, channels * BAND, LANES), jnp.float32),
            pltpu.VMEM((channels, BAND * width), jnp.bfloat16),
            pltpu.VMEM((channels, BAND * width), jnp.bfloat16),
        ]
        + [pltpu.VMEM((orders * BAND, LANES), jnp.float32)] * (2 if last else 0),
        compiler_params=params(60),
        cost_estimate=pl.CostEstimate(
            flops=2 * cells * channels * (5 * hidden + orders),
            bytes_accessed=6 * channels * cells,
            transcendentals=2 * hidden * cells,
        ),
        name="mlp",
    )(side, filtered, cotangent, win_t, win, wout, *tables, earlier)


def stencil_kernel(taps, *rest, first, counts):
    edges, place, _, q_ref, field, rim = rest[sum(counts) :]
    channels, columns = field.shape[1:]
    pieces = iter(rest)
    low = 0
    for count, height in zip(counts, (REACH, BAND, REACH)):
        start = 0
        for _ in range(count):
            piece = next(pieces)
            stop = start + piece.shape[2]
            field[low : low + height, :, start:stop] = piece[...]
            start = stop
        low += height

    def spread(row, carry):
        rim[row] = mm_tn(edges[row], place[...]).astype(jnp.bfloat16)
        return carry

    lax.fori_loop(0, BAND + 2 * REACH, spread, 0, unroll=5)
    lane = lax.broadcasted_iota(jnp.int32, (16, LANES), 1)
    span = 2 * REACH + 1

    def row_body(row, carry):
        weights = {}
        for north in range(span):
            source = row + 2 * REACH - north
            for east in range(span):
                weights[north, east] = taps[((first + source) * span + north) * span + east].astype(
                    jnp.bfloat16
                )

        def tile_body(tile, inner):
            part = pl.ds(pl.multiple_of(tile * 16, 16), 16)
            sums = [None] * span
            for north in range(span):
                source = row + 2 * REACH - north
                here = field[source, part, :]
                ends = rim[source, part, :]
                for east in range(span):
                    past = east - REACH
                    shifted = here
                    if past < 0:
                        rim_tile = jnp.where(lane < -past, ends, here[:, :LANES])
                        shifted = jnp.concatenate([rim_tile, here[:, LANES:]], axis=1)
                    if past > 0:
                        rim_tile = jnp.where(lane >= LANES - past, ends, here[:, -LANES:])
                        shifted = jnp.concatenate([here[:, :-LANES], rim_tile], axis=1)
                    term = shifted * weights[north, east]
                    sums[east] = term if sums[east] is None else sums[east] + term
            total = sums[REACH].astype(jnp.float32)
            for east in range(span):
                if east != REACH:
                    moved = pltpu.roll(sums[east], (east - REACH) % columns, 1)
                    total = total + moved.astype(jnp.float32)
            q_ref[row, part, :] = total.astype(jnp.bfloat16)
            return inner

        return lax.fori_loop(0, channels // 16, tile_body, carry, unroll=4)

    lax.fori_loop(0, BAND, row_body, 0)


def stencil_call(band, taps, before, rows, after, edges, place, earlier):
    sources = (before, rows, after)
    channels = rows[0][0].shape[1]
    columns = sum(piece.shape[2] for piece in rows[0])
    shape = (BAND, channels, columns)

    def piece_spec(piece, height, index):
        return pl.BlockSpec((height, channels, piece.shape[2]), lambda i: (index, 0, 0))

    return pl.pallas_call(
        functools.partial(
            stencil_kernel, first=band * BAND, counts=[len(pieces) for pieces, _ in sources]
        ),
        grid=(1,),
        in_specs=[pl.BlockSpec(memory_space=pltpu.SMEM)]
        + [
            piece_spec(piece, height, index)
            for (pieces, index), height in zip(sources, (REACH, BAND, REACH))
            for piece in pieces
        ]
        + [
            whole_block(edges.shape),
            whole_block(place.shape),
            pl.BlockSpec(memory_space=pl.ANY),
        ],
        out_specs=whole_block(shape),
        out_shape=jax.ShapeDtypeStruct(shape, jnp.bfloat16),
        scratch_shapes=[
            pltpu.VMEM((BAND + 2 * REACH, channels, columns), jnp.bfloat16),
            pltpu.VMEM((BAND + 2 * REACH, channels, LANES), jnp.bfloat16),
        ],
        compiler_params=params(48),
        cost_estimate=pl.CostEstimate(
            flops=60 * channels * BAND * columns,
            bytes_accessed=4 * channels * BAND * columns,
            transcendentals=0,
        ),
        name="stencil",
    )(taps, *before[0], *rows[0], *after[0], edges, place, earlier)


def disco_kernel_grad(bi_ref, q_ref, gd_ref, stage, flat):
    columns = q_ref.shape[2]
    gd_ref[...] = jnp.zeros_like(gd_ref)
    rows_first(bi_ref, stage, flat, columns)

    def body(row, carry):
        cells = pl.ds(pl.multiple_of(row * columns, columns), columns)
        gd_ref[...] += mm_nt(flat[:, cells], q_ref[row])
        return carry

    lax.fori_loop(0, BAND, body, 0, unroll=4)


def disco_grad_call(band, block_input, q):
    channels, _, columns = block_input.shape
    return pl.pallas_call(
        disco_kernel_grad,
        grid=(1,),
        in_specs=[
            pl.BlockSpec((channels, BAND, columns), lambda i: (0, band, 0)),
            whole_block(q.shape),
        ],
        out_specs=whole_block((channels, channels)),
        out_shape=jax.ShapeDtypeStruct((channels, channels), jnp.float32),
        scratch_shapes=[
            pltpu.VMEM((columns // LANES, channels * BAND, LANES), jnp.float32),
            pltpu.VMEM((channels, BAND * columns), jnp.bfloat16),
        ],
        compiler_params=params(48),
        cost_estimate=pl.CostEstimate(
            flops=2 * channels * channels * BAND * columns,
            bytes_accessed=4 * channels * BAND * columns,
            transcendentals=0,
        ),
        name="disco_weight",
    )(block_input, q)


def legendre_kernel(leg, p0, t0, p1, t1, gain, _, __, s0, s1, s2, stage, *, steps, block):
    order = pl.program_id(0)
    degrees = leg.shape[1]
    half = leg.shape[2] // 2
    total = None
    for band, refs in enumerate(((p0, t0), (p1, t1))):
        pair = jnp.concatenate([ref[...].reshape(half, LANES) for ref in refs], axis=1)
        term = mm(leg[0, :, band * half : (band + 1) * half], pair)
        total = term if total is None else total + term
    real = total[:, :LANES]
    imag = total[:, LANES:]
    owners, band = s0.shape[:2]
    shape = (owners, -1, LANES)
    s2[:, order] = jnp.concatenate(
        [real.reshape(shape), imag.reshape(shape)], axis=1
    ).astype(jnp.bfloat16)
    g = gain[:, 0, 0].reshape(degrees, LANES)
    k = gain[:, 0, 1].reshape(degrees, LANES)
    scaled = jnp.concatenate([g * real + k * imag, g * imag - k * real], axis=1).astype(
        jnp.bfloat16
    )
    synth = mm_tn(leg[0], scaled)
    for r in range(2):
        stage[pl.ds(r * steps + order, 2 * half, stride=block), :] = synth[
            :, r * LANES : (r + 1) * LANES
        ]

    @pl.when(order == steps - 1)
    def _():
        s0[...] = stage[: half * block].astype(jnp.bfloat16).reshape(s0.shape)
        s1[:, :band] = stage[half * block :].astype(jnp.bfloat16).reshape(s0.shape)


def legendre_call(leg, r0, r1, gain, earlier):
    owners, block, band, lanes = r0.shape
    degrees = leg.shape[1]
    steps = block // 2
    real = pl.BlockSpec((owners, None, band, lanes), lambda m: (0, m, 0, 0))
    imag = pl.BlockSpec((owners, None, band, lanes), lambda m: (0, m + steps, 0, 0))
    g_shape = (owners, 1, 2, degrees // owners, lanes)
    g_spec = pl.BlockSpec(g_shape, lambda m: (0, m, 0, 0, 0))
    out = (owners, band, block, lanes)
    more = (owners, band + 1, block, lanes)
    owned = (owners, steps, block, lanes)
    return pl.pallas_call(
        functools.partial(legendre_kernel, steps=steps, block=block),
        grid=(steps,),
        in_specs=[
            pl.BlockSpec((1, degrees, leg.shape[2]), lambda m: (m, 0, 0)),
            real,
            imag,
            real,
            imag,
            g_spec,
        ]
        + [pl.BlockSpec(memory_space=pl.ANY)] * 2,
        out_specs=[whole_block(out), whole_block(more), whole_block(owned)],
        out_shape=[
            jax.ShapeDtypeStruct(out, jnp.bfloat16),
            jax.ShapeDtypeStruct(more, jnp.bfloat16),
            jax.ShapeDtypeStruct(owned, jnp.bfloat16),
        ],
        scratch_shapes=[pltpu.VMEM((2 * owners * band * block, lanes), jnp.float32)],
        compiler_params=params(48),
        cost_estimate=pl.CostEstimate(
            flops=8 * steps * degrees * leg.shape[2] * 256,
            bytes_accessed=7 * MIB,
            transcendentals=0,
        ),
        name="legendre",
    )(leg, r0, r0, r1, r1, gain, *earlier)


def pair_sum_kernel(kept, arrived, *rest):
    out = rest[-1]
    block = kept.shape[0] // out.shape[0]
    total = kept[...].astype(jnp.float32) + arrived[...].astype(jnp.float32)
    out[:, :block] = total.astype(jnp.bfloat16).reshape(-1, block, *kept.shape[1:])
    if out.shape[1] > block:
        total = rest[0][...].astype(jnp.float32) + rest[1][...].astype(jnp.float32)
        out[:, block:] = total.astype(jnp.bfloat16)


def pair_sum_call(owners, kept, arrived, more, earlier):
    orders, band, lanes = kept.shape
    extra = more[0].shape[1] if more else 0
    shape = (owners, orders // owners + extra, band, lanes)
    return pl.pallas_call(
        pair_sum_kernel,
        grid=(1,),
        in_specs=[whole_block(array.shape) for array in (kept, arrived, *more)]
        + [pl.BlockSpec(memory_space=pl.ANY)] * len(earlier),
        out_specs=whole_block(shape),
        out_shape=jax.ShapeDtypeStruct(shape, jnp.bfloat16),
        compiler_params=params(32),
        name="pair_sum",
    )(kept, arrived, *more, *earlier)


def share_kernel(kept, arrived, before, out):
    total = kept[...].astype(jnp.float32) + arrived[...].astype(jnp.float32)
    out[...] = total.astype(jnp.bfloat16).reshape(out.shape)


def share_call(kept, arrived, parcel):
    owners, blocks, band, lanes = parcel.shape
    return pl.pallas_call(
        share_kernel,
        grid=(1,),
        in_specs=[whole_block(kept.shape)] * 2 + [pl.BlockSpec(memory_space=pl.ANY)],
        out_specs=pl.BlockSpec((owners, 1, band, lanes), lambda i: (0, blocks - 1, 0, 0)),
        out_shape=jax.ShapeDtypeStruct(parcel.shape, jnp.bfloat16),
        input_output_aliases={2: 0},
        name="share",
    )(kept, arrived, parcel)


def split_kernel(parcel, shares, earlier, synth, totals):
    band = synth.shape[1]
    synth[...] = parcel[:, :band]
    blocks = totals.shape[1] - 1
    first = shares[...].astype(jnp.float32).sum(axis=0).astype(jnp.bfloat16)
    last = parcel[:, band:].astype(jnp.float32).sum(axis=0).astype(jnp.bfloat16)
    totals[:, :blocks] = jnp.broadcast_to(first[None], (totals.shape[0],) + first.shape)
    totals[:, blocks:] = jnp.broadcast_to(last[None], (totals.shape[0],) + last.shape)


def split_call(count, parcel, shares, earlier):
    owners, _, band, lanes = parcel.shape
    more = shares.shape[1] - band
    shapes = ((owners, band, band, lanes), (count, more + 1, band, lanes))
    return pl.pallas_call(
        split_kernel,
        grid=(1,),
        in_specs=[
            whole_block(parcel.shape),
            pl.BlockSpec((owners, more, band, lanes), lambda i: (0, band // more, 0, 0)),
            pl.BlockSpec(memory_space=pl.ANY),
        ],
        out_specs=[whole_block(shape) for shape in shapes],
        out_shape=[jax.ShapeDtypeStruct(shape, jnp.bfloat16) for shape in shapes],
        compiler_params=params(32),
        name="split",
    )(parcel, shares, earlier)


def later_kernel(array, earlier, other, out):
    out[...] = array[...]


def later_call(array, *earlier):
    return pl.pallas_call(
        later_kernel,
        grid=(1,),
        in_specs=[whole_block(array.shape)] + [pl.BlockSpec(memory_space=pl.ANY)] * 2,
        out_specs=whole_block(array.shape),
        out_shape=jax.ShapeDtypeStruct(array.shape, array.dtype),
        name="later",
    )(array, *earlier)


def final_kernel(side, q_ref, own, other, table, wd, *rest):
    out_ref, stage = rest[-2:]
    width = q_ref.shape[2]
    orders = table.shape[0]
    channels = out_ref.shape[0]
    first = side[0] == 0

    def body(row, carry):
        mine = own[:, row].reshape(orders, LANES)
        theirs = other[:, row].reshape(orders, LANES)
        synth = jnp.concatenate(
            [jnp.where(first, mine, theirs), jnp.where(first, theirs, mine)], axis=1
        )
        out = mm_tn(synth, table[...]) + mm(wd[...], q_ref[row])
        for tile in range(width // LANES):
            stage[tile, pl.ds(row, channels, stride=BAND), :] = out[
                :, tile * LANES : (tile + 1) * LANES
            ]
        return carry

    lax.fori_loop(0, BAND, body, 0, unroll=2)
    for tile in range(width // LANES):
        out_ref[:, :, tile * LANES : (tile + 1) * LANES] = (
            stage[tile].astype(jnp.bfloat16).reshape(channels, BAND, LANES)
        )


def final_call(band, rows, side, q, own, other, table, wd, previous):
    _, channels, columns = q.shape
    width = 2 * LANES
    cells = BAND * columns
    extra = [] if previous is None else [previous]
    return pl.pallas_call(
        final_kernel,
        grid=(columns // width,),
        in_specs=[
            pl.BlockSpec(memory_space=pltpu.SMEM),
            pl.BlockSpec((BAND, channels, width), lambda i: (0, 0, i)),
            whole_block(other.shape),
            whole_block(other.shape),
            pl.BlockSpec((table.shape[0], width), lambda i: (0, i)),
            whole_block(wd.shape),
        ]
        + [pl.BlockSpec(memory_space=pl.ANY)] * len(extra),
        out_specs=pl.BlockSpec((channels, BAND, width), lambda i: (0, band, i)),
        out_shape=jax.ShapeDtypeStruct((channels, rows, columns), jnp.bfloat16),
        scratch_shapes=[pltpu.VMEM((width // LANES, channels * BAND, LANES), jnp.float32)],
        input_output_aliases={6: 0} if extra else {},
        compiler_params=params(48),
        cost_estimate=pl.CostEstimate(
            flops=2 * cells * channels * (channels + table.shape[0]),
            bytes_accessed=5 * channels * cells,
            transcendentals=0,
        ),
        name="final",
    )(side, q, own, other, table, wd, *extra)


def gain_kernel(gain, out, *, degrees):
    for degree in range(degrees):
        for r in range(2):
            part = gain[pl.ds(degree * 2 * LANES + r, LANES, stride=2), :]
            out[pl.ds(r * degrees + degree, LANES, stride=2 * degrees), :] = part.T


def gain_call(gain):
    degrees, channels, _, orders = gain.shape
    flat = gain.reshape(degrees * channels * 2, orders)
    return pl.pallas_call(
        functools.partial(gain_kernel, degrees=degrees),
        out_shape=jax.ShapeDtypeStruct((orders * 2 * degrees, channels), jnp.float32),
        name="gain",
    )(flat)


def grad_gain_kernel(owned, saved, out, *, degrees):
    for degree in range(degrees):
        real = owned[pl.ds(degree, LANES, stride=2 * degrees), :].T
        imag = owned[pl.ds(degrees + degree, LANES, stride=2 * degrees), :].T
        start = degree * 2 * LANES
        s = saved[pl.ds(start, LANES, stride=2), :]
        t = saved[pl.ds(start + 1, LANES, stride=2), :]
        out[pl.ds(start, LANES, stride=2), :] = real * s + imag * t
        out[pl.ds(start + 1, LANES, stride=2), :] = imag * s - real * t


def grad_gain_call(owned, saved):
    degrees, channels, _, orders = saved.shape
    flat = saved.reshape(degrees * channels * 2, orders)
    out = pl.pallas_call(
        functools.partial(grad_gain_kernel, degrees=degrees),
        out_shape=jax.ShapeDtypeStruct(flat.shape, jnp.float32),
        name="grad_gain",
    )(owned, flat)
    return out.reshape(saved.shape)


def legendre_whole():
    upper, lower, diagonal_log = legendre_tables()
    theta = (np.arange(NLAT) + 0.5) * (math.pi / NLAT)
    sine, cosine = np.sin(theta)[None], np.cos(theta)[None]
    orders = np.arange(M)
    start = np.exp(diagonal_log[:, None] + orders[:, None] * np.log(sine))
    table = np.zeros((M, L, NLAT))
    previous = before = np.zeros((M, NLAT))
    for degree in range(L):
        fresh = np.where(
            (orders == degree)[:, None],
            start,
            upper[degree][:, None] * (cosine * previous - lower[degree][:, None] * before),
        )
        table[:, degree] = fresh
        previous, before = fresh, previous
    return table * np.sqrt(sine * (math.pi / NLAT))[None]


def host_tables(lat_count, lon_count):
    columns, rows, own = NLON // lon_count, NLAT // lat_count, M // lat_count
    angle = (np.arange(M)[:, None] * np.arange(NLON)[None, :] % NLON) * (2.0 * math.pi / NLON)
    waves = np.stack([np.cos(angle), -np.sin(angle)]) / math.sqrt(NLON)
    factor = np.where(np.arange(M) == 0, 1.0, 2.0)[None, :, None]

    def arrange(table):
        table = table.reshape(2, lat_count, own, lon_count, columns)
        return table.transpose(3, 1, 0, 2, 4).reshape(lon_count, 2 * M, columns)

    pick = np.zeros((lon_count, 16, columns))
    for row, column in enumerate((0, 1, columns - 2, columns - 1)):
        pick[:, row, column] = 1.0
    forward = np.concatenate([arrange(waves * factor), pick], axis=1)
    legendre = legendre_whole().reshape(M, L, lat_count, rows // BAND, BAND)
    legendre = legendre.transpose(0, 1, 3, 2, 4).reshape(M, L, NLAT)
    kind = jnp.bfloat16
    return forward.astype(kind), arrange(waves).astype(kind), legendre.astype(kind)


def shards_banded(
    cotangent,
    block_input,
    filtered,
    spectral_saved,
    spectral_gain,
    w_in,
    w_out,
    w_disco,
    quad_weights,
    lat_offsets,
    lon_offsets,
    weight_index,
):
    channels, rows, columns = cotangent.shape
    lat_count = lax.axis_size("lat")
    lon_count = lax.axis_size("lon")
    lat_index = lax.axis_index("lat")
    lon_index = lax.axis_index("lon")
    own = M // lat_count
    degrees = L // lat_count
    side = lon_index.reshape(1).astype(jnp.int32)
    forward, inverse, legendre = host_tables(lat_count, lon_count)
    forward = lax.dynamic_index_in_dim(jnp.asarray(forward), lon_index, 0, keepdims=False)
    inverse = lax.dynamic_index_in_dim(jnp.asarray(inverse), lon_index, 0, keepdims=False)
    legendre = lax.dynamic_slice_in_dim(jnp.asarray(legendre), lat_index * own, own, 0)
    swap = [(i, (i + 1) % lon_count) for i in range(lon_count)]
    exchange = functools.partial(lax.all_to_all, axis_name="lat", split_axis=0, concat_axis=0, tiled=True)

    kernel = disco_kernel(quad_weights, lat_offsets, lon_offsets, weight_index)
    kernel_pad = jnp.pad(kernel, ((REACH, REACH), (0, 0), (0, 0)))
    kernel_rim = lax.dynamic_slice_in_dim(kernel_pad, lat_index * rows, rows + 2 * REACH, 0)
    taps = kernel_rim.reshape(-1)
    place = np.zeros((16, LANES), np.float32)
    for row, lane in enumerate((0, 1, LANES - 2, LANES - 1)):
        place[row, lane] = 1.0
    place = jnp.asarray(place, jnp.bfloat16)
    w_in_t = w_in.T

    down = [(i, (i + 1) % lat_count) for i in range(lat_count)]
    up = [(target, source) for source, target in down]

    def across(moves):
        return [
            (a * lon_count + i, b * lon_count + j) for a, b in moves for i, j in swap
        ]

    def dealt(array):
        blocks = array.astype(jnp.bfloat16).reshape(lat_count, lon_count, -1, BAND, LANES)
        half = functools.partial(lax.dynamic_index_in_dim, blocks, axis=1, keepdims=False)
        return half(lon_index), lax.ppermute(half(1 - lon_index), "lon", swap)

    gain = gain_call(spectral_gain).reshape(lat_count, own, 2, degrees, LANES)
    gf0, kept0, sent0, ends0, head, gin0, gout0 = mlp_call(
        0, (0, columns), side, filtered, cotangent, w_in_t, w_in, w_out, (), forward, gain
    )
    gain = exchange(gain)
    arrived0 = lax.ppermute(sent0, "lon", swap)
    bottom = lax.ppermute(head, "lat", up)
    sides0 = lax.ppermute(ends0, "lon", swap)
    bottom_side = lax.ppermute(ends0[:REACH], ("lat", "lon"), across(up))
    middle = columns // 2
    left1, gin1, gout1 = mlp_call(
        1, (0, middle), side, filtered, cotangent, w_in_t, w_in, w_out, (), forward, gain
    )
    sum0 = pair_sum_call(lat_count, kept0, arrived0, (), (bottom, bottom_side, sides0, gin1))
    received0 = exchange(sum0)
    right1, kept1, sent1, ends1, tail, gin2, gout2 = mlp_call(
        1, (middle, columns), side, filtered, cotangent, w_in_t, w_in, w_out, (left1,), forward, sum0
    )
    gf1 = (left1, right1)
    sides1 = lax.ppermute(ends1, "lon", swap)
    top = lax.ppermute(tail, "lat", down)
    top_side = lax.ppermute(ends1[BAND - REACH :], ("lat", "lon"), across(down))
    arrived1 = lax.ppermute(sent1, "lon", swap)
    half = w_in.shape[1] // 2
    gin = gin0 + gin1 + gin2
    weights = jnp.concatenate([gin[:, :half], gin[:, half:], gout0 + gout1 + gout2], axis=0)
    edges1 = jnp.concatenate([sides0[BAND - REACH :], sides1, bottom_side], axis=0)
    q1 = stencil_call(
        1, taps, ((gf0,), BAND // REACH - 1), (gf1, 0), ((bottom,), 0), edges1, place, received0
    )
    received1 = exchange(
        pair_sum_call(lat_count, kept1, arrived1, dealt(weights), (q1, top, top_side))
    )
    edges0 = jnp.concatenate([top_side, sides0, sides1[:REACH]], axis=0)
    q0 = stencil_call(0, taps, ((top,), 0), ((gf0,), 0), (gf1, 0), edges0, place, q1)
    disco1 = disco_grad_call(1, block_input, q1)
    disco0 = disco_grad_call(0, block_input, q0)
    s0, s1, owned = legendre_call(legendre, received0, received1, gain, (q0, disco1))
    local0 = exchange(s0)
    other0 = lax.ppermute(local0, "lon", swap)
    parcel = exchange(share_call(*dealt(disco0 + disco1), s1))
    result = final_call(0, rows, side, q0, local0, other0, inverse, w_disco, None)
    count = lat_count * lon_count
    synth1, totals = split_call(count, parcel, received1, other0)
    other1 = lax.ppermute(synth1, "lon", swap)
    totals = lax.all_to_all(totals, ("lat", "lon"), split_axis=0, concat_axis=0, tiled=True)
    owned = exchange(later_call(owned, result, totals))
    owned = owned.astype(jnp.float32).reshape(M * 2 * degrees, LANES)
    grad_gain = grad_gain_call(owned, spectral_saved)
    result = final_call(1, rows, side, q1, synth1, other1, inverse, w_disco, result)
    totals = totals.astype(jnp.float32)
    total_disco = totals[:, -1].reshape(channels, channels)
    totals = totals[:, :-1].reshape(-1, channels)
    total_in = jnp.concatenate([totals[:channels], totals[channels : 2 * channels]], axis=1)
    total_out = totals[2 * channels :]
    scale = 1.0 / math.sqrt(NLAT * NLON)
    return (result, grad_gain, total_in * scale, total_out * scale, total_disco * scale)


def shards(*arrays):
    channels, rows, columns = arrays[0].shape
    lat_count = lax.axis_size("lat")
    lon_count = lax.axis_size("lon")
    fits = (
        rows == 2 * BAND
        and lon_count == 2
        and channels == lon_count * LANES
        and columns % (2 * LANES) == 0
        and M == LANES
        and M // lat_count == 8
        and L // lat_count == 8
    )
    return shards_banded(*arrays) if fits else shards_general(*arrays)


def solution(mesh):
    placed = (
        P(None, "lat", "lon"),
        P(None, "lat", "lon"),
        P(None, "lat", "lon"),
        P("lat", "lon", None, None),
        P("lat", "lon", None, None),
        P(),
        P(),
        P(),
        P(),
        P(),
        P(),
        P(),
    )
    return jax.shard_map(
        shards,
        mesh=mesh,
        in_specs=placed,
        out_specs=(P(None, "lat", "lon"), P("lat", "lon", None, None), P(), P(), P()),
        check_vma=False,
    )
```
